128 devices in a mesh: row: 8 (over y, core), col: 16 (over x, z).
Axes of the slice: x: 4, y: 4, z: 4, core: 2. Of those that a mesh axis runs over, the one named last changes fastest.
Arguments:
- front: float32 [24, 8, 128, 2, 16, 128], P(None, 'row', None, None, 'col')
- child_one: float32 [8, 8, 128, 2, 16, 128], P(None, 'row', None, None, 'col'), may hold values from -3 to 3
- child_two: float32 [16, 8, 128, 2, 16, 128], P(None, 'row', None, None, 'col'), may hold values from -3 to 3
- map_one: int32 [64], replicated, may hold values from 0 to 191, as said below
- map_two: int32 [128], replicated, may hold values from 0 to 191, as said below
- owner_one: int32 [64], replicated, may hold values from 0 to 7, as said below
- owner_two: int32 [128], replicated, may hold values from 0 to 7, as said below
Outputs:
- factored: float32 [24, 8, 128, 2, 16, 128], P(None, 'row', None, None, 'col')
The draws below stay inside these ranges and needn't reach their ends.
Inputs may be any that keep to these rules, and one draw needn't show every extreme that they name: map_one is increasing and made of whole aligned runs of 8 front tile rows; it always holds the first and the last run. map_two is increasing and made of whole aligned runs of 8 front tile rows; it always holds the first and the last run. `owner_one`: every row index holds 8 tile rows of child one; of these, for each value v, exactly 1 have map_one mod 8 equal to v. `owner_two`: every row index holds 16 tile rows of child two; of these, for each value v, exactly 2 have map_two mod 8 equal to v.
All inputs are finite; a program needn't handle non-finite values.
Results may differ from the reference program's by a relative error of at most 0.0001.
Values sent between devices are 32-bit elements; how exact they have to be, the bound alone decides.
A program may use at most 128 MiB of HBM per device.

```python
import math
import jax
import jax.numpy as jnp
from jax import lax

TILE = 128
NF = 24576
PB = 8
C1_TILES = 64
C2_TILES = 128
CT_DEV = 2
PANEL = 1024
WC = 4096
C1R = 8
C2R = 16
N_ROW = 8
N_COL = 16


def spread_runs(key, child_tiles):
    runs_total = NF // TILE // N_ROW
    runs = child_tiles // N_ROW
    middle = jnp.sort(jax.random.permutation(key, runs_total - 2)[:runs - 2] + 1)
    chosen = jnp.concatenate([jnp.zeros((1,), jnp.int32), middle.astype(jnp.int32), jnp.full((1,), runs_total - 1, jnp.int32)])
    index = jnp.arange(child_tiles, dtype=jnp.int32)
    return (chosen[index // N_ROW] * N_ROW + index % N_ROW).astype(jnp.int32)


def owner_list(key, child_tiles):
    rotation = (jax.random.permutation(key, child_tiles // N_ROW) % N_ROW).astype(jnp.int32)
    index = jnp.arange(child_tiles, dtype=jnp.int32)
    return ((index % N_ROW + rotation[index // N_ROW]) % N_ROW).astype(jnp.int32)


def coupled_front(spread, level, amplitude):
    rows = jnp.arange(NF, dtype=jnp.int32)[:, None]
    columns = jnp.arange(WC, dtype=jnp.int32)[None, :]
    amp_rows = jnp.concatenate([amplitude, jnp.zeros((NF - PANEL,), jnp.float32)])
    amp_cols = jnp.concatenate([amplitude, jnp.zeros((WC - PANEL,), jnp.float32)])
    level_rows = jnp.concatenate([level, jnp.zeros((NF - PANEL,), jnp.float32)])
    distance = jnp.abs(rows - columns).astype(jnp.float32)
    coupled = amp_rows[:, None] * amp_cols[None, :] * jnp.exp(distance * math.log(0.95))
    boost = jnp.where(rows == columns, level_rows[:, None] * math.sqrt(PANEL), jnp.float32(0.0))
    return spread + coupled + boost


def draw_front(key, part):
    key = jax.random.fold_in(key, 11)
    first, second, third = jax.random.split(key, 3)
    spread = jnp.clip(jax.random.normal(first, (NF, WC), jnp.float32), -6.0, 6.0)
    level = jax.random.uniform(second, (PANEL,), jnp.float32, 3.0, 6.0)
    amplitude = jax.random.uniform(third, (PANEL,), jnp.float32, 2.0, 6.0)
    full = coupled_front(spread, level, amplitude)
    return full.reshape(NF // (N_ROW * TILE), N_ROW, TILE, CT_DEV, N_COL, TILE)


def draw_map_one(key, part):
    key = jax.random.fold_in(key, 3)
    return spread_runs(key, C1_TILES)


def draw_map_two(key, part):
    key = jax.random.fold_in(key, 5)
    return spread_runs(key, C2_TILES)


def draw_owner_one(key, part):
    key = jax.random.fold_in(key, 7)
    return owner_list(key, C1_TILES)


def draw_owner_two(key, part):
    key = jax.random.fold_in(key, 9)
    return owner_list(key, C2_TILES)


def level_of(rng, shape, cuts, low, top_value):
    gain, own = 1.0, jax.random.fold_in(rng, 6)
    for dim, parts in cuts:
        draws = jnp.exp(jax.random.uniform(jax.random.fold_in(own, dim), (parts,), jnp.float32, low / len(cuts), top_value / len(cuts)))
        gain = gain * jnp.repeat(draws, shape[dim] // parts).reshape([-1 if axis == dim else 1 for axis in range(len(shape))])
    return gain


def noise(own_key, extent, deviation, reach, cuts=(), kind=jnp.bfloat16):
    array = jax.random.normal(own_key, extent, jnp.float32) * deviation
    if len(cuts) > 0:
        array = level_of(own_key, extent, cuts, -0.22, 0.18) * array
    return jnp.clip(array, min=-reach, max=reach).astype(kind)


def setup_inputs(seed: int = 0) -> dict:
    key_list = jax.random.split(jax.random.key(seed), 8)
    front = draw_front(jax.random.fold_in(key_list[7], 71), 0)
    child_one = noise(key_list[1], (C1R, N_ROW, TILE, CT_DEV, N_COL, TILE), 0.5, 3.0, ((1, 8), (4, 16)), jnp.float32)
    child_two = noise(key_list[2], (C2R, N_ROW, TILE, CT_DEV, N_COL, TILE), 0.5, 3.0, ((1, 8), (4, 16)), jnp.float32)
    map_one = draw_map_one(jax.random.fold_in(key_list[7], 71), 0)
    map_two = draw_map_two(jax.random.fold_in(key_list[7], 71), 0)
    owner_one = draw_owner_one(jax.random.fold_in(key_list[7], 71), 0)
    owner_two = draw_owner_two(jax.random.fold_in(key_list[7], 71), 0)
    return dict(front=front, child_one=child_one, child_two=child_two, map_one=map_one, map_two=map_two, owner_one=owner_one, owner_two=owner_two)


def symmetric(square):
    return jnp.tril(square) + jnp.tril(square, -1).T

def place_child(whole, held, owner, target_rows):
    slots = held.reshape(held.shape[0], N_ROW, TILE, WC)
    member = owner[:, None] == jnp.arange(N_ROW, dtype=jnp.int32)[None, :]
    ranks = jnp.cumsum(member.astype(jnp.int32), axis=0) - 1
    position = jnp.sum(jnp.where(member, ranks, 0), axis=1).astype(jnp.int32)
    rows = slots[position, owner.astype(jnp.int32)]
    stacked = whole.reshape(NF // TILE, TILE, WC).at[target_rows.astype(jnp.int32)].add(rows)
    return stacked.reshape(NF, WC)

def reference(front, child_one, child_two, map_one, map_two, owner_one, owner_two):
    whole = front.reshape(NF, WC)
    whole = place_child(whole, child_one, owner_one, map_one)
    whole = place_child(whole, child_two, owner_two, map_two)
    row_tile = jnp.arange(NF, dtype=jnp.int32) // TILE
    column_tile = jnp.arange(WC, dtype=jnp.int32) // TILE
    sent_blocks = []
    for block in range(PB):
        start = block * TILE
        lower = jnp.linalg.cholesky(symmetric(whole[start:start + TILE, start:start + TILE]))
        column = whole[:, start:start + TILE]
        below = lax.linalg.triangular_solve(lower, column, left_side=False, lower=True, transpose_a=True)
        repeated = jnp.tile(lower, (NF // TILE, 1))
        factor = jnp.where((row_tile > block)[:, None], below, jnp.where((row_tile == block)[:, None], repeated, column))
        whole = whole.at[:, start:start + TILE].set(factor)
        outgoing = jnp.where((row_tile >= block)[:, None], factor, jnp.float32(0.0))
        sent_blocks.append(outgoing)
        if block + 1 < PB:
            pieces = outgoing[start + TILE:PANEL]
            update = jnp.dot(outgoing, pieces.T, precision=lax.Precision.HIGHEST)
            keep = row_tile[:, None] >= column_tile[None, start + TILE:PANEL]
            whole = whole.at[:, start + TILE:PANEL].add(-jnp.where(keep, update, jnp.float32(0.0)))
    panel = jnp.concatenate(sent_blocks, axis=1)
    update = jnp.dot(panel, panel[PANEL:WC].T, precision=lax.Precision.HIGHEST)
    keep = row_tile[:, None] >= column_tile[None, PANEL:]
    whole = whole.at[:, PANEL:].add(-jnp.where(keep, update, jnp.float32(0.0)))
    return whole.reshape(front.shape)
```

```python
import functools

import jax
import jax.numpy as jnp
from jax import lax
from jax.experimental import pallas as pl
from jax.experimental.pallas import tpu as pltpu
from jax.sharding import PartitionSpec as P

F32, BF16, I32 = jnp.float32, jnp.bfloat16, jnp.int32
HIGHEST = lax.Precision.HIGHEST
MESH = pl.DeviceIdType.MESH
TILE, PB, NT = 128, 8, 24
LEAF = 16
NN = (((1,), (0,)), ((), ()))
NTC = (((1,), (1,)), ((), ()))
TN = (((0,), (0,)), ((), ()))
GROUPS = ((0, 1, True), (1, 4, False), (4, 17, True), (17, 24, False))


def dot(a, b, dims):
    return lax.dot_general(a, b, dims, precision=HIGHEST, preferred_element_type=F32)


def split3(v):
    high = v.astype(BF16)
    rest = v - high.astype(F32)
    middle = rest.astype(BF16)
    low = (rest - middle.astype(F32)).astype(BF16)
    return [part.astype(F32) for part in (high, middle, low)]


def rank_update(a, b):
    ah, am, al = split3(a)
    bh, bm, bl = split3(b)
    left = jnp.concatenate([ah, ah, am, ah, am, al], 0).astype(BF16)
    right = jnp.concatenate([bl, bm, bm, bh, bh, bh], 0).astype(BF16)
    return lax.dot_general(left, right, TN, preferred_element_type=F32)


def leaf(rows_u, rows_v, offset):
    count = rows_u.shape[0]
    index = lax.broadcasted_iota(I32, (count, TILE), 0)
    cols = [
        jnp.broadcast_to(rows_u[:, offset + k : offset + k + 1], (count, TILE)) for k in range(count)
    ]
    scale = jnp.zeros((count, TILE), F32)
    for j in range(count):
        pivot = cols[j][j : j + 1, :]
        scale = jnp.where(index == j, lax.rsqrt(pivot), scale)
        if j + 1 < count:
            ratio = cols[j] * (1.0 / pivot)
            for k in range(j + 1, count):
                cols[k] = cols[k] - ratio * cols[k][j : j + 1, :]
            ratio = jnp.where(index > j, ratio, 0.0)
            rows_u = rows_u - ratio * rows_u[j : j + 1, :]
            rows_v = rows_v - ratio * rows_v[j : j + 1, :]
    return rows_u * scale, rows_v * scale


def factor_tile(square):
    row = lax.broadcasted_iota(I32, (TILE, TILE), 0)
    col = lax.broadcasted_iota(I32, (TILE, TILE), 1)
    unit = jnp.where(row == col, 1.0, 0.0).astype(F32)
    count = TILE // LEAF
    left = [square[i * LEAF : (i + 1) * LEAF] for i in range(count)]
    right = [unit[i * LEAF : (i + 1) * LEAF] for i in range(count)]
    for b in range(count):
        left[b], right[b] = leaf(left[b], right[b], b * LEAF)
        if b + 1 < count:
            change = rank_update(left[b], jnp.concatenate([left[b], right[b]], 1))
            for i in range(b + 1, count):
                left[i] = left[i] - change[i * LEAF : (i + 1) * LEAF, :TILE]
                right[i] = right[i] - change[i * LEAF : (i + 1) * LEAF, TILE:]
    upper = jnp.where(col >= row, jnp.concatenate(left, 0), 0.0)
    inverse = jnp.where(col <= row, jnp.concatenate(right, 0), 0.0)
    return upper, inverse


def partner_slot(c):
    return 12 - 4 * (c // 4) + c % 4


def kernel(
    front, one, two, map_one, map_two, own_one, own_two, out,
    stage0, stage1, got0, got1, sum0, sum1, panel0, panel1, panel2, panel3, drows, brows, cols, inv, wt_hi, wt_lo,
    slots, table,
    child_send, child_recv, spread_send, spread_recv, ring_send, ring_recv,
    d_send, d_recv, b_send, b_recv,
):
    r, c = lax.axis_index("row"), lax.axis_index("col")
    y, core = r // 2, r % 2
    x, z = c // 4, c % 4
    source = x < 2
    partner = (3 - x) * 4 + z

    def at_col(dx, dz):
        return lax.rem(x + dx + 4, 4) * 4 + lax.rem(z + dz + 4, 4)

    def row_peer(step):
        return lax.rem(r + step, 8)

    def y_peer(step, other=0):
        mine = core if other == 0 else 1 - core
        return lax.rem(y + step, 4) * 2 + mine

    barrier = pltpu.get_barrier_semaphore()
    for step in range(1, 8):
        pl.semaphore_signal(barrier, inc=1, device_id=(row_peer(step), c), device_id_type=MESH)
    for dx, dz in ((1, 0), (-1, 0), (0, 1), (0, -1)):
        pl.semaphore_signal(barrier, inc=1, device_id=(r, at_col(dx, dz)), device_id_type=MESH)
    pl.semaphore_signal(barrier, inc=1, device_id=(r, partner), device_id_type=MESH)

    def find_one(g, carry):
        seen, picks = carry[0], list(carry[1:])
        for v in range(8):
            mine = own_one[8 * g + v] == r
            picks[v] = jnp.where(mine, seen, picks[v])
            seen = seen + mine.astype(I32)
        return (seen, *picks)

    picks_one = lax.fori_loop(0, 8, find_one, (jnp.int32(0),) * 9)[1:]

    def find_two(g, carry):
        seen, first, second = carry[0], list(carry[1:9]), list(carry[9:])
        for v in range(8):
            mine = own_two[8 * g + v] == r
            first[v] = jnp.where(mine, second[v], first[v])
            second[v] = jnp.where(mine, seen, second[v])
            seen = seen + mine.astype(I32)
        return (seen, *first, *second)

    picks_two = lax.fori_loop(0, 16, find_two, (jnp.int32(0),) * 17)[1:]
    for v in range(8):
        slots[v] = jnp.minimum(picks_one[v], 7)
        slots[8 + v] = jnp.minimum(picks_two[v], 15)
        slots[16 + v] = jnp.minimum(picks_two[8 + v], 15)

    def stage(ct, buffer):
        def body(v, carry):
            pick = pl.ds(ct, TILE, stride=2)
            buffer[v, 0] = one[slots[v], pick, :]
            buffer[v, 1] = two[slots[8 + v], pick, :]
            buffer[v, 2] = two[slots[16 + v], pick, :]
            return carry

        lax.fori_loop(0, 8, body, 0)

    def child_copy(ct, step):
        peer = row_peer(step)
        return pltpu.make_async_remote_copy(
            src_ref=(stage0, stage1)[ct].at[peer],
            dst_ref=(got0, got1)[ct].at[r],
            send_sem=child_send.at[ct, step - 1],
            recv_sem=child_recv.at[ct, step - 1],
            device_id=(peer, c),
            device_id_type=MESH,
        )

    stage(0, stage0)
    pl.semaphore_wait(barrier, 12)
    for step in range(1, 8):
        child_copy(0, step).start()
    stage(1, stage1)
    for step in range(1, 8):
        child_copy(1, step).start()
    for ct, buffer, staged in ((0, got0, stage0), (1, got1, stage1)):
        buffer[r] = staged[r]
        buffer[8] = jnp.zeros((3, TILE, TILE), F32)

    sources = [own_two[8 * g + r] for g in range(16)]
    for g in range(16):
        rank = jnp.int32(0)
        for h in range(g):
            rank = rank + (sources[h] == sources[g]).astype(I32)
        table[g] = jnp.clip(sources[g], 0, 7)
        table[16 + g] = jnp.minimum(rank, 1)

    def find_targets(t, carry):
        at_one, at_two = carry
        hit_one = map_one[8 * at_one] // 8 == t
        hit_two = map_two[8 * at_two] // 8 == t
        slots[32 + t] = jnp.where(hit_one, jnp.clip(own_one[8 * at_one + r], 0, 7), 8)
        slots[64 + t] = jnp.where(hit_two, table[at_two], 8)
        slots[96 + t] = jnp.where(hit_two, table[16 + at_two] + 1, 1)
        return (
            jnp.minimum(at_one + hit_one.astype(I32), 7),
            jnp.minimum(at_two + hit_two.astype(I32), 15),
        )

    lax.fori_loop(0, NT, find_targets, (jnp.int32(0), jnp.int32(0)))

    def assemble(ct, buffer, total):
        for step in range(1, 8):
            child_copy(ct, step).wait_recv()

        def body(t, carry):
            total[t] = (
                front[t, pl.ds(ct, TILE, stride=2), :] + buffer[slots[32 + t], 0]
            ) + buffer[slots[64 + t], slots[96 + t]]
            return carry

        lax.fori_loop(0, NT, body, 0)

    assemble(0, got0, sum0)

    panels = (panel0, panel1, panel2, panel3)

    @pl.when(source)
    def _():
        for g in range(4):
            lo, hi, _ = GROUPS[g]
            panels[g][c] = sum0[lo:hi, :64, :]

    def spread(g):
        lo, hi, _ = GROUPS[g]
        return pltpu.make_async_remote_copy(
            src_ref=sum0.at[pl.ds(lo, hi - lo), pl.ds(64, 64)],
            dst_ref=panels[g].at[partner],
            send_sem=spread_send.at[g],
            recv_sem=spread_recv.at[g],
            device_id=(r, partner),
            device_id_type=MESH,
        )

    def part(slot, g, half):
        lo, hi, _ = GROUPS[g]
        count, panel = hi - lo, panels[g]
        if half is None:
            return panel.at[slot]
        if count == 1:
            return panel.at[slot, pl.ds(0, 1), pl.ds(32 * half, 32)]
        upper = (count + 1) // 2
        return panel.at[slot, pl.ds(0, upper)] if half == 0 else panel.at[slot, pl.ds(upper, count - upper)]

    def move(g, axis, da, db, direction, half, index):
        x_first = GROUPS[g][2]
        offset = (da, db) if x_first else (db, da)
        along = (direction, 0) if (axis == 0) == x_first else (0, direction)
        ref = part(at_col(*offset), g, half)
        return pltpu.make_async_remote_copy(
            src_ref=ref,
            dst_ref=ref,
            send_sem=ring_send.at[g, index],
            recv_sem=ring_recv.at[g, index],
            device_id=(r, at_col(*along)),
            device_id_type=MESH,
        )

    def arrival(g, axis, da, db, direction, half, index):
        back = (da - direction, db) if axis == 0 else (da, db - direction)
        return move(g, axis, back[0], back[1], direction, half, index)

    def first(g, k):
        return (g, 0, 0, 0, (1, -1)[k], None, k)

    def first_on(g, k):
        return (g, 0, (-1, 1)[k], 0, (1, -1)[k], k, 2 + k)

    OFFSETS = (0, -1, 1, 2)

    def second(g, q, k):
        return (g, 1, OFFSETS[q], 0, (1, -1)[k], None, 4 + 4 * q + k)

    def second_on(g, q, k):
        return (g, 1, OFFSETS[q], (-1, 1)[k], (1, -1)[k], k, 6 + 4 * q + k)

    started = []

    def start(spec):
        started.append(spec)
        move(*spec).start()

    def wait(spec):
        g, axis, da, db, direction, half, index = spec
        arrival(g, axis, da, db, direction, half, index).wait_recv()

    def s0(g):
        @pl.when(source)
        def _():
            spread(g).start()

    def s1(g):
        @pl.when(jnp.logical_not(source))
        def _():
            spread(g).wait_recv()

        for k in range(2):
            start(first(g, k))
        for k in range(2):
            start(second(g, 0, k))

    def s2(g):
        for k in range(2):
            wait(first(g, k))
            start(first_on(g, k))
        for q in (1, 2):
            for k in range(2):
                start(second(g, q, k))

    def s3(g):
        for k in range(2):
            wait(second(g, 0, k))
            start(second_on(g, 0, k))

    def s4(g):
        for k in range(2):
            wait(first_on(g, k))
        for k in range(2):
            start(second(g, 3, k))

    def s5(g):
        for q in (1, 2):
            for k in range(2):
                wait(second(g, q, k))
                start(second_on(g, q, k))

    def s6(g):
        for k in range(2):
            wait(second(g, 3, k))
            start(second_on(g, 3, k))

    def s7(g):
        for q in range(4):
            for k in range(2):
                wait(second_on(g, q, k))

    def d_out(step):
        return pltpu.make_async_remote_copy(
            src_ref=panel0.at[:, 0],
            dst_ref=drows.at[r],
            send_sem=d_send.at[step - 1],
            recv_sem=d_recv.at[step - 1],
            device_id=(y_peer(step), c),
            device_id_type=MESH,
        )

    def d_pair(step):
        held = y_peer(step)
        return pltpu.make_async_remote_copy(
            src_ref=panel0.at[:, 0] if step == 0 else drows.at[held],
            dst_ref=drows.at[held],
            send_sem=d_send.at[3 + step],
            recv_sem=d_recv.at[3 + step],
            device_id=(y_peer(0, 1), c),
            device_id_type=MESH,
        )

    b_row = lax.rem(c, 8)
    b_y, b_core = b_row // 2, b_row % 2
    b_root, b_even = r == b_row, core == b_core

    def b_out(step):
        return pltpu.make_async_remote_copy(
            src_ref=brows,
            dst_ref=brows,
            send_sem=b_send.at[step - 1],
            recv_sem=b_recv.at[step - 1],
            device_id=(y_peer(step), c),
            device_id_type=MESH,
        )

    b_pair = pltpu.make_async_remote_copy(
        src_ref=brows,
        dst_ref=brows,
        send_sem=b_send.at[3],
        recv_sem=b_recv.at[3],
        device_id=(y_peer(0, 1), c),
        device_id_type=MESH,
    )

    def b_start():
        @pl.when(b_root)
        def _():
            low = c < 8
            for s in range(16):
                brows[0, s] = jnp.where(low, panel0[s, 0], panel1[s, 0])
                brows[1, s] = jnp.where(low, panel1[s, 1], panel1[s, 2])
            for step in (1, 3, 2):
                b_out(step).start()
            b_pair.start()

    def b_finish():
        for step in (1, 2, 3):

            @pl.when(jnp.logical_and(b_even, lax.rem(b_y + step, 4) == y))
            def _():
                b_out(step).wait_recv()
                b_pair.start()

        @pl.when(b_root)
        def _():
            for step in (1, 2, 3):
                b_out(step).wait_send()

        @pl.when(b_even)
        def _():
            b_pair.wait_send()

        @pl.when(jnp.logical_not(b_even))
        def _():
            b_pair.wait_recv()

    for g in range(4):
        s0(g)
    s1(0)
    s1(1)
    s2(0)
    s3(0)
    s4(0)
    s5(0)
    s6(0)
    s2(1)
    s7(0)
    for step in (1, 3, 2):
        d_out(step).start()
    d_pair(0).start()
    drows[r] = panel0[:, 0]
    s1(2)
    s1(3)
    s3(1)
    s4(1)
    s5(1)
    for step in (1, 3, 2):
        d_out(step).wait_recv()
        d_pair(4 - step).start()
    for step in range(4):
        d_pair(step).wait_recv()

    row = lax.broadcasted_iota(I32, (TILE, TILE), 0)
    col = lax.broadcasted_iota(I32, (TILE, TILE), 1)
    for k in range(PB):
        for i in range(k, PB):
            cols[k, pl.ds(i * TILE, 64), :] = drows[i, k]
            cols[k, pl.ds(i * TILE + 64, 64), :] = drows[i, partner_slot(k)]
        square = cols[k, pl.ds(k * TILE, TILE), :]
        low = jnp.where(row >= col, square, 0.0)
        cols[k, pl.ds(k * TILE, TILE), :] = low + jnp.where(row > col, square, 0.0).T
    inv[...] = jnp.zeros_like(inv)

    progress = {
        0: [(s6, 1)],
        1: [(s7, 1), (b_start, None), (s2, 2)],
        2: [(s2, 3), (s3, 2), (s3, 3)],
        3: [(s4, 2), (s4, 3)],
        4: [(s5, 2), (s5, 3)],
        5: [],
        6: [(s6, 2), (s6, 3)],
        7: [(b_finish, None)],
    }

    def step_tile(k, carry):
        square = cols[k, pl.ds(pl.multiple_of(k * TILE, TILE), TILE), :]
        upper, inverse = factor_tile(square)
        cols[k, pl.ds(pl.multiple_of(k * TILE, TILE), TILE), :] = upper.T
        for j in range(PB):

            @pl.when(k == j)
            def _():
                here = pl.ds(j * TILE, TILE)
                if j > 0:
                    inv[here, : j * TILE] = -dot(inverse, inv[here, : j * TILE], NN)
                inv[here, here] = inverse
                if j + 1 < PB:
                    below = pl.ds((j + 1) * TILE, (PB - 1 - j) * TILE)
                    lower = dot(cols[j, below, :], inverse, NTC)
                    cols[j, below, :] = lower
                    for i in range(j + 1, PB):
                        first_row = (i - j - 1) * TILE
                        rest = pl.ds(i * TILE, (PB - i) * TILE)
                        cols[i, rest, :] = cols[i, rest, :] - dot(
                            lower[first_row:], lower[first_row : first_row + TILE], NTC
                        )
                    inv[below, : (j + 1) * TILE] += dot(lower, inv[here, : (j + 1) * TILE], NN)
                for act, g in progress[j]:
                    if g is None:
                        act()
                    else:
                        act(g)

        return carry

    lax.fori_loop(0, PB, step_tile, 0)

    def b_rows(slot_list):
        halves = [jnp.concatenate([brows[q, s] for s in slot_list], 1) for q in range(2)]
        return halves

    top = b_rows(list(range(8)))
    bottom = b_rows([partner_slot(k) for k in range(8)])
    mine = jnp.concatenate([top[0], bottom[0], top[1], bottom[1]], 0)
    half = dot(mine, inv[...], NTC)
    weights = dot(half, inv[...], NN)
    panel_column = c < PB
    own = inv[pl.ds(pl.multiple_of(lax.rem(c, 8) * TILE, TILE), TILE), :]
    weights = jnp.concatenate([jnp.where(panel_column, -own, weights[:TILE]), weights[TILE:]], 0)
    high = weights.astype(BF16)
    wt_hi[...] = high
    wt_lo[...] = (weights - high.astype(F32)).astype(BF16)

    assemble(1, got1, sum1)

    def finish_rows(g, t, carry):
        panel, lo = panels[g], GROUPS[g][0]
        for h in range(2):
            order = list(range(8)) if h == 0 else [partner_slot(k) for k in range(8)]
            rows = jnp.concatenate([panel[s, t - lo] for s in order], 1)
            rows_hi = rows.astype(BF16)
            rows_lo = (rows - rows_hi.astype(F32)).astype(BF16)
            update = lax.dot_general(rows_hi, wt_hi[...], NTC, preferred_element_type=F32)
            update += lax.dot_general(rows_lo, wt_hi[...], NTC, preferred_element_type=F32)
            update += lax.dot_general(rows_hi, wt_lo[...], NTC, preferred_element_type=F32)
            i = 8 * t + r
            base0, base1 = sum0[t, pl.ds(64 * h, 64), :], sum1[t, pl.ds(64 * h, 64), :]
            new0 = jnp.where(panel_column, 0.0, base0) - update[:, :TILE]
            new1 = base1 - update[:, TILE:]
            out[t, pl.ds(128 * h, 64, stride=2), :] = jnp.where(i >= c, new0, base0)
            out[t, pl.ds(128 * h + 1, 64, stride=2), :] = jnp.where(i >= 16 + c, new1, base1)
        return carry

    block = cols[lax.rem(c, 8), pl.ds(pl.multiple_of(r * TILE, TILE), TILE), :]
    factored = jnp.logical_and(panel_column, r >= c)
    out[0, pl.ds(0, TILE, stride=2), :] = jnp.where(factored, block, sum0[0])
    out[0, pl.ds(1, TILE, stride=2), :] = sum1[0]
    lax.fori_loop(1, 4, functools.partial(finish_rows, 1), 0)
    s7(2)
    lax.fori_loop(4, 17, functools.partial(finish_rows, 2), 0)
    s7(3)
    lax.fori_loop(17, 24, functools.partial(finish_rows, 3), 0)

    for ct in range(2):
        for step in range(1, 8):
            child_copy(ct, step).wait_send()
    for g in range(4):

        @pl.when(source)
        def _():
            spread(g).wait_send()

    for spec in started:
        move(*spec).wait_send()
    for step in range(1, 4):
        d_out(step).wait_send()
    for step in range(4):
        d_pair(step).wait_send()


def shards(front, child_one, child_two, map_one, map_two, owner_one, owner_two):
    vmem = pl.BlockSpec(memory_space=pltpu.VMEM)
    smem = pl.BlockSpec(memory_space=pltpu.SMEM)
    dma = pltpu.SemaphoreType.DMA
    out = pl.pallas_call(
        kernel,
        out_shape=jax.ShapeDtypeStruct((NT, 256, TILE), F32),
        in_specs=[vmem] * 3 + [smem] * 4,
        out_specs=vmem,
        scratch_shapes=[
            pltpu.VMEM((8, 3, TILE, TILE), F32),
            pltpu.VMEM((8, 3, TILE, TILE), F32),
            pltpu.VMEM((9, 3, TILE, TILE), F32),
            pltpu.VMEM((9, 3, TILE, TILE), F32),
            pltpu.VMEM((NT, TILE, TILE), F32),
            pltpu.VMEM((NT, TILE, TILE), F32),
            *[pltpu.VMEM((16, hi - lo, 64, TILE), F32) for lo, hi, _ in GROUPS],
            pltpu.VMEM((8, 16, 64, TILE), F32),
            pltpu.VMEM((2, 16, 64, TILE), F32),
            pltpu.VMEM((PB, PB * TILE, TILE), F32),
            pltpu.VMEM((PB * TILE, PB * TILE), F32),
            pltpu.VMEM((256, PB * TILE), BF16),
            pltpu.VMEM((256, PB * TILE), BF16),
            pltpu.SMEM((128,), I32),
            pltpu.SMEM((32,), I32),
            dma((2, 7)), dma((2, 7)),
            dma((4,)), dma((4,)),
            dma((4, 20)), dma((4, 20)),
            dma((7,)), dma((7,)),
            dma((4,)), dma((4,)),
        ],
        compiler_params=pltpu.CompilerParams(
            collective_id=0, has_side_effects=True, vmem_limit_bytes=60 * 2**20
        ),
    )(
        front.reshape(NT, 256, TILE),
        child_one.reshape(8, 256, TILE),
        child_two.reshape(16, 256, TILE),
        map_one, map_two, owner_one, owner_two,
    )
    return out.reshape(front.shape)


def solution(mesh):
    placed = P(None, "row", None, None, "col", None)
    return jax.shard_map(
        shards,
        mesh=mesh,
        in_specs=(placed, placed, placed, P(), P(), P(), P()),
        out_specs=placed,
        check_vma=False,
    )
```

```python
import functools

import jax
import jax.numpy as jnp
from jax import lax
from jax.experimental import pallas as pl
from jax.experimental.pallas import tpu as pltpu
from jax.sharding import PartitionSpec as P

F32, BF16, I32 = jnp.float32, jnp.bfloat16, jnp.int32
HIGHEST = lax.Precision.HIGHEST
MESH = pl.DeviceIdType.MESH
TILE, PB, NT = 128, 8, 24
LEAF = 16
NN = (((1,), (0,)), ((), ()))
NTC = (((1,), (1,)), ((), ()))
TN = (((0,), (0,)), ((), ()))
GROUPS = ((1, 4, False), (4, 17, True), (17, 24, False))
CHUNKS = ((0, 1), (1, 4), (4, 8))
STEPS = (1, 7, 2, 6, 3, 5, 4)


def dot(a, b, dims):
    return lax.dot_general(a, b, dims, precision=HIGHEST, preferred_element_type=F32)


def split3(v):
    high = v.astype(BF16)
    rest = v - high.astype(F32)
    middle = rest.astype(BF16)
    low = (rest - middle.astype(F32)).astype(BF16)
    return [part.astype(F32) for part in (high, middle, low)]


def rank_update(a, b):
    ah, am, al = split3(a)
    bh, bm, bl = split3(b)
    left = jnp.concatenate([ah, ah, am, ah, am, al], 0).astype(BF16)
    right = jnp.concatenate([bl, bm, bm, bh, bh, bh], 0).astype(BF16)
    return lax.dot_general(left, right, TN, preferred_element_type=F32)


def leaf(rows_u, rows_v, offset):
    count = rows_u.shape[0]
    index = lax.broadcasted_iota(I32, (count, TILE), 0)
    cols = [
        jnp.broadcast_to(rows_u[:, offset + k : offset + k + 1], (count, TILE)) for k in range(count)
    ]
    scale = jnp.zeros((count, TILE), F32)
    for j in range(count):
        pivot = cols[j][j : j + 1, :]
        scale = jnp.where(index == j, lax.rsqrt(pivot), scale)
        if j + 1 < count:
            ratio = cols[j] * (1.0 / pivot)
            for k in range(j + 1, count):
                cols[k] = cols[k] - ratio * cols[k][j : j + 1, :]
            ratio = jnp.where(index > j, ratio, 0.0)
            rows_u = rows_u - ratio * rows_u[j : j + 1, :]
            rows_v = rows_v - ratio * rows_v[j : j + 1, :]
    return rows_u * scale, rows_v * scale


def factor_tile(square):
    row = lax.broadcasted_iota(I32, (TILE, TILE), 0)
    col = lax.broadcasted_iota(I32, (TILE, TILE), 1)
    unit = jnp.where(row == col, 1.0, 0.0).astype(F32)
    count = TILE // LEAF
    left = [square[i * LEAF : (i + 1) * LEAF] for i in range(count)]
    right = [unit[i * LEAF : (i + 1) * LEAF] for i in range(count)]
    for b in range(count):
        left[b], right[b] = leaf(left[b], right[b], b * LEAF)
        if b + 1 < count:
            change = rank_update(left[b], jnp.concatenate([left[b], right[b]], 1))
            for i in range(b + 1, count):
                left[i] = left[i] - change[i * LEAF : (i + 1) * LEAF, :TILE]
                right[i] = right[i] - change[i * LEAF : (i + 1) * LEAF, TILE:]
    upper = jnp.where(col >= row, jnp.concatenate(left, 0), 0.0)
    inverse = jnp.where(col <= row, jnp.concatenate(right, 0), 0.0)
    return upper, inverse


def partner_slot(c):
    return 12 - 4 * (c // 4) + c % 4


def kernel(
    front_in, one_in, two_in, map_one, map_two, own_one, own_two, out,
    front, one, two, stage_d, stage0, stage1, got_d, got0, got1, sum0, sum1,
    panel_a, panel_b, panel_c, dplane, drows, brows, diag, lmat, inv, half, wt_hi, wt_lo,
    slots, table,
    load, dchild_send, dchild_recv, child_send, child_recv, spread_send, spread_recv, ring_send, ring_recv,
    dx_send, dx_recv, dz_send, dz_recv, d_send, d_recv, b_send, b_recv,
):
    r, c = lax.axis_index("row"), lax.axis_index("col")
    y, core = r // 2, r % 2
    x, z = c // 4, c % 4
    source = x < 2
    other = jnp.logical_not(source)
    partner = (3 - x) * 4 + z
    panels = (panel_a, panel_b, panel_c)

    def at_col(dx, dz):
        return lax.rem(x + dx + 4, 4) * 4 + lax.rem(z + dz + 4, 4)

    def row_peer(step):
        return lax.rem(r + step, 8)

    def y_peer(step, across=0):
        return lax.rem(y + step, 4) * 2 + (core if across == 0 else 1 - core)

    barrier = pltpu.get_barrier_semaphore()
    for step in range(1, 8):
        pl.semaphore_signal(barrier, inc=1, device_id=(row_peer(step), c), device_id_type=MESH)
    for step in range(1, 4):
        pl.semaphore_signal(barrier, inc=1, device_id=(r, at_col(step, 0)), device_id_type=MESH)
        pl.semaphore_signal(barrier, inc=1, device_id=(r, at_col(0, step)), device_id_type=MESH)

    loads = [
        pltpu.make_async_copy(a, b, load.at[i])
        for i, (a, b) in enumerate(((one_in, one), (two_in, two), (front_in, front)))
    ]
    for copy in loads:
        copy.start()

    def find_one(g, carry):
        seen, picks = carry[0], list(carry[1:])
        for v in range(8):
            mine = own_one[8 * g + v] == r
            picks[v] = jnp.where(mine, seen, picks[v])
            seen = seen + mine.astype(I32)
        return (seen, *picks)

    picks_one = lax.fori_loop(0, 8, find_one, (jnp.int32(0),) * 9)[1:]

    def find_two(g, carry):
        seen, first, second = carry[0], list(carry[1:9]), list(carry[9:])
        for v in range(8):
            mine = own_two[8 * g + v] == r
            first[v] = jnp.where(mine, second[v], first[v])
            second[v] = jnp.where(mine, seen, second[v])
            seen = seen + mine.astype(I32)
        return (seen, *first, *second)

    picks_two = lax.fori_loop(0, 16, find_two, (jnp.int32(0),) * 17)[1:]
    for v in range(8):
        slots[v] = jnp.minimum(picks_one[v], 7)
        slots[8 + v] = jnp.minimum(picks_two[v], 15)
        slots[16 + v] = jnp.minimum(picks_two[8 + v], 15)

    def stage_diagonal():
        def body(v, carry):
            pick = pl.ds(0, TILE, stride=2)
            stage_d[v] = jnp.where(own_one[v] == r, one[slots[v], pick, :], 0.0) + jnp.where(
                own_two[v] == r, two[slots[8 + v], pick, :], 0.0
            )
            return carry

        lax.fori_loop(0, 8, body, 0)

    def stage(ct, buffer):
        def body(v, carry):
            pick = pl.ds(ct, TILE, stride=2)
            buffer[v, 0] = one[slots[v], pick, :]
            buffer[v, 1] = two[slots[8 + v], pick, :]
            buffer[v, 2] = two[slots[16 + v], pick, :]
            return carry

        lax.fori_loop(0, 8, body, 0)

    def dchild_copy(step):
        peer = row_peer(step)
        return pltpu.make_async_remote_copy(
            src_ref=stage_d.at[peer],
            dst_ref=got_d.at[r],
            send_sem=dchild_send.at[step - 1],
            recv_sem=dchild_recv.at[step - 1],
            device_id=(peer, c),
            device_id_type=MESH,
        )

    def child_copy(ct, step):
        peer = row_peer(step)
        return pltpu.make_async_remote_copy(
            src_ref=(stage0, stage1)[ct].at[peer],
            dst_ref=(got0, got1)[ct].at[r],
            send_sem=child_send.at[ct, step - 1],
            recv_sem=child_recv.at[ct, step - 1],
            device_id=(peer, c),
            device_id_type=MESH,
        )

    loads[0].wait()
    loads[1].wait()
    stage_diagonal()
    pl.semaphore_wait(barrier, 13)

    @pl.when(source)
    def _():
        for step in STEPS:
            dchild_copy(step).start()

    stage(0, stage0)
    for step in STEPS:
        child_copy(0, step).start()
    stage(1, stage1)
    for buffer, staged in ((got0, stage0), (got1, stage1)):
        buffer[r] = staged[r]
        buffer[8] = jnp.zeros((3, TILE, TILE), F32)
    got_d[r] = stage_d[r]

    sources = [own_two[8 * g + r] for g in range(16)]
    for g in range(16):
        rank = jnp.int32(0)
        for h in range(g):
            rank = rank + (sources[h] == sources[g]).astype(I32)
        table[g] = jnp.clip(sources[g], 0, 7)
        table[16 + g] = jnp.minimum(rank, 1)

    def find_targets(t, carry):
        at_one, at_two = carry
        hit_one = map_one[8 * at_one] // 8 == t
        hit_two = map_two[8 * at_two] // 8 == t
        slots[32 + t] = jnp.where(hit_one, jnp.clip(own_one[8 * at_one + r], 0, 7), 8)
        slots[64 + t] = jnp.where(hit_two, table[at_two], 8)
        slots[96 + t] = jnp.where(hit_two, table[16 + at_two] + 1, 1)
        return (
            jnp.minimum(at_one + hit_one.astype(I32), 7),
            jnp.minimum(at_two + hit_two.astype(I32), 15),
        )

    lax.fori_loop(0, NT, find_targets, (jnp.int32(0), jnp.int32(0)))
    loads[2].wait()

    def assemble(ct, buffer, total):
        for step in STEPS:
            child_copy(ct, step).wait_recv()

        def body(t, carry):
            total[t] = (
                front[t, pl.ds(ct, TILE, stride=2), :] + buffer[slots[32 + t], 0]
            ) + buffer[slots[64 + t], slots[96 + t]]
            return carry

        lax.fori_loop(0, NT, body, 0)

    def dx_copy(step):
        held = lax.rem(c, 8)
        return pltpu.make_async_remote_copy(
            src_ref=dplane.at[held],
            dst_ref=dplane.at[held],
            send_sem=dx_send.at[step - 1],
            recv_sem=dx_recv.at[lax.rem(x, 2)],
            device_id=(r, at_col(step, 0)),
            device_id_type=MESH,
        )

    def dx_arrival(sx):
        held = 4 * sx + z
        return pltpu.make_async_remote_copy(
            src_ref=dplane.at[held],
            dst_ref=dplane.at[held],
            send_sem=dx_send.at[0],
            recv_sem=dx_recv.at[sx],
            device_id=(r, at_col(1, 0)),
            device_id_type=MESH,
        )

    def dz_copy(sx, step, back=0):
        held = 4 * sx + lax.rem(z + 4 - back, 4)
        return pltpu.make_async_remote_copy(
            src_ref=dplane.at[held],
            dst_ref=dplane.at[held],
            send_sem=dz_send.at[sx, step - 1],
            recv_sem=dz_recv.at[sx, step - 1],
            device_id=(r, at_col(0, step)),
            device_id_type=MESH,
        )

    @pl.when(source)
    def _():
        for step in STEPS:
            dchild_copy(step).wait_recv()
        total = got_d[0]
        for s in range(1, 8):
            total = total + got_d[s]
        dplane[lax.rem(c, 8)] = front[0, pl.ds(0, TILE, stride=2), :] + total
        for step in (1, 3, 2):
            dx_copy(step).start()

    for sx in range(2):

        @pl.when(x != sx)
        def _():
            dx_arrival(sx).wait_recv()

        for step in (1, 3, 2):
            dz_copy(sx, step).start()
    for sx in range(2):
        for step in (1, 3, 2):
            dz_copy(sx, step, step).wait_recv()

    def d_out(q, step):
        lo, hi = CHUNKS[q]
        return pltpu.make_async_remote_copy(
            src_ref=dplane.at[pl.ds(lo, hi - lo)],
            dst_ref=drows.at[r, pl.ds(lo, hi - lo)],
            send_sem=d_send.at[q, step - 1],
            recv_sem=d_recv.at[q, step - 1],
            device_id=(y_peer(step), c),
            device_id_type=MESH,
        )

    def d_pair(q, step):
        lo, hi = CHUNKS[q]
        held = y_peer(step)
        return pltpu.make_async_remote_copy(
            src_ref=dplane.at[pl.ds(lo, hi - lo)] if step == 0 else drows.at[held, pl.ds(lo, hi - lo)],
            dst_ref=drows.at[held, pl.ds(lo, hi - lo)],
            send_sem=d_send.at[q, 3 + step],
            recv_sem=d_recv.at[q, 3 + step],
            device_id=(y_peer(0, 1), c),
            device_id_type=MESH,
        )

    def d_start(q):
        @pl.when(r >= CHUNKS[q][0])
        def _():
            for step in (1, 3, 2):
                d_out(q, step).start()
            d_pair(q, 0).start()

    def d_relay(q):
        for step in (1, 3, 2):

            @pl.when(y_peer(4 - step) >= CHUNKS[q][0])
            def _():
                d_out(q, step).wait_recv()
                d_pair(q, 4 - step).start()

    def d_wait(q):
        for step in range(4):

            @pl.when(y_peer(step, 1) >= CHUNKS[q][0])
            def _():
                d_pair(q, step).wait_recv()

    def d_end(q):
        @pl.when(r >= CHUNKS[q][0])
        def _():
            for step in (1, 3, 2):
                d_out(q, step).wait_send()
            d_pair(q, 0).wait_send()

        for step in (1, 3, 2):

            @pl.when(y_peer(4 - step) >= CHUNKS[q][0])
            def _():
                d_pair(q, 4 - step).wait_send()

    for q in range(3):
        d_start(q)
    drows[r] = dplane[...]

    assemble(0, got0, sum0)

    @pl.when(source)
    def _():
        for g in range(3):
            lo, hi, _ = GROUPS[g]
            panels[g][c] = sum0[lo:hi, :64, :]

    def spread(g):
        lo, hi, _ = GROUPS[g]
        return pltpu.make_async_remote_copy(
            src_ref=sum0.at[pl.ds(lo, hi - lo), pl.ds(64, 64)],
            dst_ref=panels[g].at[partner],
            send_sem=spread_send.at[g],
            recv_sem=spread_recv.at[g],
            device_id=(r, partner),
            device_id_type=MESH,
        )

    def part(slot, g, half):
        lo, hi, _ = GROUPS[g]
        count, panel = hi - lo, panels[g]
        upper = (count + 1) // 2
        if half is None:
            return panel.at[slot]
        return panel.at[slot, pl.ds(0, upper)] if half == 0 else panel.at[slot, pl.ds(upper, count - upper)]

    def move(g, axis, da, db, direction, half, index):
        x_first = GROUPS[g][2]
        offset = (da, db) if x_first else (db, da)
        along = (direction, 0) if (axis == 0) == x_first else (0, direction)
        ref = part(at_col(*offset), g, half)
        return pltpu.make_async_remote_copy(
            src_ref=ref,
            dst_ref=ref,
            send_sem=ring_send.at[g, index],
            recv_sem=ring_recv.at[g, index],
            device_id=(r, at_col(*along)),
            device_id_type=MESH,
        )

    def wait(spec):
        g, axis, da, db, direction, half, index = spec
        back = (da - direction, db) if axis == 0 else (da, db - direction)
        move(g, axis, back[0], back[1], direction, half, index).wait_recv()

    def first(g, k):
        return (g, 0, 0, 0, (1, -1)[k], None, k)

    def first_on(g, k):
        return (g, 0, (-1, 1)[k], 0, (1, -1)[k], k, 2 + k)

    def second(g, q, k):
        return (g, 1, (0, -1, 1, 2)[q], 0, (1, -1)[k], None, 4 + 4 * q + k)

    def second_on(g, q, k):
        return (g, 1, (0, -1, 1, 2)[q], (-1, 1)[k], (1, -1)[k], k, 6 + 4 * q + k)

    started = []

    def start(spec):
        started.append(spec)
        move(*spec).start()

    def own_blocks(g):
        return [first(g, 0), first(g, 1), second(g, 0, 0), second(g, 0, 1)]

    def s1(g):
        @pl.when(other)
        def _():
            spread(g).wait_recv()
            for spec in own_blocks(g):
                move(*spec).start()

    def s2(g):
        for k in range(2):
            wait(first(g, k))
            start(first_on(g, k))
        for q in (1, 2):
            for k in range(2):
                start(second(g, q, k))

    def s3(g):
        for k in range(2):
            wait(second(g, 0, k))
            start(second_on(g, 0, k))

    def s4(g):
        for k in range(2):
            wait(first_on(g, k))
        for k in range(2):
            start(second(g, 3, k))

    def s5(g):
        for q in (1, 2):
            for k in range(2):
                wait(second(g, q, k))
                start(second_on(g, q, k))

    def s6(g):
        for k in range(2):
            wait(second(g, 3, k))
            start(second_on(g, 3, k))

    def s7(g):
        for q in range(4):
            for k in range(2):
                wait(second_on(g, q, k))

    b_row = lax.rem(c, 8)
    b_y, b_core = b_row // 2, b_row % 2
    b_root, b_even = r == b_row, core == b_core

    def b_out(step):
        return pltpu.make_async_remote_copy(
            src_ref=brows,
            dst_ref=brows,
            send_sem=b_send.at[step - 1],
            recv_sem=b_recv.at[step - 1],
            device_id=(y_peer(step), c),
            device_id_type=MESH,
        )

    b_pair = pltpu.make_async_remote_copy(
        src_ref=brows,
        dst_ref=brows,
        send_sem=b_send.at[3],
        recv_sem=b_recv.at[3],
        device_id=(y_peer(0, 1), c),
        device_id_type=MESH,
    )

    def b_start(_):
        @pl.when(b_root)
        def _():
            for s in range(16):
                brows[0, s] = jnp.where(source, 0.0, panel_a[s, 0])
                brows[1, s] = jnp.where(source, panel_a[s, 1], panel_a[s, 2])
            for step in (1, 3, 2):
                b_out(step).start()
            b_pair.start()

    def b_relay(_):
        for step in (1, 2, 3):

            @pl.when(jnp.logical_and(b_even, lax.rem(b_y + step, 4) == y))
            def _():
                b_out(step).wait_recv()
                b_pair.start()

    def b_wait():
        @pl.when(jnp.logical_not(b_even))
        def _():
            b_pair.wait_recv()

    def b_end():
        @pl.when(b_root)
        def _():
            for step in (1, 2, 3):
                b_out(step).wait_send()

        @pl.when(b_even)
        def _():
            b_pair.wait_send()

    def child1(_):
        for step in STEPS:
            child_copy(1, step).start()

    for g in (0, 2, 1):

        @pl.when(source)
        def _():
            spread(g).start()

    for g in (0, 2, 1):
        started.extend(own_blocks(g))

        @pl.when(source)
        def _():
            for spec in own_blocks(g):
                move(*spec).start()

    d_relay(0)
    d_wait(0)

    row = lax.broadcasted_iota(I32, (TILE, TILE), 0)
    col = lax.broadcasted_iota(I32, (TILE, TILE), 1)
    inv[...] = jnp.zeros_like(inv)

    a, b, e = 0, 1, 2
    before = {
        0: [(s1, a)],
        1: [(s2, a)],
        2: [(s2, e), (s4, a)],
        3: [(s6, a), (s2, b)],
        4: [(s3, b)],
        5: [(s4, b)],
        6: [(s5, b)],
        7: [(b_relay, a)],
    }
    after = {
        0: [(d_relay, 1), (d_wait, 1), (d_relay, 2), (child1, 0), (s1, e)],
        1: [(s1, b), (s3, a)],
        2: [(s5, a), (s3, e), (d_wait, 2)],
        3: [(s4, e), (s7, a), (b_start, 0)],
        4: [(s5, e)],
        5: [(s6, e)],
        6: [],
        7: [(s6, b)],
    }

    def step_tile(k, carry):
        for j in range(PB):

            @pl.when(k == j)
            def _():
                for act, g in before[j]:
                    act(g)
                here = pl.ds(j * TILE, TILE)
                square = drows[j, j]
                square = jnp.where(row >= col, square, 0.0) + jnp.where(row > col, square, 0.0).T
                below = [drows[i, j] for i in range(j + 1, PB)]
                if j == 0:
                    diag[...] = square
                    lmat[TILE:, here] = jnp.concatenate(below, 0)
                else:
                    done = pl.ds(0, j * TILE)
                    left = lmat[here, done]
                    diag[...] = square - dot(left, left, NTC)
                    if below:
                        under = pl.ds((j + 1) * TILE, (PB - 1 - j) * TILE)
                        lmat[under, here] = jnp.concatenate(below, 0) - dot(lmat[under, done], left, NTC)
                    inv[here, done] = dot(left, inv[done, done], NN)

        upper, inverse = factor_tile(diag[...])
        diag[...] = inverse
        lmat_here = upper.T
        for j in range(PB):

            @pl.when(k == j)
            def _():
                here = pl.ds(j * TILE, TILE)
                inverse = diag[...]
                lmat[here, here] = lmat_here
                if j > 0:
                    done = pl.ds(0, j * TILE)
                    inv[here, done] = -dot(inverse, inv[here, done], NN)
                inv[here, here] = inverse
                if j + 1 < PB:
                    under = pl.ds((j + 1) * TILE, (PB - 1 - j) * TILE)
                    lmat[under, here] = dot(lmat[under, here], inverse, NTC)
                for act, g in after[j]:
                    act(g)

        return carry

    lax.fori_loop(0, PB, step_tile, 0)
    b_wait()

    top, bottom = list(range(8)), [partner_slot(k) for k in range(8)]
    mine = jnp.concatenate(
        [jnp.concatenate([brows[q, s] for s in order], 1) for q in range(2) for order in (top, bottom)], 0
    )
    for k in range(4):
        here, upto = pl.ds(256 * k, 256), 256 * (k + 1)
        half[:, here] = dot(mine[:, :upto], inv[here, :upto], NTC)
    own = inv.at[pl.ds(pl.multiple_of(lax.rem(c, 8) * TILE, TILE), TILE)]
    for k in range(4):
        here, rest = pl.ds(256 * k, 256), pl.ds(256 * k, 1024 - 256 * k)
        weights = dot(half[:, rest], inv[rest, here], NN)
        weights = jnp.concatenate([jnp.where(source, -own[:, here], weights[:TILE]), weights[TILE:]], 0)
        high = weights.astype(BF16)
        wt_hi[:, here] = high
        wt_lo[:, here] = (weights - high.astype(F32)).astype(BF16)

    assemble(1, got1, sum1)

    def finish(g, lo, hi):
        panel, base = panels[g], GROUPS[g][0]
        count = hi - lo
        for h, order in enumerate((top, bottom)):
            rows = jnp.concatenate(
                [panel[s, lo - base : hi - base].reshape(count * 64, TILE) for s in order], 1
            )
            rows_hi = rows.astype(BF16)
            rows_lo = (rows - rows_hi.astype(F32)).astype(BF16)
            update = lax.dot_general(rows_hi, wt_hi[...], NTC, preferred_element_type=F32)
            update += lax.dot_general(rows_lo, wt_hi[...], NTC, preferred_element_type=F32)
            update += lax.dot_general(rows_hi, wt_lo[...], NTC, preferred_element_type=F32)
            for t in range(lo, hi):
                piece = update[64 * (t - lo) : 64 * (t - lo + 1)]
                base0, base1 = sum0[t, pl.ds(64 * h, 64), :], sum1[t, pl.ds(64 * h, 64), :]
                new0 = jnp.where(source, 0.0, base0) - piece[:, :TILE]
                new1 = base1 - piece[:, TILE:]
                if t < 4:
                    i = 8 * t + r
                    new0 = jnp.where(i >= c, new0, base0)
                    new1 = jnp.where(i >= 16 + c, new1, base1)
                out[t, pl.ds(128 * h, 64, stride=2), :] = new0
                out[t, pl.ds(128 * h + 1, 64, stride=2), :] = new1

    block = lmat[
        pl.ds(pl.multiple_of(r * TILE, TILE), TILE), pl.ds(pl.multiple_of(lax.rem(c, 8) * TILE, TILE), TILE)
    ]
    factored = jnp.logical_and(source, r >= c)
    out[0, pl.ds(0, TILE, stride=2), :] = jnp.where(factored, block, sum0[0])
    out[0, pl.ds(1, TILE, stride=2), :] = sum1[0]
    finish(a, 1, 4)
    s7(e)
    finish(e, 17, 24)
    s7(b)
    finish(b, 4, 11)
    finish(b, 11, 17)

    @pl.when(source)
    def _():
        for step in STEPS:
            dchild_copy(step).wait_send()
        for step in range(1, 4):
            dx_copy(step).wait_send()
        for g in range(3):
            spread(g).wait_send()

    for ct in range(2):
        for step in STEPS:
            child_copy(ct, step).wait_send()
    for sx in range(2):
        for step in range(1, 4):
            dz_copy(sx, step).wait_send()
    for spec in started:
        move(*spec).wait_send()
    for q in range(3):
        d_end(q)
    b_end()


def copy_kernel(source, out):
    out[...] = source[...]


def shards(front, child_one, child_two, map_one, map_two, owner_one, owner_two):
    whole = pl.BlockSpec(memory_space=pl.ANY)
    vmem = pl.BlockSpec(memory_space=pltpu.VMEM)
    smem = pl.BlockSpec(memory_space=pltpu.SMEM)
    dma = pltpu.SemaphoreType.DMA

    def space(*shape):
        return pltpu.VMEM(shape, F32)

    out = pl.pallas_call(
        kernel,
        out_shape=jax.ShapeDtypeStruct((NT, 256, TILE), F32),
        in_specs=[whole] * 3 + [smem] * 4,
        out_specs=vmem,
        scratch_shapes=[
            space(NT, 256, TILE), space(8, 256, TILE), space(16, 256, TILE),
            space(8, TILE, TILE), space(8, 3, TILE, TILE), space(8, 3, TILE, TILE),
            space(8, TILE, TILE), space(9, 3, TILE, TILE), space(9, 3, TILE, TILE),
            space(NT, TILE, TILE), space(NT, TILE, TILE),
            *[space(16, hi - lo, 64, TILE) for lo, hi, _ in GROUPS],
            space(8, TILE, TILE), space(8, 8, TILE, TILE), space(2, 16, 64, TILE),
            space(TILE, TILE), space(PB * TILE, PB * TILE), space(PB * TILE, PB * TILE),
            space(256, PB * TILE),
            pltpu.VMEM((256, PB * TILE), BF16), pltpu.VMEM((256, PB * TILE), BF16),
            pltpu.SMEM((128,), I32), pltpu.SMEM((32,), I32),
            dma((3,)), dma((7,)), dma((7,)), dma((2, 7)), dma((2, 7)),
            dma((3,)), dma((3,)), dma((3, 20)), dma((3, 20)),
            dma((3,)), dma((2,)), dma((2, 3)), dma((2, 3)), dma((3, 7)), dma((3, 7)),
            dma((4,)), dma((4,)),
        ],
        compiler_params=pltpu.CompilerParams(
            collective_id=0, has_side_effects=True, vmem_limit_bytes=60 * 2**20
        ),
    )(
        front.reshape(NT, 256, TILE),
        child_one.reshape(8, 256, TILE),
        child_two.reshape(16, 256, TILE),
        map_one, map_two, owner_one, owner_two,
    )
    block = pl.BlockSpec((4, 256, TILE), lambda i: (i, 0, 0))
    out = pl.pallas_call(
        copy_kernel,
        grid=(6,),
        out_shape=jax.ShapeDtypeStruct((NT, 256, TILE), F32),
        in_specs=[block],
        out_specs=block,
        compiler_params=pltpu.CompilerParams(vmem_limit_bytes=8 * 2**20),
    )(out)
    return out.reshape(front.shape)


def solution(mesh):
    placed = P(None, "row", None, None, "col", None)
    return jax.shard_map(
        shards,
        mesh=mesh,
        in_specs=(placed, placed, placed, P(), P(), P(), P()),
        out_specs=placed,
        check_vma=False,
    )
```

```python
import functools

import jax
import jax.numpy as jnp
from jax import lax
from jax.experimental import pallas as pl
from jax.experimental.pallas import tpu as pltpu
from jax.sharding import PartitionSpec as P

F32, BF16, I32 = jnp.float32, jnp.bfloat16, jnp.int32
HIGHEST = lax.Precision.HIGHEST
MESH = pl.DeviceIdType.MESH
TILE, PB, NT = 128, 8, 24
LEAF = 16
NN = (((1,), (0,)), ((), ()))
NTC = (((1,), (1,)), ((), ()))
TN = (((0,), (0,)), ((), ()))
GROUPS = ((1, 10, False), (10, 24, True))
CHUNKS = ((0, 1), (1, 4), (4, 8))
STEPS = (1, 7, 2, 6, 3, 5, 4)


def dot(a, b, dims):
    return lax.dot_general(a, b, dims, precision=HIGHEST, preferred_element_type=F32)


def split3(v):
    high = v.astype(BF16)
    rest = v - high.astype(F32)
    middle = rest.astype(BF16)
    low = (rest - middle.astype(F32)).astype(BF16)
    return [part.astype(F32) for part in (high, middle, low)]


def rank_update(a, b):
    ah, am, al = split3(a)
    bh, bm, bl = split3(b)
    left = jnp.concatenate([ah, ah, am, ah, am, al], 0).astype(BF16)
    right = jnp.concatenate([bl, bm, bm, bh, bh, bh], 0).astype(BF16)
    return lax.dot_general(left, right, TN, preferred_element_type=F32)


def leaf(rows_u, rows_v, offset):
    count = rows_u.shape[0]
    index = lax.broadcasted_iota(I32, (count, TILE), 0)
    cols = [
        jnp.broadcast_to(rows_u[:, offset + k : offset + k + 1], (count, TILE)) for k in range(count)
    ]
    scale = jnp.zeros((count, TILE), F32)
    for j in range(count):
        pivot = cols[j][j : j + 1, :]
        scale = jnp.where(index == j, lax.rsqrt(pivot), scale)
        if j + 1 < count:
            ratio = cols[j] * (1.0 / pivot)
            for k in range(j + 1, count):
                cols[k] = cols[k] - ratio * cols[k][j : j + 1, :]
            ratio = jnp.where(index > j, ratio, 0.0)
            rows_u = rows_u - ratio * rows_u[j : j + 1, :]
            rows_v = rows_v - ratio * rows_v[j : j + 1, :]
    return rows_u * scale, rows_v * scale


def factor_tile(square):
    row = lax.broadcasted_iota(I32, (TILE, TILE), 0)
    col = lax.broadcasted_iota(I32, (TILE, TILE), 1)
    unit = jnp.where(row == col, 1.0, 0.0).astype(F32)
    count = TILE // LEAF
    left = [square[i * LEAF : (i + 1) * LEAF] for i in range(count)]
    right = [unit[i * LEAF : (i + 1) * LEAF] for i in range(count)]
    for b in range(count):
        left[b], right[b] = leaf(left[b], right[b], b * LEAF)
        if b + 1 < count:
            change = rank_update(left[b], jnp.concatenate([left[b], right[b]], 1))
            for i in range(b + 1, count):
                left[i] = left[i] - change[i * LEAF : (i + 1) * LEAF, :TILE]
                right[i] = right[i] - change[i * LEAF : (i + 1) * LEAF, TILE:]
    upper = jnp.where(col >= row, jnp.concatenate(left, 0), 0.0)
    inverse = jnp.where(col <= row, jnp.concatenate(right, 0), 0.0)
    return upper, inverse


def partner_slot(c):
    return 12 - 4 * (c // 4) + c % 4


def kernel(
    front_in, one_in, two_in, map_one, map_two, own_one, own_two, out,
    front, one, two, stage0, stage2, stage1, got0, got2, got1, sum0, sum1,
    panel_a, panel_b, dplane, drows, brows, diag, lmat, inv, half, wt_hi, wt_lo,
    slots, table,
    load, child_send, child_recv, spread_send, spread_recv, ring_send, ring_recv,
    dx_send, dx_recv, dz_send, dz_recv, d_send, d_recv, bx_send, bx_recv, b_send, b_recv,
):
    r, c = lax.axis_index("row"), lax.axis_index("col")
    y, core = r // 2, r % 2
    x, z = c // 4, c % 4
    source = x < 2
    other = jnp.logical_not(source)
    partner = (3 - x) * 4 + z
    panels = (panel_a, panel_b)

    def at_col(dx, dz):
        return lax.rem(x + dx + 4, 4) * 4 + lax.rem(z + dz + 4, 4)

    def row_peer(step):
        return lax.rem(r + step, 8)

    def y_peer(step, across=0):
        return lax.rem(y + step, 4) * 2 + (core if across == 0 else 1 - core)

    barrier = pltpu.get_barrier_semaphore()
    for step in range(1, 8):
        pl.semaphore_signal(barrier, inc=1, device_id=(row_peer(step), c), device_id_type=MESH)
    for step in range(1, 4):
        pl.semaphore_signal(barrier, inc=1, device_id=(r, at_col(step, 0)), device_id_type=MESH)
        pl.semaphore_signal(barrier, inc=1, device_id=(r, at_col(0, step)), device_id_type=MESH)

    @pl.when(lax.rem(c, 8) == r)
    def _():
        for held in range(8):

            @pl.when(c != held)
            def _():
                pl.semaphore_signal(barrier, inc=1, device_id=(r, held), device_id_type=MESH)

    loads = [
        pltpu.make_async_copy(a, b, load.at[i])
        for i, (a, b) in enumerate(((one_in, one), (two_in, two), (front_in, front)))
    ]
    for copy in loads:
        copy.start()

    def find_one(g, carry):
        seen, picks = carry[0], list(carry[1:])
        for v in range(8):
            mine = own_one[8 * g + v] == r
            picks[v] = jnp.where(mine, seen, picks[v])
            seen = seen + mine.astype(I32)
        return (seen, *picks)

    picks_one = lax.fori_loop(0, 8, find_one, (jnp.int32(0),) * 9)[1:]

    def find_two(g, carry):
        seen, first, second = carry[0], list(carry[1:9]), list(carry[9:])
        for v in range(8):
            mine = own_two[8 * g + v] == r
            first[v] = jnp.where(mine, second[v], first[v])
            second[v] = jnp.where(mine, seen, second[v])
            seen = seen + mine.astype(I32)
        return (seen, *first, *second)

    picks_two = lax.fori_loop(0, 16, find_two, (jnp.int32(0),) * 17)[1:]
    for v in range(8):
        slots[v] = jnp.minimum(picks_one[v], 7)
        slots[8 + v] = jnp.minimum(picks_two[v], 15)
        slots[16 + v] = jnp.minimum(picks_two[8 + v], 15)

    def stage0_rows(v, carry):
        pick = pl.ds(0, TILE, stride=2)
        stage0[v, 0] = one[slots[v], pick, :]
        stage0[v, 1] = two[slots[8 + v], pick, :]
        stage2[v] = two[slots[16 + v], pick, :]
        return carry

    def stage1_rows(v, carry):
        pick = pl.ds(1, TILE, stride=2)
        stage1[v, 0] = one[slots[v], pick, :]
        stage1[v, 1] = two[slots[8 + v], pick, :]
        stage1[v, 2] = two[slots[16 + v], pick, :]
        return carry

    def child_copy(kind, step):
        peer = row_peer(step)
        return pltpu.make_async_remote_copy(
            src_ref=(stage0, stage1, stage2)[kind].at[peer],
            dst_ref=(got0, got1, got2)[kind].at[r],
            send_sem=child_send.at[kind, step - 1],
            recv_sem=child_recv.at[kind, step - 1],
            device_id=(peer, c),
            device_id_type=MESH,
        )

    loads[0].wait()
    loads[1].wait()
    lax.fori_loop(0, 8, stage0_rows, 0)
    pl.semaphore_wait(
        barrier, 13 + source.astype(I32) + jnp.logical_and(source, c != r).astype(I32)
    )
    for kind in (0, 2):
        for step in STEPS:
            child_copy(kind, step).start()
    lax.fori_loop(0, 8, stage1_rows, 0)
    for buffer, staged in ((got0, stage0), (got1, stage1), (got2, stage2)):
        buffer[r] = staged[r]
        buffer[8] = jnp.zeros(buffer.shape[1:], F32)

    sources = [own_two[8 * g + r] for g in range(16)]
    for g in range(16):
        rank = jnp.int32(0)
        for h in range(g):
            rank = rank + (sources[h] == sources[g]).astype(I32)
        table[g] = jnp.clip(sources[g], 0, 7)
        table[16 + g] = jnp.minimum(rank, 1)

    def find_targets(t, carry):
        at_one, at_two = carry
        hit_one = map_one[8 * at_one] // 8 == t
        hit_two = map_two[8 * at_two] // 8 == t
        slots[32 + t] = jnp.where(hit_one, jnp.clip(own_one[8 * at_one + r], 0, 7), 8)
        slots[64 + t] = jnp.where(hit_two, table[at_two], 8)
        slots[96 + t] = jnp.where(hit_two, table[16 + at_two] + 1, 1)
        return (
            jnp.minimum(at_one + hit_one.astype(I32), 7),
            jnp.minimum(at_two + hit_two.astype(I32), 15),
        )

    lax.fori_loop(0, NT, find_targets, (jnp.int32(0), jnp.int32(0)))
    loads[2].wait()

    def assemble0():
        for step in STEPS:
            child_copy(2, step).wait_recv()

        def body(t, carry):
            origin, second = slots[64 + t], slots[96 + t] == 2
            total = front[t, pl.ds(0, TILE, stride=2), :] + got0[slots[32 + t], 0]
            total = total + got0[jnp.where(second, 8, origin), 1]
            sum0[t] = total + got2[jnp.where(second, origin, 8)]
            return carry

        lax.fori_loop(0, NT, body, 0)

    def assemble1():
        for step in STEPS:
            child_copy(1, step).wait_recv()

        def body(t, carry):
            sum1[t] = (
                front[t, pl.ds(1, TILE, stride=2), :] + got1[slots[32 + t], 0]
            ) + got1[slots[64 + t], slots[96 + t]]
            return carry

        lax.fori_loop(0, NT, body, 0)

    def dx_copy(step):
        held = lax.rem(c, 8)
        return pltpu.make_async_remote_copy(
            src_ref=dplane.at[held],
            dst_ref=dplane.at[held],
            send_sem=dx_send.at[step - 1],
            recv_sem=dx_recv.at[lax.rem(x, 2)],
            device_id=(r, at_col(step, 0)),
            device_id_type=MESH,
        )

    def dx_arrival(sx):
        held = 4 * sx + z
        return pltpu.make_async_remote_copy(
            src_ref=dplane.at[held],
            dst_ref=dplane.at[held],
            send_sem=dx_send.at[0],
            recv_sem=dx_recv.at[sx],
            device_id=(r, at_col(1, 0)),
            device_id_type=MESH,
        )

    def dz_copy(sx, step, back=0):
        held = 4 * sx + lax.rem(z + 4 - back, 4)
        return pltpu.make_async_remote_copy(
            src_ref=dplane.at[held],
            dst_ref=dplane.at[held],
            send_sem=dz_send.at[sx, step - 1],
            recv_sem=dz_recv.at[sx, step - 1],
            device_id=(r, at_col(0, step)),
            device_id_type=MESH,
        )

    for step in STEPS:
        child_copy(0, step).wait_recv()

    @pl.when(source)
    def _():
        total = front[0, pl.ds(0, TILE, stride=2), :] + got0[jnp.clip(own_one[r], 0, 7), 0]
        dplane[lax.rem(c, 8)] = total + got0[jnp.clip(own_two[r], 0, 7), 1]
        for step in (1, 3, 2):
            dx_copy(step).start()

    for sx in range(2):

        @pl.when(x != sx)
        def _():
            dx_arrival(sx).wait_recv()

        for step in (1, 3, 2):
            dz_copy(sx, step).start()
    def d_out(q, step):
        lo, hi = CHUNKS[q]
        return pltpu.make_async_remote_copy(
            src_ref=dplane.at[pl.ds(lo, hi - lo)],
            dst_ref=drows.at[r, pl.ds(lo, hi - lo)],
            send_sem=d_send.at[q, step - 1],
            recv_sem=d_recv.at[q, step - 1],
            device_id=(y_peer(step), c),
            device_id_type=MESH,
        )

    def d_pair(q, step):
        lo, hi = CHUNKS[q]
        held = y_peer(step)
        return pltpu.make_async_remote_copy(
            src_ref=dplane.at[pl.ds(lo, hi - lo)] if step == 0 else drows.at[held, pl.ds(lo, hi - lo)],
            dst_ref=drows.at[held, pl.ds(lo, hi - lo)],
            send_sem=d_send.at[q, 3 + step],
            recv_sem=d_recv.at[q, 3 + step],
            device_id=(y_peer(0, 1), c),
            device_id_type=MESH,
        )

    def d_start(q):
        @pl.when(r >= CHUNKS[q][0])
        def _():
            for step in (1, 3, 2):
                d_out(q, step).start()
            d_pair(q, 0).start()

    def d_relay(q):
        for step in (1, 3, 2):

            @pl.when(y_peer(4 - step) >= CHUNKS[q][0])
            def _():
                d_out(q, step).wait_recv()
                d_pair(q, 4 - step).start()

    def d_wait(q):
        for step in range(4):

            @pl.when(y_peer(step, 1) >= CHUNKS[q][0])
            def _():
                d_pair(q, step).wait_recv()

    def d_end(q):
        @pl.when(r >= CHUNKS[q][0])
        def _():
            for step in (1, 3, 2):
                d_out(q, step).wait_send()
            d_pair(q, 0).wait_send()

        for step in (1, 3, 2):

            @pl.when(y_peer(4 - step) >= CHUNKS[q][0])
            def _():
                d_pair(q, 4 - step).wait_send()

    assemble0()

    @pl.when(source)
    def _():
        for g in range(2):
            lo, hi, _ = GROUPS[g]
            panels[g][c] = sum0[lo:hi, :64, :]

    def spread(g):
        lo, hi, _ = GROUPS[g]
        return pltpu.make_async_remote_copy(
            src_ref=sum0.at[pl.ds(lo, hi - lo), pl.ds(64, 64)],
            dst_ref=panels[g].at[partner],
            send_sem=spread_send.at[g],
            recv_sem=spread_recv.at[g],
            device_id=(r, partner),
            device_id_type=MESH,
        )

    def part(slot, g, half):
        lo, hi, _ = GROUPS[g]
        count, panel = hi - lo, panels[g]
        upper = (count + 1) // 2
        if half is None:
            return panel.at[slot]
        return panel.at[slot, pl.ds(0, upper)] if half == 0 else panel.at[slot, pl.ds(upper, count - upper)]

    def move(g, axis, da, db, direction, half, index):
        x_first = GROUPS[g][2]
        offset = (da, db) if x_first else (db, da)
        along = (direction, 0) if (axis == 0) == x_first else (0, direction)
        ref = part(at_col(*offset), g, half)
        return pltpu.make_async_remote_copy(
            src_ref=ref,
            dst_ref=ref,
            send_sem=ring_send.at[g, index],
            recv_sem=ring_recv.at[g, index],
            device_id=(r, at_col(*along)),
            device_id_type=MESH,
        )

    def wait(spec):
        g, axis, da, db, direction, half, index = spec
        back = (da - direction, db) if axis == 0 else (da, db - direction)
        move(g, axis, back[0], back[1], direction, half, index).wait_recv()

    def first(g, k):
        return (g, 0, 0, 0, (1, -1)[k], None, k)

    def first_on(g, k):
        return (g, 0, (-1, 1)[k], 0, (1, -1)[k], k, 2 + k)

    def second(g, q, k):
        return (g, 1, (0, -1, 1, 2)[q], 0, (1, -1)[k], None, 4 + 4 * q + k)

    def second_on(g, q, k):
        return (g, 1, (0, -1, 1, 2)[q], (-1, 1)[k], (1, -1)[k], k, 6 + 4 * q + k)

    started = []

    def start(spec):
        started.append(spec)
        move(*spec).start()

    def own_blocks(g):
        return [first(g, 0), first(g, 1), second(g, 0, 0), second(g, 0, 1)]

    def s1(g):
        @pl.when(other)
        def _():
            spread(g).wait_recv()
            for spec in own_blocks(g):
                move(*spec).start()

    def s2(g):
        for k in range(2):
            wait(first(g, k))
            start(first_on(g, k))
        for q in (1, 2):
            for k in range(2):
                start(second(g, q, k))

    def s3(g):
        for k in range(2):
            wait(second(g, 0, k))
            start(second_on(g, 0, k))

    def s4(g):
        for k in range(2):
            wait(first_on(g, k))
        for k in range(2):
            start(second(g, 3, k))

    def s5(g):
        for q in (1, 2):
            for k in range(2):
                wait(second(g, q, k))
                start(second_on(g, q, k))

    def s6(g):
        for k in range(2):
            wait(second(g, 3, k))
            start(second_on(g, 3, k))

    def s7(g):
        for q in range(4):
            for k in range(2):
                wait(second_on(g, q, k))

    b_row = lax.rem(c, 8)
    b_y, b_core = b_row // 2, b_row % 2
    b_root, b_even = r == b_row, core == b_core

    def bx_copy(q, t, target):
        held = lax.rem(c, 8)
        return pltpu.make_async_remote_copy(
            src_ref=sum0.at[t],
            dst_ref=brows.at[q, held],
            send_sem=bx_send.at[t - 1],
            recv_sem=bx_recv.at[q, held],
            device_id=(r, target),
            device_id_type=MESH,
        )

    def bx_arrival(q, held):
        return pltpu.make_async_remote_copy(
            src_ref=sum0.at[1],
            dst_ref=brows.at[q, held],
            send_sem=bx_send.at[0],
            recv_sem=bx_recv.at[q, held],
            device_id=(r, at_col(1, 0)),
            device_id_type=MESH,
        )

    def bx_start():
        @pl.when(source)
        def _():
            bx_copy(0, 1, r + 8).start()
            bx_copy(1, 3, r + 8).start()

        @pl.when(jnp.logical_and(source, c != r))
        def _():
            bx_copy(1, 2, r).start()

        @pl.when(jnp.logical_and(source, c == r))
        def _():
            brows[1, r] = sum0[2]

    def bx_end():
        @pl.when(source)
        def _():
            bx_copy(0, 1, r + 8).wait_send()
            bx_copy(1, 3, r + 8).wait_send()

        @pl.when(jnp.logical_and(source, c != r))
        def _():
            bx_copy(1, 2, r).wait_send()

    def b_out(q, step):
        return pltpu.make_async_remote_copy(
            src_ref=brows.at[q],
            dst_ref=brows.at[q],
            send_sem=b_send.at[q, step - 1],
            recv_sem=b_recv.at[q, step - 1],
            device_id=(y_peer(step), c),
            device_id_type=MESH,
        )

    def b_pair(q):
        return pltpu.make_async_remote_copy(
            src_ref=brows.at[q],
            dst_ref=brows.at[q],
            send_sem=b_send.at[q, 3],
            recv_sem=b_recv.at[q, 3],
            device_id=(y_peer(0, 1), c),
            device_id_type=MESH,
        )

    def with_b(q, condition):
        return condition if q == 1 else jnp.logical_and(condition, other)

    def b_start(_):
        for q in (1, 0):

            @pl.when(with_b(q, b_root))
            def _():
                for held in range(8):

                    @pl.when(c != held)
                    def _():
                        bx_arrival(q, held).wait_recv()

                for step in (1, 3, 2):
                    b_out(q, step).start()
                b_pair(q).start()

    def b_relay(_):
        for q in (1, 0):
            for step in (1, 2, 3):

                @pl.when(with_b(q, jnp.logical_and(b_even, lax.rem(b_y + step, 4) == y)))
                def _():
                    b_out(q, step).wait_recv()
                    b_pair(q).start()

    def b_wait():
        for q in (1, 0):

            @pl.when(with_b(q, jnp.logical_not(b_even)))
            def _():
                b_pair(q).wait_recv()

    def b_end():
        for q in (1, 0):

            @pl.when(with_b(q, b_root))
            def _():
                for step in (1, 2, 3):
                    b_out(q, step).wait_send()

            @pl.when(with_b(q, b_even))
            def _():
                b_pair(q).wait_send()

    def child1(_):
        for step in STEPS:
            child_copy(1, step).start()

    bx_start()
    for g in range(2):

        @pl.when(source)
        def _():
            spread(g).start()

    for g in range(2):
        started.extend(own_blocks(g))

        @pl.when(source)
        def _():
            for spec in own_blocks(g):
                move(*spec).start()

    for sx in range(2):
        for step in (1, 3, 2):
            dz_copy(sx, step, step).wait_recv()
    for q in range(3):
        d_start(q)
    drows[r] = dplane[...]
    d_relay(0)
    d_wait(0)

    row = lax.broadcasted_iota(I32, (TILE, TILE), 0)
    col = lax.broadcasted_iota(I32, (TILE, TILE), 1)
    inv[...] = jnp.zeros_like(inv)

    e, b = 0, 1
    before = {
        0: [(s1, e)],
        1: [(s1, b)],
        2: [(s2, e), (s3, e)],
        3: [],
        4: [(b_relay, 0), (s4, e)],
        5: [(s4, b)],
        6: [(s5, b)],
        7: [(s6, e)],
    }
    after = {
        0: [(d_relay, 1), (d_wait, 1), (b_start, 0)],
        1: [(d_relay, 2)],
        2: [(d_wait, 2)],
        3: [(s2, b), (s3, b)],
        4: [(child1, 0)],
        5: [(s5, e)],
        6: [],
        7: [(s6, b)],
    }

    def step_tile(k, carry):
        for j in range(PB):

            @pl.when(k == j)
            def _():
                for act, g in before[j]:
                    act(g)
                here = pl.ds(j * TILE, TILE)
                square = drows[j, j]
                square = jnp.where(row >= col, square, 0.0) + jnp.where(row > col, square, 0.0).T
                below = [drows[i, j] for i in range(j + 1, PB)]
                if j == 0:
                    diag[...] = square
                    lmat[TILE:, here] = jnp.concatenate(below, 0)
                else:
                    done = pl.ds(0, j * TILE)
                    left = lmat[here, done]
                    diag[...] = square - dot(left, left, NTC)
                    if below:
                        under = pl.ds((j + 1) * TILE, (PB - 1 - j) * TILE)
                        lmat[under, here] = jnp.concatenate(below, 0) - dot(lmat[under, done], left, NTC)
                    inv[here, done] = dot(left, inv[done, done], NN)

        upper, inverse = factor_tile(diag[...])
        diag[...] = inverse
        lmat_here = upper.T
        for j in range(PB):

            @pl.when(k == j)
            def _():
                here = pl.ds(j * TILE, TILE)
                inverse = diag[...]
                lmat[here, here] = lmat_here
                if j > 0:
                    done = pl.ds(0, j * TILE)
                    inv[here, done] = -dot(inverse, inv[here, done], NN)
                inv[here, here] = inverse
                if j + 1 < PB:
                    under = pl.ds((j + 1) * TILE, (PB - 1 - j) * TILE)
                    lmat[under, here] = dot(lmat[under, here], inverse, NTC)
                for act, g in after[j]:
                    act(g)

        return carry

    lax.fori_loop(0, PB, step_tile, 0)
    b_wait()

    top, bottom = list(range(8)), [partner_slot(k) for k in range(8)]
    unused = jnp.zeros((TILE, TILE), F32)
    mine = jnp.concatenate(
        [
            jnp.concatenate([jnp.where(source, unused, brows[0, s]) for s in range(8)], 1),
            jnp.concatenate([brows[1, s] for s in range(8)], 1),
        ],
        0,
    )
    for k in range(4):
        here, upto = pl.ds(256 * k, 256), 256 * (k + 1)
        half[:, here] = dot(mine[:, :upto], inv[here, :upto], NTC)
    own = inv.at[pl.ds(pl.multiple_of(lax.rem(c, 8) * TILE, TILE), TILE)]
    for k in range(4):
        here, rest = pl.ds(256 * k, 256), pl.ds(256 * k, 1024 - 256 * k)
        weights = dot(half[:, rest], inv[rest, here], NN)
        weights = jnp.concatenate([jnp.where(source, -own[:, here], weights[:TILE]), weights[TILE:]], 0)
        high = weights.astype(BF16)
        wt_hi[:, here] = high
        wt_lo[:, here] = (weights - high.astype(F32)).astype(BF16)

    assemble1()

    def finish(g, lo, hi):
        panel, base = panels[g], GROUPS[g][0]
        count = hi - lo
        for h, order in enumerate((top, bottom)):
            rows = jnp.concatenate(
                [panel[s, lo - base : hi - base].reshape(count * 64, TILE) for s in order], 1
            )
            rows_hi = rows.astype(BF16)
            rows_lo = (rows - rows_hi.astype(F32)).astype(BF16)
            update = lax.dot_general(rows_hi, wt_hi[...], NTC, preferred_element_type=F32)
            update += lax.dot_general(rows_lo, wt_hi[...], NTC, preferred_element_type=F32)
            update += lax.dot_general(rows_hi, wt_lo[...], NTC, preferred_element_type=F32)
            for t in range(lo, hi):
                piece = update[64 * (t - lo) : 64 * (t - lo + 1)]
                base0, base1 = sum0[t, pl.ds(64 * h, 64), :], sum1[t, pl.ds(64 * h, 64), :]
                new0 = jnp.where(source, 0.0, base0) - piece[:, :TILE]
                new1 = base1 - piece[:, TILE:]
                if t < 4:
                    i = 8 * t + r
                    new0 = jnp.where(i >= c, new0, base0)
                    new1 = jnp.where(i >= 16 + c, new1, base1)
                out[t, pl.ds(128 * h, 64, stride=2), :] = new0
                out[t, pl.ds(128 * h + 1, 64, stride=2), :] = new1

    block = lmat[
        pl.ds(pl.multiple_of(r * TILE, TILE), TILE), pl.ds(pl.multiple_of(lax.rem(c, 8) * TILE, TILE), TILE)
    ]
    factored = jnp.logical_and(source, r >= c)
    out[0, pl.ds(0, TILE, stride=2), :] = jnp.where(factored, block, sum0[0])
    out[0, pl.ds(1, TILE, stride=2), :] = sum1[0]
    s7(e)
    finish(e, 1, 10)
    s7(b)
    finish(b, 10, 17)
    finish(b, 17, 24)

    @pl.when(source)
    def _():
        for step in range(1, 4):
            dx_copy(step).wait_send()
        for g in range(2):
            spread(g).wait_send()

    for kind in range(3):
        for step in STEPS:
            child_copy(kind, step).wait_send()
    for sx in range(2):
        for step in range(1, 4):
            dz_copy(sx, step).wait_send()
    for spec in started:
        move(*spec).wait_send()
    for q in range(3):
        d_end(q)
    bx_end()
    b_end()


def copy_kernel(source, out):
    out[...] = source[...]


def shards(front, child_one, child_two, map_one, map_two, owner_one, owner_two):
    whole = pl.BlockSpec(memory_space=pl.ANY)
    vmem = pl.BlockSpec(memory_space=pltpu.VMEM)
    smem = pl.BlockSpec(memory_space=pltpu.SMEM)
    dma = pltpu.SemaphoreType.DMA

    def space(*shape):
        return pltpu.VMEM(shape, F32)

    out = pl.pallas_call(
        kernel,
        out_shape=jax.ShapeDtypeStruct((NT, 256, TILE), F32),
        in_specs=[whole] * 3 + [smem] * 4,
        out_specs=vmem,
        scratch_shapes=[
            space(NT, 256, TILE), space(8, 256, TILE), space(16, 256, TILE),
            space(8, 2, TILE, TILE), space(8, TILE, TILE), space(8, 3, TILE, TILE),
            space(9, 2, TILE, TILE), space(9, TILE, TILE), space(9, 3, TILE, TILE),
            space(NT, TILE, TILE), space(NT, TILE, TILE),
            *[space(16, hi - lo, 64, TILE) for lo, hi, _ in GROUPS],
            space(8, TILE, TILE), space(8, 8, TILE, TILE), space(2, 8, TILE, TILE),
            space(TILE, TILE), space(PB * TILE, PB * TILE), space(PB * TILE, PB * TILE),
            space(256, PB * TILE),
            pltpu.VMEM((256, PB * TILE), BF16), pltpu.VMEM((256, PB * TILE), BF16),
            pltpu.SMEM((128,), I32), pltpu.SMEM((32,), I32),
            dma((3,)), dma((3, 7)), dma((3, 7)),
            dma((2,)), dma((2,)), dma((2, 20)), dma((2, 20)),
            dma((3,)), dma((2,)), dma((2, 3)), dma((2, 3)), dma((3, 7)), dma((3, 7)),
            dma((3,)), dma((2, 8)), dma((2, 4)), dma((2, 4)),
        ],
        compiler_params=pltpu.CompilerParams(
            collective_id=0, has_side_effects=True, vmem_limit_bytes=60 * 2**20
        ),
    )(
        front.reshape(NT, 256, TILE),
        child_one.reshape(8, 256, TILE),
        child_two.reshape(16, 256, TILE),
        map_one, map_two, owner_one, owner_two,
    )
    block = pl.BlockSpec((4, 256, TILE), lambda i: (i, 0, 0))
    out = pl.pallas_call(
        copy_kernel,
        grid=(6,),
        out_shape=jax.ShapeDtypeStruct((NT, 256, TILE), F32),
        in_specs=[block],
        out_specs=block,
        compiler_params=pltpu.CompilerParams(vmem_limit_bytes=60 * 2**20),
    )(out)
    return out.reshape(front.shape)


def solution(mesh):
    placed = P(None, "row", None, None, "col", None)
    return jax.shard_map(
        shards,
        mesh=mesh,
        in_specs=(placed, placed, placed, P(), P(), P(), P()),
        out_specs=placed,
        check_vma=False,
    )
```

```python
import functools

import jax
import jax.numpy as jnp
from jax import lax
from jax.experimental import pallas as pl
from jax.experimental.pallas import tpu as pltpu
from jax.sharding import PartitionSpec as P

F32, BF16, I32 = jnp.float32, jnp.bfloat16, jnp.int32
HIGHEST = lax.Precision.HIGHEST
MESH = pl.DeviceIdType.MESH
TILE, PB, NT = 128, 8, 24
LEAF = 16
NN = (((1,), (0,)), ((), ()))
NTC = (((1,), (1,)), ((), ()))
TN = (((0,), (0,)), ((), ()))
GROUPS = ((1, 9, True), (9, 18, False), (18, 24, True))
CHUNKS = ((0, 1), (1, 4), (4, 8))
STEPS = (1, 7, 2, 6, 3, 5, 4)


def dot(a, b, dims):
    return lax.dot_general(a, b, dims, precision=HIGHEST, preferred_element_type=F32)


def split3(v):
    high = v.astype(BF16)
    rest = v - high.astype(F32)
    middle = rest.astype(BF16)
    low = (rest - middle.astype(F32)).astype(BF16)
    return [part.astype(F32) for part in (high, middle, low)]


def rank_update(a, b):
    ah, am, al = split3(a)
    bh, bm, bl = split3(b)
    left = jnp.concatenate([ah, ah, am, ah, am, al], 0).astype(BF16)
    right = jnp.concatenate([bl, bm, bm, bh, bh, bh], 0).astype(BF16)
    return lax.dot_general(left, right, TN, preferred_element_type=F32)


def leaf(rows_u, rows_v, offset):
    count = rows_u.shape[0]
    index = lax.broadcasted_iota(I32, (count, TILE), 0)
    cols = [
        jnp.broadcast_to(rows_u[:, offset + k : offset + k + 1], (count, TILE)) for k in range(count)
    ]
    scale = jnp.zeros((count, TILE), F32)
    for j in range(count):
        pivot = cols[j][j : j + 1, :]
        scale = jnp.where(index == j, lax.rsqrt(pivot), scale)
        if j + 1 < count:
            ratio = cols[j] * (1.0 / pivot)
            for k in range(j + 1, count):
                cols[k] = cols[k] - ratio * cols[k][j : j + 1, :]
            ratio = jnp.where(index > j, ratio, 0.0)
            rows_u = rows_u - ratio * rows_u[j : j + 1, :]
            rows_v = rows_v - ratio * rows_v[j : j + 1, :]
    return rows_u * scale, rows_v * scale


def factor_tile(square):
    row = lax.broadcasted_iota(I32, (TILE, TILE), 0)
    col = lax.broadcasted_iota(I32, (TILE, TILE), 1)
    unit = jnp.where(row == col, 1.0, 0.0).astype(F32)
    count = TILE // LEAF
    left = [square[i * LEAF : (i + 1) * LEAF] for i in range(count)]
    right = [unit[i * LEAF : (i + 1) * LEAF] for i in range(count)]
    for b in range(count):
        left[b], right[b] = leaf(left[b], right[b], b * LEAF)
        if b + 1 < count:
            change = rank_update(left[b], jnp.concatenate([left[b], right[b]], 1))
            for i in range(b + 1, count):
                left[i] = left[i] - change[i * LEAF : (i + 1) * LEAF, :TILE]
                right[i] = right[i] - change[i * LEAF : (i + 1) * LEAF, TILE:]
    upper = jnp.where(col >= row, jnp.concatenate(left, 0), 0.0)
    inverse = jnp.where(col <= row, jnp.concatenate(right, 0), 0.0)
    return upper, inverse


def partner_slot(c):
    return 12 - 4 * (c // 4) + c % 4


def kernel(
    front_in, one_in, two_in, map_one, map_two, own_one, own_two, out_any,
    front, one, two, stage0, stage2, stage1, got0, got2, got1, sum0, sum1,
    panel_a, panel_b, panel_c, dplane, drows, brows, diag, lmat, inv, half, wt_hi, wt_lo, out,
    slots, table,
    load, child_send, child_recv, spread_send, spread_recv, ring_send, ring_recv,
    dx_send, dx_recv, dz_send, dz_recv, d_send, d_recv, bx_send, bx_recv, b_send, b_recv, stored,
):
    r, c = lax.axis_index("row"), lax.axis_index("col")
    y, core = r // 2, r % 2
    x, z = c // 4, c % 4
    source = x < 2
    other = jnp.logical_not(source)
    partner = (3 - x) * 4 + z
    panels = (panel_a, panel_b, panel_c)

    def at_col(dx, dz):
        return lax.rem(x + dx + 4, 4) * 4 + lax.rem(z + dz + 4, 4)

    def row_peer(step):
        return lax.rem(r + step, 8)

    def y_peer(step, across=0):
        return lax.rem(y + step, 4) * 2 + (core if across == 0 else 1 - core)

    barrier = pltpu.get_barrier_semaphore()
    for step in range(1, 8):
        pl.semaphore_signal(barrier, inc=1, device_id=(row_peer(step), c), device_id_type=MESH)
    for step in range(1, 4):
        pl.semaphore_signal(barrier, inc=1, device_id=(r, at_col(step, 0)), device_id_type=MESH)
        pl.semaphore_signal(barrier, inc=1, device_id=(r, at_col(0, step)), device_id_type=MESH)

    @pl.when(lax.rem(c, 8) == r)
    def _():
        for held in range(8):

            @pl.when(c != held)
            def _():
                pl.semaphore_signal(barrier, inc=1, device_id=(r, held), device_id_type=MESH)

    loads = [
        pltpu.make_async_copy(a, b, load.at[i])
        for i, (a, b) in enumerate(((one_in, one), (two_in, two), (front_in, front)))
    ]
    for copy in loads:
        copy.start()

    def find_one(g, carry):
        seen, picks = carry[0], list(carry[1:])
        for v in range(8):
            mine = own_one[8 * g + v] == r
            picks[v] = jnp.where(mine, seen, picks[v])
            seen = seen + mine.astype(I32)
        return (seen, *picks)

    picks_one = lax.fori_loop(0, 8, find_one, (jnp.int32(0),) * 9)[1:]

    def find_two(g, carry):
        seen, first, second = carry[0], list(carry[1:9]), list(carry[9:])
        for v in range(8):
            mine = own_two[8 * g + v] == r
            first[v] = jnp.where(mine, second[v], first[v])
            second[v] = jnp.where(mine, seen, second[v])
            seen = seen + mine.astype(I32)
        return (seen, *first, *second)

    picks_two = lax.fori_loop(0, 16, find_two, (jnp.int32(0),) * 17)[1:]
    for v in range(8):
        slots[v] = jnp.minimum(picks_one[v], 7)
        slots[8 + v] = jnp.minimum(picks_two[v], 15)
        slots[16 + v] = jnp.minimum(picks_two[8 + v], 15)

    def stage0_rows(v, carry):
        pick = pl.ds(0, TILE, stride=2)
        stage0[v, 0] = one[slots[v], pick, :]
        stage0[v, 1] = two[slots[8 + v], pick, :]
        stage2[v] = two[slots[16 + v], pick, :]
        return carry

    def stage1_rows(v, carry):
        pick = pl.ds(1, TILE, stride=2)
        stage1[v, 0] = one[slots[v], pick, :]
        stage1[v, 1] = two[slots[8 + v], pick, :]
        stage1[v, 2] = two[slots[16 + v], pick, :]
        return carry

    def child_copy(kind, step):
        peer = row_peer(step)
        return pltpu.make_async_remote_copy(
            src_ref=(stage0, stage1, stage2)[kind].at[peer],
            dst_ref=(got0, got1, got2)[kind].at[r],
            send_sem=child_send.at[kind, step - 1],
            recv_sem=child_recv.at[kind, step - 1],
            device_id=(peer, c),
            device_id_type=MESH,
        )

    loads[0].wait()
    loads[1].wait()
    lax.fori_loop(0, 8, stage0_rows, 0)
    pl.semaphore_wait(
        barrier, 13 + source.astype(I32) + jnp.logical_and(source, c != r).astype(I32)
    )
    for kind in (0, 2):
        for step in STEPS:
            child_copy(kind, step).start()
    lax.fori_loop(0, 8, stage1_rows, 0)
    for buffer, staged in ((got0, stage0), (got1, stage1), (got2, stage2)):
        buffer[r] = staged[r]
        buffer[8] = jnp.zeros(buffer.shape[1:], F32)

    sources = [own_two[8 * g + r] for g in range(16)]
    for g in range(16):
        rank = jnp.int32(0)
        for h in range(g):
            rank = rank + (sources[h] == sources[g]).astype(I32)
        table[g] = jnp.clip(sources[g], 0, 7)
        table[16 + g] = jnp.minimum(rank, 1)

    def find_targets(t, carry):
        at_one, at_two = carry
        hit_one = map_one[8 * at_one] // 8 == t
        hit_two = map_two[8 * at_two] // 8 == t
        slots[32 + t] = jnp.where(hit_one, jnp.clip(own_one[8 * at_one + r], 0, 7), 8)
        slots[64 + t] = jnp.where(hit_two, table[at_two], 8)
        slots[96 + t] = jnp.where(hit_two, table[16 + at_two] + 1, 1)
        return (
            jnp.minimum(at_one + hit_one.astype(I32), 7),
            jnp.minimum(at_two + hit_two.astype(I32), 15),
        )

    lax.fori_loop(0, NT, find_targets, (jnp.int32(0), jnp.int32(0)))
    loads[2].wait()

    def assemble0():
        for step in STEPS:
            child_copy(2, step).wait_recv()

        def body(t, carry):
            origin, second = slots[64 + t], slots[96 + t] == 2
            total = front[t, pl.ds(0, TILE, stride=2), :] + got0[slots[32 + t], 0]
            total = total + got0[jnp.where(second, 8, origin), 1]
            sum0[t] = total + got2[jnp.where(second, origin, 8)]
            return carry

        lax.fori_loop(0, NT, body, 0)

    def assemble1():
        for step in STEPS:
            child_copy(1, step).wait_recv()

        def body(t, carry):
            sum1[t] = (
                front[t, pl.ds(1, TILE, stride=2), :] + got1[slots[32 + t], 0]
            ) + got1[slots[64 + t], slots[96 + t]]
            return carry

        lax.fori_loop(0, NT, body, 0)

    def dx_copy(step):
        held = lax.rem(c, 8)
        return pltpu.make_async_remote_copy(
            src_ref=dplane.at[held],
            dst_ref=dplane.at[held],
            send_sem=dx_send.at[step - 1],
            recv_sem=dx_recv.at[lax.rem(x, 2)],
            device_id=(r, at_col(step, 0)),
            device_id_type=MESH,
        )

    def dx_arrival(sx):
        held = 4 * sx + z
        return pltpu.make_async_remote_copy(
            src_ref=dplane.at[held],
            dst_ref=dplane.at[held],
            send_sem=dx_send.at[0],
            recv_sem=dx_recv.at[sx],
            device_id=(r, at_col(1, 0)),
            device_id_type=MESH,
        )

    def dz_copy(sx, step, back=0):
        held = 4 * sx + lax.rem(z + 4 - back, 4)
        return pltpu.make_async_remote_copy(
            src_ref=dplane.at[held],
            dst_ref=dplane.at[held],
            send_sem=dz_send.at[sx, step - 1],
            recv_sem=dz_recv.at[sx, step - 1],
            device_id=(r, at_col(0, step)),
            device_id_type=MESH,
        )

    for step in STEPS:
        child_copy(0, step).wait_recv()

    @pl.when(source)
    def _():
        total = front[0, pl.ds(0, TILE, stride=2), :] + got0[jnp.clip(own_one[r], 0, 7), 0]
        dplane[lax.rem(c, 8)] = total + got0[jnp.clip(own_two[r], 0, 7), 1]
        for step in (1, 3, 2):
            dx_copy(step).start()

    for sx in range(2):

        @pl.when(x != sx)
        def _():
            dx_arrival(sx).wait_recv()

        for step in (1, 3, 2):
            dz_copy(sx, step).start()
    def d_out(q, step):
        lo, hi = CHUNKS[q]
        return pltpu.make_async_remote_copy(
            src_ref=dplane.at[pl.ds(lo, hi - lo)],
            dst_ref=drows.at[r, pl.ds(lo, hi - lo)],
            send_sem=d_send.at[q, step - 1],
            recv_sem=d_recv.at[q, step - 1],
            device_id=(y_peer(step), c),
            device_id_type=MESH,
        )

    def d_pair(q, step):
        lo, hi = CHUNKS[q]
        held = y_peer(step)
        return pltpu.make_async_remote_copy(
            src_ref=dplane.at[pl.ds(lo, hi - lo)] if step == 0 else drows.at[held, pl.ds(lo, hi - lo)],
            dst_ref=drows.at[held, pl.ds(lo, hi - lo)],
            send_sem=d_send.at[q, 3 + step],
            recv_sem=d_recv.at[q, 3 + step],
            device_id=(y_peer(0, 1), c),
            device_id_type=MESH,
        )

    def d_start(q):
        @pl.when(r >= CHUNKS[q][0])
        def _():
            for step in (1, 3, 2):
                d_out(q, step).start()
            d_pair(q, 0).start()

    def d_relay(q):
        for step in (1, 3, 2):

            @pl.when(y_peer(4 - step) >= CHUNKS[q][0])
            def _():
                d_out(q, step).wait_recv()
                d_pair(q, 4 - step).start()

    def d_wait(q):
        for step in range(4):

            @pl.when(y_peer(step, 1) >= CHUNKS[q][0])
            def _():
                d_pair(q, step).wait_recv()

    def d_end(q):
        @pl.when(r >= CHUNKS[q][0])
        def _():
            for step in (1, 3, 2):
                d_out(q, step).wait_send()
            d_pair(q, 0).wait_send()

        for step in (1, 3, 2):

            @pl.when(y_peer(4 - step) >= CHUNKS[q][0])
            def _():
                d_pair(q, 4 - step).wait_send()

    for sx in range(2):
        for step in (1, 3, 2):
            dz_copy(sx, step, step).wait_recv()
    d_start(0)
    drows[r] = dplane[...]
    assemble0()

    @pl.when(source)
    def _():
        for g in range(3):
            lo, hi, _ = GROUPS[g]
            panels[g][c] = sum0[lo:hi, :64, :]

    def spread(g):
        lo, hi, _ = GROUPS[g]
        return pltpu.make_async_remote_copy(
            src_ref=sum0.at[pl.ds(lo, hi - lo), pl.ds(64, 64)],
            dst_ref=panels[g].at[partner],
            send_sem=spread_send.at[g],
            recv_sem=spread_recv.at[g],
            device_id=(r, partner),
            device_id_type=MESH,
        )

    def part(slot, g, half):
        lo, hi, _ = GROUPS[g]
        count, panel = hi - lo, panels[g]
        upper = (count + 1) // 2
        if half is None:
            return panel.at[slot]
        return panel.at[slot, pl.ds(0, upper)] if half == 0 else panel.at[slot, pl.ds(upper, count - upper)]

    def move(g, axis, da, db, direction, half, index):
        x_first = GROUPS[g][2]
        offset = (da, db) if x_first else (db, da)
        along = (direction, 0) if (axis == 0) == x_first else (0, direction)
        ref = part(at_col(*offset), g, half)
        return pltpu.make_async_remote_copy(
            src_ref=ref,
            dst_ref=ref,
            send_sem=ring_send.at[g, index],
            recv_sem=ring_recv.at[g, index],
            device_id=(r, at_col(*along)),
            device_id_type=MESH,
        )

    def wait(spec):
        g, axis, da, db, direction, half, index = spec
        back = (da - direction, db) if axis == 0 else (da, db - direction)
        move(g, axis, back[0], back[1], direction, half, index).wait_recv()

    def first(g, k):
        return (g, 0, 0, 0, (1, -1)[k], None, k)

    def first_on(g, k):
        return (g, 0, (-1, 1)[k], 0, (1, -1)[k], k, 2 + k)

    def second(g, q, k):
        return (g, 1, (0, -1, 1, 2)[q], 0, (1, -1)[k], None, 4 + 4 * q + k)

    def second_on(g, q, k):
        return (g, 1, (0, -1, 1, 2)[q], (-1, 1)[k], (1, -1)[k], k, 6 + 4 * q + k)

    started = []

    def start(spec):
        started.append(spec)
        move(*spec).start()

    def own_blocks(g):
        return [first(g, 0), first(g, 1), second(g, 0, 0), second(g, 0, 1)]

    def s1(g):
        @pl.when(other)
        def _():
            spread(g).wait_recv()
            for spec in own_blocks(g):
                move(*spec).start()

    def s2(g):
        for k in range(2):
            wait(first(g, k))
            start(first_on(g, k))
        for q in (1, 2):
            for k in range(2):
                start(second(g, q, k))

    def s3(g):
        for k in range(2):
            wait(second(g, 0, k))
            start(second_on(g, 0, k))

    def s4(g):
        for k in range(2):
            wait(first_on(g, k))
        for k in range(2):
            start(second(g, 3, k))

    def s5a(g):
        for k in range(2):
            wait(second(g, 1, k))
            start(second_on(g, 1, k))

    def s5b(g):
        for k in range(2):
            wait(second(g, 2, k))
            start(second_on(g, 2, k))

    def s6(g):
        for k in range(2):
            wait(second(g, 3, k))
            start(second_on(g, 3, k))

    def s7(g):
        for q in range(4):
            for k in range(2):
                wait(second_on(g, q, k))

    b_row = lax.rem(c, 8)
    b_y, b_core = b_row // 2, b_row % 2
    b_root, b_even = r == b_row, core == b_core

    def bx_copy(q, t, target):
        held = lax.rem(c, 8)
        return pltpu.make_async_remote_copy(
            src_ref=sum0.at[t],
            dst_ref=brows.at[q, held],
            send_sem=bx_send.at[t - 1],
            recv_sem=bx_recv.at[q, held],
            device_id=(r, target),
            device_id_type=MESH,
        )

    def bx_arrival(q, held):
        return pltpu.make_async_remote_copy(
            src_ref=sum0.at[1],
            dst_ref=brows.at[q, held],
            send_sem=bx_send.at[0],
            recv_sem=bx_recv.at[q, held],
            device_id=(r, at_col(1, 0)),
            device_id_type=MESH,
        )

    def bx_start():
        @pl.when(source)
        def _():
            bx_copy(0, 1, r + 8).start()
            bx_copy(1, 3, r + 8).start()

        @pl.when(jnp.logical_and(source, c != r))
        def _():
            bx_copy(1, 2, r).start()

        @pl.when(jnp.logical_and(source, c == r))
        def _():
            brows[1, r] = sum0[2]

    def bx_end():
        @pl.when(source)
        def _():
            bx_copy(0, 1, r + 8).wait_send()
            bx_copy(1, 3, r + 8).wait_send()

        @pl.when(jnp.logical_and(source, c != r))
        def _():
            bx_copy(1, 2, r).wait_send()

    def b_out(q, step):
        return pltpu.make_async_remote_copy(
            src_ref=brows.at[q],
            dst_ref=brows.at[q],
            send_sem=b_send.at[q, step - 1],
            recv_sem=b_recv.at[q, step - 1],
            device_id=(y_peer(step), c),
            device_id_type=MESH,
        )

    def b_pair(q):
        return pltpu.make_async_remote_copy(
            src_ref=brows.at[q],
            dst_ref=brows.at[q],
            send_sem=b_send.at[q, 3],
            recv_sem=b_recv.at[q, 3],
            device_id=(y_peer(0, 1), c),
            device_id_type=MESH,
        )

    def with_b(q, condition):
        return condition if q == 1 else jnp.logical_and(condition, other)

    def b_start(_):
        for q in (1, 0):

            @pl.when(with_b(q, b_root))
            def _():
                for held in range(8):

                    @pl.when(c != held)
                    def _():
                        bx_arrival(q, held).wait_recv()

                for step in (1, 3, 2):
                    b_out(q, step).start()
                b_pair(q).start()

    def b_relay(_):
        for q in (1, 0):
            for step in (1, 2, 3):

                @pl.when(with_b(q, jnp.logical_and(b_even, lax.rem(b_y + step, 4) == y)))
                def _():
                    b_out(q, step).wait_recv()
                    b_pair(q).start()

    def b_wait():
        for q in (1, 0):

            @pl.when(with_b(q, jnp.logical_not(b_even)))
            def _():
                b_pair(q).wait_recv()

    def b_end():
        for q in (1, 0):

            @pl.when(with_b(q, b_root))
            def _():
                for step in (1, 2, 3):
                    b_out(q, step).wait_send()

            @pl.when(with_b(q, b_even))
            def _():
                b_pair(q).wait_send()

    def child1(_):
        for step in STEPS:
            child_copy(1, step).start()

    bx_start()
    for g in range(3):

        @pl.when(source)
        def _():
            spread(g).start()

    for g in range(3):
        started.extend(own_blocks(g))

        @pl.when(source)
        def _():
            for spec in own_blocks(g):
                move(*spec).start()

    d_relay(0)
    d_start(1)
    d_wait(0)

    row = lax.broadcasted_iota(I32, (TILE, TILE), 0)
    col = lax.broadcasted_iota(I32, (TILE, TILE), 1)
    inv[...] = jnp.zeros_like(inv)

    b, e, f = 0, 1, 2
    before = {
        0: [(s1, b)],
        1: [(s1, f)],
        2: [(s2, b), (d_relay, 2)],
        3: [(d_wait, 2)],
        4: [(s5a, b), (s2, f)],
        5: [(s3, f), (b_relay, 0)],
        6: [(s5b, e), (s5b, b)],
        7: [(s4, f), (s6, b), (s5a, e)],
    }
    after = {
        0: [(d_relay, 1), (d_wait, 1), (d_start, 2), (s1, e)],
        1: [(b_start, 0)],
        2: [],
        3: [(s2, e), (s3, b), (child1, 0)],
        4: [(s4, b)],
        5: [(s4, e)],
        6: [(s3, e)],
        7: [(s6, e)],
    }

    def step_tile(k, carry):
        for j in range(PB):

            @pl.when(k == j)
            def _():
                for act, g in before[j]:
                    act(g)
                here = pl.ds(j * TILE, TILE)
                square = drows[j, j]
                square = jnp.where(row >= col, square, 0.0) + jnp.where(row > col, square, 0.0).T
                below = [drows[i, j] for i in range(j + 1, PB)]
                if j == 0:
                    diag[...] = square
                    lmat[TILE:, here] = jnp.concatenate(below, 0)
                else:
                    done = pl.ds(0, j * TILE)
                    left = lmat[here, done]
                    diag[...] = square - dot(left, left, NTC)
                    if below:
                        under = pl.ds((j + 1) * TILE, (PB - 1 - j) * TILE)
                        lmat[under, here] = jnp.concatenate(below, 0) - dot(lmat[under, done], left, NTC)
                    inv[here, done] = dot(left, inv[done, done], NN)

        upper, inverse = factor_tile(diag[...])
        diag[...] = inverse
        lmat_here = upper.T
        for j in range(PB):

            @pl.when(k == j)
            def _():
                here = pl.ds(j * TILE, TILE)
                inverse = diag[...]
                lmat[here, here] = lmat_here
                if j > 0:
                    done = pl.ds(0, j * TILE)
                    inv[here, done] = -dot(inverse, inv[here, done], NN)
                inv[here, here] = inverse
                if j + 1 < PB:
                    under = pl.ds((j + 1) * TILE, (PB - 1 - j) * TILE)
                    lmat[under, here] = dot(lmat[under, here], inverse, NTC)
                for act, g in after[j]:
                    act(g)

        return carry

    lax.fori_loop(0, PB, step_tile, 0)
    b_wait()

    top, bottom = list(range(8)), [partner_slot(k) for k in range(8)]
    unused = jnp.zeros((TILE, TILE), F32)
    mine = jnp.concatenate(
        [
            jnp.concatenate([jnp.where(source, unused, brows[0, s]) for s in range(8)], 1),
            jnp.concatenate([brows[1, s] for s in range(8)], 1),
        ],
        0,
    )
    for k in range(4):
        here, upto = pl.ds(256 * k, 256), 256 * (k + 1)
        half[:, here] = dot(mine[:, :upto], inv[here, :upto], NTC)
    s5a(f)
    s5b(f)
    own = inv.at[pl.ds(pl.multiple_of(lax.rem(c, 8) * TILE, TILE), TILE)]
    for k in range(4):
        here, rest = pl.ds(256 * k, 256), pl.ds(256 * k, 1024 - 256 * k)
        weights = dot(half[:, rest], inv[rest, here], NN)
        weights = jnp.concatenate([jnp.where(source, -own[:, here], weights[:TILE]), weights[TILE:]], 0)
        high = weights.astype(BF16)
        wt_hi[:, here] = high
        wt_lo[:, here] = (weights - high.astype(F32)).astype(BF16)

    s6(f)
    assemble1()

    def finish(g, lo, hi):
        panel, base = panels[g], GROUPS[g][0]
        count = hi - lo
        for h, order in enumerate((top, bottom)):
            rows = jnp.concatenate(
                [panel[s, lo - base : hi - base].reshape(count * 64, TILE) for s in order], 1
            )
            rows_hi = rows.astype(BF16)
            rows_lo = (rows - rows_hi.astype(F32)).astype(BF16)
            update = lax.dot_general(rows_hi, wt_hi[...], NTC, preferred_element_type=F32)
            update += lax.dot_general(rows_lo, wt_hi[...], NTC, preferred_element_type=F32)
            update += lax.dot_general(rows_hi, wt_lo[...], NTC, preferred_element_type=F32)
            for t in range(lo, hi):
                piece = update[64 * (t - lo) : 64 * (t - lo + 1)]
                base0, base1 = sum0[t, pl.ds(64 * h, 64), :], sum1[t, pl.ds(64 * h, 64), :]
                new0 = jnp.where(source, 0.0, base0) - piece[:, :TILE]
                new1 = base1 - piece[:, TILE:]
                if t < 4:
                    i = 8 * t + r
                    new0 = jnp.where(i >= c, new0, base0)
                    new1 = jnp.where(i >= 16 + c, new1, base1)
                out[t, pl.ds(128 * h, 64, stride=2), :] = new0
                out[t, pl.ds(128 * h + 1, 64, stride=2), :] = new1

    def store(piece, lo, hi):
        return pltpu.make_async_copy(
            out.at[pl.ds(lo, hi - lo)], out_any.at[pl.ds(lo, hi - lo)], stored.at[piece]
        )

    block = lmat[
        pl.ds(pl.multiple_of(r * TILE, TILE), TILE), pl.ds(pl.multiple_of(lax.rem(c, 8) * TILE, TILE), TILE)
    ]
    factored = jnp.logical_and(source, r >= c)
    out[0, pl.ds(0, TILE, stride=2), :] = jnp.where(factored, block, sum0[0])
    out[0, pl.ds(1, TILE, stride=2), :] = sum1[0]
    store(0, 0, 1).start()
    for g, (lo, hi, _) in enumerate(GROUPS):
        s7(g)
        finish(g, lo, hi)
        store(1 + g, lo, hi).start()

    @pl.when(source)
    def _():
        for step in range(1, 4):
            dx_copy(step).wait_send()
        for g in range(3):
            spread(g).wait_send()

    for kind in range(3):
        for step in STEPS:
            child_copy(kind, step).wait_send()
    for sx in range(2):
        for step in range(1, 4):
            dz_copy(sx, step).wait_send()
    for spec in started:
        move(*spec).wait_send()
    for q in range(3):
        d_end(q)
    bx_end()
    b_end()
    store(0, 0, 1).wait()
    for g, (lo, hi, _) in enumerate(GROUPS):
        store(1 + g, lo, hi).wait()


def copy_kernel(source, out, buffer, load, store):
    parts = [pl.ds(6 * i, 6) for i in range(4)]
    loads = [pltpu.make_async_copy(source.at[p], buffer.at[p], load.at[i]) for i, p in enumerate(parts)]
    stores = [pltpu.make_async_copy(buffer.at[p], out.at[p], store.at[i]) for i, p in enumerate(parts)]
    for copy in loads:
        copy.start()
    for first, second in zip(loads, stores):
        first.wait()
        second.start()
    for copy in stores:
        copy.wait()


def shards(front, child_one, child_two, map_one, map_two, owner_one, owner_two):
    whole = pl.BlockSpec(memory_space=pl.ANY)
    smem = pl.BlockSpec(memory_space=pltpu.SMEM)
    dma = pltpu.SemaphoreType.DMA

    def space(*shape):
        return pltpu.VMEM(shape, F32)

    out = pl.pallas_call(
        kernel,
        out_shape=jax.ShapeDtypeStruct((NT, 256, TILE), F32),
        in_specs=[whole] * 3 + [smem] * 4,
        out_specs=whole,
        scratch_shapes=[
            space(NT, 256, TILE), space(8, 256, TILE), space(16, 256, TILE),
            space(8, 2, TILE, TILE), space(8, TILE, TILE), space(8, 3, TILE, TILE),
            space(9, 2, TILE, TILE), space(9, TILE, TILE), space(9, 3, TILE, TILE),
            space(NT, TILE, TILE), space(NT, TILE, TILE),
            *[space(16, hi - lo, 64, TILE) for lo, hi, _ in GROUPS],
            space(8, TILE, TILE), space(8, 8, TILE, TILE), space(2, 8, TILE, TILE),
            space(TILE, TILE), space(PB * TILE, PB * TILE), space(PB * TILE, PB * TILE),
            space(256, PB * TILE),
            pltpu.VMEM((256, PB * TILE), BF16), pltpu.VMEM((256, PB * TILE), BF16),
            space(NT, 256, TILE),
            pltpu.SMEM((128,), I32), pltpu.SMEM((32,), I32),
            dma((3,)), dma((3, 7)), dma((3, 7)),
            dma((3,)), dma((3,)), dma((3, 20)), dma((3, 20)),
            dma((3,)), dma((2,)), dma((2, 3)), dma((2, 3)), dma((3, 7)), dma((3, 7)),
            dma((3,)), dma((2, 8)), dma((2, 4)), dma((2, 4)), dma((4,)),
        ],
        compiler_params=pltpu.CompilerParams(
            collective_id=0, has_side_effects=True, vmem_limit_bytes=60 * 2**20
        ),
    )(
        front.reshape(NT, 256, TILE),
        child_one.reshape(8, 256, TILE),
        child_two.reshape(16, 256, TILE),
        map_one, map_two, owner_one, owner_two,
    )
    out = pl.pallas_call(
        copy_kernel,
        out_shape=jax.ShapeDtypeStruct((NT, 256, TILE), F32),
        in_specs=[whole],
        out_specs=whole,
        scratch_shapes=[space(NT, 256, TILE), dma((4,)), dma((4,))],
        compiler_params=pltpu.CompilerParams(vmem_limit_bytes=60 * 2**20),
    )(out)
    return out.reshape(front.shape)


def solution(mesh):
    placed = P(None, "row", None, None, "col", None)
    return jax.shard_map(
        shards,
        mesh=mesh,
        in_specs=(placed, placed, placed, P(), P(), P(), P()),
        out_specs=placed,
        check_vma=False,
    )
```

```python
import functools

import jax
import jax.numpy as jnp
from jax import lax
from jax.experimental import pallas as pl
from jax.experimental.pallas import tpu as pltpu
from jax.sharding import PartitionSpec as P

F32, BF16, I32 = jnp.float32, jnp.bfloat16, jnp.int32
HIGHEST = lax.Precision.HIGHEST
MESH = pl.DeviceIdType.MESH
TILE, PB, NT = 128, 8, 24
LEAF = 16
NN = (((1,), (0,)), ((), ()))
NTC = (((1,), (1,)), ((), ()))
TN = (((0,), (0,)), ((), ()))
GROUPS = ((1, 9, True), (9, 18, False), (18, 24, True))
CHUNKS = ((0, 1), (1, 2), (2, 4), (4, 8))
STEPS = (1, 7, 2, 6, 3, 5, 4)


def dot(a, b, dims):
    return lax.dot_general(a, b, dims, precision=HIGHEST, preferred_element_type=F32)


def split3(v):
    high = v.astype(BF16)
    rest = v - high.astype(F32)
    middle = rest.astype(BF16)
    low = (rest - middle.astype(F32)).astype(BF16)
    return [part.astype(F32) for part in (high, middle, low)]


def rank_update(a, b):
    ah, am, al = split3(a)
    bh, bm, bl = split3(b)
    left = jnp.concatenate([ah, ah, am, ah, am, al], 0).astype(BF16)
    right = jnp.concatenate([bl, bm, bm, bh, bh, bh], 0).astype(BF16)
    return lax.dot_general(left, right, TN, preferred_element_type=F32)


def leaf(rows_u, rows_v, offset):
    count = rows_u.shape[0]
    index = lax.broadcasted_iota(I32, (count, TILE), 0)
    cols = [
        jnp.broadcast_to(rows_u[:, offset + k : offset + k + 1], (count, TILE)) for k in range(count)
    ]
    scale = jnp.zeros((count, TILE), F32)
    for j in range(count):
        pivot = cols[j][j : j + 1, :]
        scale = jnp.where(index == j, lax.rsqrt(pivot), scale)
        if j + 1 < count:
            ratio = cols[j] * (1.0 / pivot)
            for k in range(j + 1, count):
                cols[k] = cols[k] - ratio * cols[k][j : j + 1, :]
            ratio = jnp.where(index > j, ratio, 0.0)
            rows_u = rows_u - ratio * rows_u[j : j + 1, :]
            rows_v = rows_v - ratio * rows_v[j : j + 1, :]
    return rows_u * scale, rows_v * scale


def factor_tile(square):
    row = lax.broadcasted_iota(I32, (TILE, TILE), 0)
    col = lax.broadcasted_iota(I32, (TILE, TILE), 1)
    unit = jnp.where(row == col, 1.0, 0.0).astype(F32)
    count = TILE // LEAF
    left = [square[i * LEAF : (i + 1) * LEAF] for i in range(count)]
    right = [unit[i * LEAF : (i + 1) * LEAF] for i in range(count)]
    for b in range(count):
        left[b], right[b] = leaf(left[b], right[b], b * LEAF)
        if b + 1 < count:
            change = rank_update(left[b], jnp.concatenate([left[b], right[b]], 1))
            for i in range(b + 1, count):
                left[i] = left[i] - change[i * LEAF : (i + 1) * LEAF, :TILE]
                right[i] = right[i] - change[i * LEAF : (i + 1) * LEAF, TILE:]
    upper = jnp.where(col >= row, jnp.concatenate(left, 0), 0.0)
    inverse = jnp.where(col <= row, jnp.concatenate(right, 0), 0.0)
    return upper, inverse


def partner_slot(c):
    return 12 - 4 * (c // 4) + c % 4


def kernel(
    front_in, one_in, two_in, map_one, map_two, own_one, own_two, out_any,
    front, one, two, stage0, stage2, stage1, got0, got2, got1, sum0, sum1,
    panel_a, panel_b, panel_c, dplane, drows, brows, lmat, inv, half, wt_hi, wt_lo, out,
    slots, table,
    load, child_send, child_recv, spread_send, spread_recv, ring_send, ring_recv,
    dx_send, dx_recv, dz_send, dz_recv, d_send, d_recv, bx_send, bx_recv, b_send, b_recv, stored,
):
    r, c = lax.axis_index("row"), lax.axis_index("col")
    y, core = r // 2, r % 2
    x, z = c // 4, c % 4
    source = x < 2
    other = jnp.logical_not(source)
    partner = (3 - x) * 4 + z
    panels = (panel_a, panel_b, panel_c)

    def at_col(dx, dz):
        return lax.rem(x + dx + 4, 4) * 4 + lax.rem(z + dz + 4, 4)

    def row_peer(step):
        return lax.rem(r + step, 8)

    def y_peer(step, across=0):
        return lax.rem(y + step, 4) * 2 + (core if across == 0 else 1 - core)

    barrier = pltpu.get_barrier_semaphore()
    for step in range(1, 8):
        pl.semaphore_signal(barrier, inc=1, device_id=(row_peer(step), c), device_id_type=MESH)
    for step in range(1, 4):
        pl.semaphore_signal(barrier, inc=1, device_id=(r, at_col(step, 0)), device_id_type=MESH)
        pl.semaphore_signal(barrier, inc=1, device_id=(r, at_col(0, step)), device_id_type=MESH)

    @pl.when(lax.rem(c, 8) == r)
    def _():
        for held in range(8):

            @pl.when(c != held)
            def _():
                pl.semaphore_signal(barrier, inc=1, device_id=(r, held), device_id_type=MESH)

    loads = [
        pltpu.make_async_copy(a, b, load.at[i])
        for i, (a, b) in enumerate(((one_in, one), (two_in, two), (front_in, front)))
    ]
    for copy in loads:
        copy.start()

    def find_one(g, carry):
        seen, picks = carry[0], list(carry[1:])
        for v in range(8):
            mine = own_one[8 * g + v] == r
            picks[v] = jnp.where(mine, seen, picks[v])
            seen = seen + mine.astype(I32)
        return (seen, *picks)

    picks_one = lax.fori_loop(0, 8, find_one, (jnp.int32(0),) * 9)[1:]

    def find_two(g, carry):
        seen, first, second = carry[0], list(carry[1:9]), list(carry[9:])
        for v in range(8):
            mine = own_two[8 * g + v] == r
            first[v] = jnp.where(mine, second[v], first[v])
            second[v] = jnp.where(mine, seen, second[v])
            seen = seen + mine.astype(I32)
        return (seen, *first, *second)

    picks_two = lax.fori_loop(0, 16, find_two, (jnp.int32(0),) * 17)[1:]
    for v in range(8):
        slots[v] = jnp.minimum(picks_one[v], 7)
        slots[8 + v] = jnp.minimum(picks_two[v], 15)
        slots[16 + v] = jnp.minimum(picks_two[8 + v], 15)

    def stage0_rows(v, carry):
        pick = pl.ds(0, TILE, stride=2)
        stage0[v, 0] = one[slots[v], pick, :]
        stage0[v, 1] = two[slots[8 + v], pick, :]
        stage2[v] = two[slots[16 + v], pick, :]
        return carry

    def stage1_rows(v, carry):
        pick = pl.ds(1, TILE, stride=2)
        stage1[v, 0] = one[slots[v], pick, :]
        stage1[v, 1] = two[slots[8 + v], pick, :]
        stage1[v, 2] = two[slots[16 + v], pick, :]
        return carry

    def child_copy(kind, step):
        peer = row_peer(step)
        return pltpu.make_async_remote_copy(
            src_ref=(stage0, stage1, stage2)[kind].at[peer],
            dst_ref=(got0, got1, got2)[kind].at[r],
            send_sem=child_send.at[kind, step - 1],
            recv_sem=child_recv.at[kind, step - 1],
            device_id=(peer, c),
            device_id_type=MESH,
        )

    loads[0].wait()
    loads[1].wait()
    lax.fori_loop(0, 8, stage0_rows, 0)
    pl.semaphore_wait(
        barrier, 13 + source.astype(I32) + jnp.logical_and(source, c != r).astype(I32)
    )
    for kind in (0, 2):
        for step in STEPS:
            child_copy(kind, step).start()
    lax.fori_loop(0, 8, stage1_rows, 0)
    for buffer, staged in ((got0, stage0), (got1, stage1), (got2, stage2)):
        buffer[r] = staged[r]
        buffer[8] = jnp.zeros(buffer.shape[1:], F32)

    sources = [own_two[8 * g + r] for g in range(16)]
    for g in range(16):
        rank = jnp.int32(0)
        for h in range(g):
            rank = rank + (sources[h] == sources[g]).astype(I32)
        table[g] = jnp.clip(sources[g], 0, 7)
        table[16 + g] = jnp.minimum(rank, 1)

    def find_targets(t, carry):
        at_one, at_two = carry
        hit_one = map_one[8 * at_one] // 8 == t
        hit_two = map_two[8 * at_two] // 8 == t
        slots[32 + t] = jnp.where(hit_one, jnp.clip(own_one[8 * at_one + r], 0, 7), 8)
        slots[64 + t] = jnp.where(hit_two, table[at_two], 8)
        slots[96 + t] = jnp.where(hit_two, table[16 + at_two] + 1, 1)
        return (
            jnp.minimum(at_one + hit_one.astype(I32), 7),
            jnp.minimum(at_two + hit_two.astype(I32), 15),
        )

    lax.fori_loop(0, NT, find_targets, (jnp.int32(0), jnp.int32(0)))
    loads[2].wait()

    def assemble0():
        for step in STEPS:
            child_copy(2, step).wait_recv()

        def body(t, carry):
            origin, second = slots[64 + t], slots[96 + t] == 2
            total = front[t, pl.ds(0, TILE, stride=2), :] + got0[slots[32 + t], 0]
            total = total + got0[jnp.where(second, 8, origin), 1]
            sum0[t] = total + got2[jnp.where(second, origin, 8)]
            return carry

        lax.fori_loop(0, NT, body, 0)

    def assemble1():
        for step in STEPS:
            child_copy(1, step).wait_recv()

        def body(t, carry):
            sum1[t] = (
                front[t, pl.ds(1, TILE, stride=2), :] + got1[slots[32 + t], 0]
            ) + got1[slots[64 + t], slots[96 + t]]
            return carry

        lax.fori_loop(0, NT, body, 0)

    def dx_copy(step):
        held = lax.rem(c, 8)
        return pltpu.make_async_remote_copy(
            src_ref=dplane.at[held],
            dst_ref=dplane.at[held],
            send_sem=dx_send.at[step - 1],
            recv_sem=dx_recv.at[lax.rem(x, 2)],
            device_id=(r, at_col(step, 0)),
            device_id_type=MESH,
        )

    def dx_arrival(sx):
        held = 4 * sx + z
        return pltpu.make_async_remote_copy(
            src_ref=dplane.at[held],
            dst_ref=dplane.at[held],
            send_sem=dx_send.at[0],
            recv_sem=dx_recv.at[sx],
            device_id=(r, at_col(1, 0)),
            device_id_type=MESH,
        )

    def dz_copy(sx, step, back=0):
        held = 4 * sx + lax.rem(z + 4 - back, 4)
        return pltpu.make_async_remote_copy(
            src_ref=dplane.at[held],
            dst_ref=dplane.at[held],
            send_sem=dz_send.at[sx, step - 1],
            recv_sem=dz_recv.at[sx, step - 1],
            device_id=(r, at_col(0, step)),
            device_id_type=MESH,
        )

    for step in STEPS:
        child_copy(0, step).wait_recv()

    @pl.when(source)
    def _():
        total = front[0, pl.ds(0, TILE, stride=2), :] + got0[jnp.clip(own_one[r], 0, 7), 0]
        dplane[lax.rem(c, 8)] = total + got0[jnp.clip(own_two[r], 0, 7), 1]
        for step in (1, 3, 2):
            dx_copy(step).start()

    for sx in range(2):

        @pl.when(x != sx)
        def _():
            dx_arrival(sx).wait_recv()

        for step in (1, 3, 2):
            dz_copy(sx, step).start()
    def d_out(q, step):
        lo, hi = CHUNKS[q]
        return pltpu.make_async_remote_copy(
            src_ref=dplane.at[pl.ds(lo, hi - lo)],
            dst_ref=drows.at[r, pl.ds(lo, hi - lo)],
            send_sem=d_send.at[q, step - 1],
            recv_sem=d_recv.at[q, step - 1],
            device_id=(y_peer(step), c),
            device_id_type=MESH,
        )

    def d_pair(q, step):
        lo, hi = CHUNKS[q]
        held = y_peer(step)
        return pltpu.make_async_remote_copy(
            src_ref=dplane.at[pl.ds(lo, hi - lo)] if step == 0 else drows.at[held, pl.ds(lo, hi - lo)],
            dst_ref=drows.at[held, pl.ds(lo, hi - lo)],
            send_sem=d_send.at[q, 3 + step],
            recv_sem=d_recv.at[q, 3 + step],
            device_id=(y_peer(0, 1), c),
            device_id_type=MESH,
        )

    def d_start(q):
        @pl.when(r >= CHUNKS[q][0])
        def _():
            for step in (1, 3, 2):
                d_out(q, step).start()
            d_pair(q, 0).start()

    def d_relay(q):
        for step in (1, 3, 2):

            @pl.when(y_peer(4 - step) >= CHUNKS[q][0])
            def _():
                d_out(q, step).wait_recv()
                d_pair(q, 4 - step).start()

    def d_wait(q):
        for step in range(4):

            @pl.when(y_peer(step, 1) >= CHUNKS[q][0])
            def _():
                d_pair(q, step).wait_recv()

    def d_end(q):
        @pl.when(r >= CHUNKS[q][0])
        def _():
            for step in (1, 3, 2):
                d_out(q, step).wait_send()
            d_pair(q, 0).wait_send()

        for step in (1, 3, 2):

            @pl.when(y_peer(4 - step) >= CHUNKS[q][0])
            def _():
                d_pair(q, 4 - step).wait_send()

    assemble0()

    @pl.when(source)
    def _():
        for g in range(3):
            lo, hi, _ = GROUPS[g]
            panels[g][c] = sum0[lo:hi, :64, :]

    def spread(g):
        lo, hi, _ = GROUPS[g]
        return pltpu.make_async_remote_copy(
            src_ref=sum0.at[pl.ds(lo, hi - lo), pl.ds(64, 64)],
            dst_ref=panels[g].at[partner],
            send_sem=spread_send.at[g],
            recv_sem=spread_recv.at[g],
            device_id=(r, partner),
            device_id_type=MESH,
        )

    def part(slot, g, half):
        lo, hi, _ = GROUPS[g]
        count, panel = hi - lo, panels[g]
        upper = (count + 1) // 2
        if half is None:
            return panel.at[slot]
        return panel.at[slot, pl.ds(0, upper)] if half == 0 else panel.at[slot, pl.ds(upper, count - upper)]

    def move(g, axis, da, db, direction, half, index):
        x_first = GROUPS[g][2]
        offset = (da, db) if x_first else (db, da)
        along = (direction, 0) if (axis == 0) == x_first else (0, direction)
        ref = part(at_col(*offset), g, half)
        return pltpu.make_async_remote_copy(
            src_ref=ref,
            dst_ref=ref,
            send_sem=ring_send.at[g, index],
            recv_sem=ring_recv.at[g, index],
            device_id=(r, at_col(*along)),
            device_id_type=MESH,
        )

    def wait(spec):
        g, axis, da, db, direction, half, index = spec
        back = (da - direction, db) if axis == 0 else (da, db - direction)
        move(g, axis, back[0], back[1], direction, half, index).wait_recv()

    def first(g, k):
        return (g, 0, 0, 0, (1, -1)[k], None, k)

    def first_on(g, k):
        return (g, 0, (-1, 1)[k], 0, (1, -1)[k], k, 2 + k)

    def second(g, q, k):
        return (g, 1, (0, -1, 1, 2)[q], 0, (1, -1)[k], None, 4 + 4 * q + k)

    def second_on(g, q, k):
        return (g, 1, (0, -1, 1, 2)[q], (-1, 1)[k], (1, -1)[k], k, 6 + 4 * q + k)

    started = []

    def start(spec):
        started.append(spec)
        move(*spec).start()

    def own_blocks(g):
        return [first(g, 0), first(g, 1), second(g, 0, 0), second(g, 0, 1)]

    def s1(g):
        @pl.when(other)
        def _():
            spread(g).wait_recv()
            for spec in own_blocks(g):
                move(*spec).start()

    def s2(g):
        for k in range(2):
            wait(first(g, k))
            start(first_on(g, k))
        for q in (1, 2):
            for k in range(2):
                start(second(g, q, k))

    def s3(g):
        for k in range(2):
            wait(second(g, 0, k))
            start(second_on(g, 0, k))

    def s4(g):
        for k in range(2):
            wait(first_on(g, k))
        for k in range(2):
            start(second(g, 3, k))

    def s5a(g):
        for k in range(2):
            wait(second(g, 1, k))
            start(second_on(g, 1, k))

    def s5b(g):
        for k in range(2):
            wait(second(g, 2, k))
            start(second_on(g, 2, k))

    def s6(g):
        for k in range(2):
            wait(second(g, 3, k))
            start(second_on(g, 3, k))

    def s7(g):
        for q in range(4):
            for k in range(2):
                wait(second_on(g, q, k))

    b_row = lax.rem(c, 8)
    b_y, b_core = b_row // 2, b_row % 2
    b_root, b_even = r == b_row, core == b_core

    def bx_copy(q, t, target):
        held = lax.rem(c, 8)
        return pltpu.make_async_remote_copy(
            src_ref=sum0.at[t],
            dst_ref=brows.at[q, held],
            send_sem=bx_send.at[t - 1],
            recv_sem=bx_recv.at[q, held],
            device_id=(r, target),
            device_id_type=MESH,
        )

    def bx_arrival(q, held):
        return pltpu.make_async_remote_copy(
            src_ref=sum0.at[1],
            dst_ref=brows.at[q, held],
            send_sem=bx_send.at[0],
            recv_sem=bx_recv.at[q, held],
            device_id=(r, at_col(1, 0)),
            device_id_type=MESH,
        )

    def bx_start():
        @pl.when(source)
        def _():
            bx_copy(0, 1, r + 8).start()
            bx_copy(1, 3, r + 8).start()

        @pl.when(jnp.logical_and(source, c != r))
        def _():
            bx_copy(1, 2, r).start()

        @pl.when(jnp.logical_and(source, c == r))
        def _():
            brows[1, r] = sum0[2]

    def bx_end():
        @pl.when(source)
        def _():
            bx_copy(0, 1, r + 8).wait_send()
            bx_copy(1, 3, r + 8).wait_send()

        @pl.when(jnp.logical_and(source, c != r))
        def _():
            bx_copy(1, 2, r).wait_send()

    def b_out(q, step):
        return pltpu.make_async_remote_copy(
            src_ref=brows.at[q],
            dst_ref=brows.at[q],
            send_sem=b_send.at[q, step - 1],
            recv_sem=b_recv.at[q, step - 1],
            device_id=(y_peer(step), c),
            device_id_type=MESH,
        )

    def b_pair(q):
        return pltpu.make_async_remote_copy(
            src_ref=brows.at[q],
            dst_ref=brows.at[q],
            send_sem=b_send.at[q, 3],
            recv_sem=b_recv.at[q, 3],
            device_id=(y_peer(0, 1), c),
            device_id_type=MESH,
        )

    def with_b(q, condition):
        return condition if q == 1 else jnp.logical_and(condition, other)

    def b_start(_):
        for q in (1, 0):

            @pl.when(with_b(q, b_root))
            def _():
                for held in range(8):

                    @pl.when(c != held)
                    def _():
                        bx_arrival(q, held).wait_recv()

                for step in (1, 3, 2):
                    b_out(q, step).start()
                b_pair(q).start()

    def b_relay(_):
        for q in (1, 0):
            for step in (1, 2, 3):

                @pl.when(with_b(q, jnp.logical_and(b_even, lax.rem(b_y + step, 4) == y)))
                def _():
                    b_out(q, step).wait_recv()
                    b_pair(q).start()

    def b_wait():
        for q in (1, 0):

            @pl.when(with_b(q, jnp.logical_not(b_even)))
            def _():
                b_pair(q).wait_recv()

    def b_end():
        for q in (1, 0):

            @pl.when(with_b(q, b_root))
            def _():
                for step in (1, 2, 3):
                    b_out(q, step).wait_send()

            @pl.when(with_b(q, b_even))
            def _():
                b_pair(q).wait_send()

    def child1(_):
        for step in STEPS:
            child_copy(1, step).start()

    bx_start()
    for g in range(3):

        @pl.when(source)
        def _():
            spread(g).start()

    for g in range(3):
        started.extend(own_blocks(g))

    def s0(g):
        @pl.when(source)
        def _():
            for spec in own_blocks(g):
                move(*spec).start()

    s0(0)

    for step in (1, 3, 2):
        dz_copy(0, step, step).wait_recv()
    d_start(0)
    d_start(1)
    for step in (1, 3, 2):
        dz_copy(1, step, step).wait_recv()
    drows[r] = dplane[...]
    d_relay(0)
    d_start(2)
    d_wait(0)

    row = lax.broadcasted_iota(I32, (TILE, TILE), 0)
    col = lax.broadcasted_iota(I32, (TILE, TILE), 1)
    inv[...] = jnp.zeros_like(inv)

    b, e, f = 0, 1, 2
    before = {
        0: [(s0, e), (s1, b)],
        1: [(s1, f), (s2, b)],
        2: [(s3, b)],
        3: [(s5b, b)],
        4: [(s2, f), (s4, e), (s3, e)],
        5: [(b_relay, 0)],
        6: [(s4, b)],
        7: [],
    }
    after = {
        0: [(d_relay, 1), (d_wait, 1), (d_start, 3), (s1, e)],
        1: [(d_relay, 2), (d_wait, 2), (s0, f), (b_start, 0)],
        2: [(s2, e), (d_relay, 3)],
        3: [(s3, f), (d_wait, 3), (child1, 0)],
        4: [],
        5: [(s5a, b)],
        6: [(s4, f), (s5b, e)],
        7: [(s6, b), (s5a, f), (s5a, e)],
    }

    for j in range(PB):
        for act, g in before[j]:
            act(g)
        here, done = pl.ds(j * TILE, TILE), pl.ds(0, j * TILE)
        under = pl.ds((j + 1) * TILE, (PB - 1 - j) * TILE)
        square = drows[j, j]
        square = jnp.where(row >= col, square, 0.0) + jnp.where(row > col, square, 0.0).T
        if j > 0:
            left = lmat[here, done]
            square = square - dot(left, left, NTC)
            mixed = dot(left, inv[done, done], NN)
        if j + 1 < PB:
            below = jnp.concatenate([drows[i, j] for i in range(j + 1, PB)], 0)
            if j > 0:
                below = below - dot(lmat[under, done], left, NTC)
        upper, inverse = factor_tile(square)
        lmat[here, here] = upper.T
        if j > 0:
            inv[here, done] = -dot(inverse, mixed, NN)
        inv[here, here] = inverse
        if j + 1 < PB:
            lmat[under, here] = dot(below, inverse, NTC)
        for act, g in after[j]:
            act(g)

    b_wait()

    top, bottom = list(range(8)), [partner_slot(k) for k in range(8)]
    unused = jnp.zeros((TILE, TILE), F32)
    mine = jnp.concatenate(
        [
            jnp.concatenate([jnp.where(source, unused, brows[0, s]) for s in range(8)], 1),
            jnp.concatenate([brows[1, s] for s in range(8)], 1),
        ],
        0,
    )
    for k in range(4):
        here, upto = pl.ds(256 * k, 256), 256 * (k + 1)
        half[:, here] = dot(mine[:, :upto], inv[here, :upto], NTC)
    own = inv.at[pl.ds(pl.multiple_of(lax.rem(c, 8) * TILE, TILE), TILE)]
    for k in range(4):
        here, rest = pl.ds(256 * k, 256), pl.ds(256 * k, 1024 - 256 * k)
        weights = dot(half[:, rest], inv[rest, here], NN)
        weights = jnp.concatenate([jnp.where(source, -own[:, here], weights[:TILE]), weights[TILE:]], 0)
        high = weights.astype(BF16)
        wt_hi[:, here] = high
        wt_lo[:, here] = (weights - high.astype(F32)).astype(BF16)

    s6(e)
    s5b(f)
    s6(f)
    assemble1()

    def finish(g, lo, hi):
        panel, base = panels[g], GROUPS[g][0]
        count = hi - lo
        for h, order in enumerate((top, bottom)):
            rows = jnp.concatenate(
                [panel[s, lo - base : hi - base].reshape(count * 64, TILE) for s in order], 1
            )
            rows_hi = rows.astype(BF16)
            rows_lo = (rows - rows_hi.astype(F32)).astype(BF16)
            update = lax.dot_general(rows_hi, wt_hi[...], NTC, preferred_element_type=F32)
            update += lax.dot_general(rows_lo, wt_hi[...], NTC, preferred_element_type=F32)
            update += lax.dot_general(rows_hi, wt_lo[...], NTC, preferred_element_type=F32)
            for t in range(lo, hi):
                piece = update[64 * (t - lo) : 64 * (t - lo + 1)]
                base0, base1 = sum0[t, pl.ds(64 * h, 64), :], sum1[t, pl.ds(64 * h, 64), :]
                new0 = jnp.where(source, 0.0, base0) - piece[:, :TILE]
                new1 = base1 - piece[:, TILE:]
                if t < 4:
                    i = 8 * t + r
                    new0 = jnp.where(i >= c, new0, base0)
                    new1 = jnp.where(i >= 16 + c, new1, base1)
                out[t, pl.ds(128 * h, 64, stride=2), :] = new0
                out[t, pl.ds(128 * h + 1, 64, stride=2), :] = new1

    def store(piece, lo, hi):
        return pltpu.make_async_copy(
            out.at[pl.ds(lo, hi - lo)], out_any.at[pl.ds(lo, hi - lo)], stored.at[piece]
        )

    block = lmat[
        pl.ds(pl.multiple_of(r * TILE, TILE), TILE), pl.ds(pl.multiple_of(lax.rem(c, 8) * TILE, TILE), TILE)
    ]
    factored = jnp.logical_and(source, r >= c)
    out[0, pl.ds(0, TILE, stride=2), :] = jnp.where(factored, block, sum0[0])
    out[0, pl.ds(1, TILE, stride=2), :] = sum1[0]
    store(0, 0, 1).start()
    for g, (lo, hi, _) in enumerate(GROUPS):
        s7(g)
        finish(g, lo, hi)
        store(1 + g, lo, hi).start()

    @pl.when(source)
    def _():
        for step in range(1, 4):
            dx_copy(step).wait_send()
        for g in range(3):
            spread(g).wait_send()

    for kind in range(3):
        for step in STEPS:
            child_copy(kind, step).wait_send()
    for sx in range(2):
        for step in range(1, 4):
            dz_copy(sx, step).wait_send()
    for spec in started:
        move(*spec).wait_send()
    for q in range(4):
        d_end(q)
    bx_end()
    b_end()
    store(0, 0, 1).wait()
    for g, (lo, hi, _) in enumerate(GROUPS):
        store(1 + g, lo, hi).wait()


def copy_kernel(source, out, buffer, load, store):
    parts = [pl.ds(6 * i, 6) for i in range(4)]
    loads = [pltpu.make_async_copy(source.at[p], buffer.at[p], load.at[i]) for i, p in enumerate(parts)]
    stores = [pltpu.make_async_copy(buffer.at[p], out.at[p], store.at[i]) for i, p in enumerate(parts)]
    for copy in loads:
        copy.start()
    for first, second in zip(loads, stores):
        first.wait()
        second.start()
    for copy in stores:
        copy.wait()


def shards(front, child_one, child_two, map_one, map_two, owner_one, owner_two):
    whole = pl.BlockSpec(memory_space=pl.ANY)
    smem = pl.BlockSpec(memory_space=pltpu.SMEM)
    dma = pltpu.SemaphoreType.DMA

    def space(*shape):
        return pltpu.VMEM(shape, F32)

    out = pl.pallas_call(
        kernel,
        out_shape=jax.ShapeDtypeStruct((NT, 256, TILE), F32),
        in_specs=[whole] * 3 + [smem] * 4,
        out_specs=whole,
        scratch_shapes=[
            space(NT, 256, TILE), space(8, 256, TILE), space(16, 256, TILE),
            space(8, 2, TILE, TILE), space(8, TILE, TILE), space(8, 3, TILE, TILE),
            space(9, 2, TILE, TILE), space(9, TILE, TILE), space(9, 3, TILE, TILE),
            space(NT, TILE, TILE), space(NT, TILE, TILE),
            *[space(16, hi - lo, 64, TILE) for lo, hi, _ in GROUPS],
            space(8, TILE, TILE), space(8, 8, TILE, TILE), space(2, 8, TILE, TILE),
            space(PB * TILE, PB * TILE), space(PB * TILE, PB * TILE),
            space(256, PB * TILE),
            pltpu.VMEM((256, PB * TILE), BF16), pltpu.VMEM((256, PB * TILE), BF16),
            space(NT, 256, TILE),
            pltpu.SMEM((128,), I32), pltpu.SMEM((32,), I32),
            dma((3,)), dma((3, 7)), dma((3, 7)),
            dma((3,)), dma((3,)), dma((3, 20)), dma((3, 20)),
            dma((3,)), dma((2,)), dma((2, 3)), dma((2, 3)), dma((4, 7)), dma((4, 7)),
            dma((3,)), dma((2, 8)), dma((2, 4)), dma((2, 4)), dma((4,)),
        ],
        compiler_params=pltpu.CompilerParams(
            collective_id=0, has_side_effects=True, vmem_limit_bytes=60 * 2**20
        ),
    )(
        front.reshape(NT, 256, TILE),
        child_one.reshape(8, 256, TILE),
        child_two.reshape(16, 256, TILE),
        map_one, map_two, owner_one, owner_two,
    )
    out = pl.pallas_call(
        copy_kernel,
        out_shape=jax.ShapeDtypeStruct((NT, 256, TILE), F32),
        in_specs=[whole],
        out_specs=whole,
        scratch_shapes=[space(NT, 256, TILE), dma((4,)), dma((4,))],
        compiler_params=pltpu.CompilerParams(vmem_limit_bytes=60 * 2**20),
    )(out)
    return out.reshape(front.shape)


def solution(mesh):
    placed = P(None, "row", None, None, "col", None)
    return jax.shard_map(
        shards,
        mesh=mesh,
        in_specs=(placed, placed, placed, P(), P(), P(), P()),
        out_specs=placed,
        check_vma=False,
    )
```

```python
import functools

import jax
import jax.numpy as jnp
from jax import lax
from jax.experimental import pallas as pl
from jax.experimental.pallas import tpu as pltpu
from jax.sharding import PartitionSpec as P

F32, BF16, I32 = jnp.float32, jnp.bfloat16, jnp.int32
HIGHEST = lax.Precision.HIGHEST
MESH = pl.DeviceIdType.MESH
TILE, PB, NT = 128, 8, 24
LEAF = 16
NN = (((1,), (0,)), ((), ()))
NTC = (((1,), (1,)), ((), ()))
TN = (((0,), (0,)), ((), ()))
GROUPS = ((1, 9, True), (9, 18, False), (18, 24, True))
CHUNKS = ((0, 1), (1, 2), (2, 4), (4, 8))
STEPS = (1, 7, 2, 6, 3, 5, 4)


def dot(a, b, dims):
    return lax.dot_general(a, b, dims, precision=HIGHEST, preferred_element_type=F32)


def split3(v):
    high = v.astype(BF16)
    rest = v - high.astype(F32)
    middle = rest.astype(BF16)
    low = (rest - middle.astype(F32)).astype(BF16)
    return [part.astype(F32) for part in (high, middle, low)]


def rank_update(a, b):
    ah, am, al = split3(a)
    bh, bm, bl = split3(b)
    left = jnp.concatenate([ah, ah, am, ah, am, al], 0).astype(BF16)
    right = jnp.concatenate([bl, bm, bm, bh, bh, bh], 0).astype(BF16)
    return lax.dot_general(left, right, TN, preferred_element_type=F32)


def leaf(rows_u, rows_v, offset):
    count = rows_u.shape[0]
    index = lax.broadcasted_iota(I32, (count, TILE), 0)
    cols = [
        jnp.broadcast_to(rows_u[:, offset + k : offset + k + 1], (count, TILE)) for k in range(count)
    ]
    scale = jnp.zeros((count, TILE), F32)
    for j in range(count):
        pivot = cols[j][j : j + 1, :]
        scale = jnp.where(index == j, lax.rsqrt(pivot), scale)
        if j + 1 < count:
            ratio = cols[j] * (1.0 / pivot)
            for k in range(j + 1, count):
                cols[k] = cols[k] - ratio * cols[k][j : j + 1, :]
            ratio = jnp.where(index > j, ratio, 0.0)
            rows_u = rows_u - ratio * rows_u[j : j + 1, :]
            rows_v = rows_v - ratio * rows_v[j : j + 1, :]
    return rows_u * scale, rows_v * scale


def factor_tile(square):
    row = lax.broadcasted_iota(I32, (TILE, TILE), 0)
    col = lax.broadcasted_iota(I32, (TILE, TILE), 1)
    unit = jnp.where(row == col, 1.0, 0.0).astype(F32)
    count = TILE // LEAF
    left = [square[i * LEAF : (i + 1) * LEAF] for i in range(count)]
    right = [unit[i * LEAF : (i + 1) * LEAF] for i in range(count)]
    for b in range(count):
        left[b], right[b] = leaf(left[b], right[b], b * LEAF)
        if b + 1 < count:
            change = rank_update(left[b], jnp.concatenate([left[b], right[b]], 1))
            for i in range(b + 1, count):
                left[i] = left[i] - change[i * LEAF : (i + 1) * LEAF, :TILE]
                right[i] = right[i] - change[i * LEAF : (i + 1) * LEAF, TILE:]
    upper = jnp.where(col >= row, jnp.concatenate(left, 0), 0.0)
    inverse = jnp.where(col <= row, jnp.concatenate(right, 0), 0.0)
    return upper, inverse


def partner_slot(c):
    return 12 - 4 * (c // 4) + c % 4


def kernel(
    front_in, one_in, two_in, map_one, map_two, own_one, own_two, out_any,
    front, one, two, stage0, stage2, stage1, got0, got2, got1, sum0, sum1,
    panel_a, panel_b, panel_c, dplane, drows, brows, lmat, inv, half, partial, wt_hi, wt_lo, out,
    slots, table,
    load, child_send, child_recv, spread_send, spread_recv, ring_send, ring_recv,
    dx_send, dx_recv, dz_send, dz_recv, d_send, d_recv, bx_send, bx_recv, b_send, b_recv, stored,
):
    r, c = lax.axis_index("row"), lax.axis_index("col")
    y, core = r // 2, r % 2
    x, z = c // 4, c % 4
    source = x < 2
    other = jnp.logical_not(source)
    partner = (3 - x) * 4 + z
    panels = (panel_a, panel_b, panel_c)

    def at_col(dx, dz):
        return lax.rem(x + dx + 4, 4) * 4 + lax.rem(z + dz + 4, 4)

    def row_peer(step):
        return lax.rem(r + step, 8)

    def y_peer(step, across=0):
        return lax.rem(y + step, 4) * 2 + (core if across == 0 else 1 - core)

    barrier = pltpu.get_barrier_semaphore()
    for step in range(1, 8):
        pl.semaphore_signal(barrier, inc=1, device_id=(row_peer(step), c), device_id_type=MESH)
    for step in range(1, 4):
        pl.semaphore_signal(barrier, inc=1, device_id=(r, at_col(step, 0)), device_id_type=MESH)
        pl.semaphore_signal(barrier, inc=1, device_id=(r, at_col(0, step)), device_id_type=MESH)

    @pl.when(lax.rem(c, 8) == r)
    def _():
        for held in range(8):

            @pl.when(c != held)
            def _():
                pl.semaphore_signal(barrier, inc=1, device_id=(r, held), device_id_type=MESH)

    loads = [
        pltpu.make_async_copy(a, b, load.at[i])
        for i, (a, b) in enumerate(((one_in, one), (two_in, two), (front_in, front)))
    ]
    for copy in loads:
        copy.start()

    def find_one(g, carry):
        seen, picks = carry[0], list(carry[1:])
        for v in range(8):
            mine = own_one[8 * g + v] == r
            picks[v] = jnp.where(mine, seen, picks[v])
            seen = seen + mine.astype(I32)
        return (seen, *picks)

    picks_one = lax.fori_loop(0, 8, find_one, (jnp.int32(0),) * 9)[1:]

    def find_two(g, carry):
        seen, first, second = carry[0], list(carry[1:9]), list(carry[9:])
        for v in range(8):
            mine = own_two[8 * g + v] == r
            first[v] = jnp.where(mine, second[v], first[v])
            second[v] = jnp.where(mine, seen, second[v])
            seen = seen + mine.astype(I32)
        return (seen, *first, *second)

    picks_two = lax.fori_loop(0, 16, find_two, (jnp.int32(0),) * 17)[1:]
    for v in range(8):
        slots[v] = jnp.minimum(picks_one[v], 7)
        slots[8 + v] = jnp.minimum(picks_two[v], 15)
        slots[16 + v] = jnp.minimum(picks_two[8 + v], 15)

    def stage0_rows(v, carry):
        pick = pl.ds(0, TILE, stride=2)
        stage0[v, 0] = one[slots[v], pick, :]
        stage0[v, 1] = two[slots[8 + v], pick, :]
        stage2[v] = two[slots[16 + v], pick, :]
        return carry

    def stage1_rows(v, carry):
        pick = pl.ds(1, TILE, stride=2)
        stage1[v, 0] = one[slots[v], pick, :]
        stage1[v, 1] = two[slots[8 + v], pick, :]
        stage1[v, 2] = two[slots[16 + v], pick, :]
        return carry

    def child_copy(kind, step):
        peer = row_peer(step)
        return pltpu.make_async_remote_copy(
            src_ref=(stage0, stage1, stage2)[kind].at[peer],
            dst_ref=(got0, got1, got2)[kind].at[r],
            send_sem=child_send.at[kind, step - 1],
            recv_sem=child_recv.at[kind, step - 1],
            device_id=(peer, c),
            device_id_type=MESH,
        )

    loads[0].wait()
    loads[1].wait()
    lax.fori_loop(0, 8, stage0_rows, 0)
    pl.semaphore_wait(
        barrier, 13 + source.astype(I32) + jnp.logical_and(source, c != r).astype(I32)
    )
    for kind in (0, 2):
        for step in STEPS:
            child_copy(kind, step).start()
    lax.fori_loop(0, 8, stage1_rows, 0)
    for buffer, staged in ((got0, stage0), (got1, stage1), (got2, stage2)):
        buffer[r] = staged[r]
        buffer[8] = jnp.zeros(buffer.shape[1:], F32)

    sources = [own_two[8 * g + r] for g in range(16)]
    for g in range(16):
        rank = jnp.int32(0)
        for h in range(g):
            rank = rank + (sources[h] == sources[g]).astype(I32)
        table[g] = jnp.clip(sources[g], 0, 7)
        table[16 + g] = jnp.minimum(rank, 1)

    def find_targets(t, carry):
        at_one, at_two = carry
        hit_one = map_one[8 * at_one] // 8 == t
        hit_two = map_two[8 * at_two] // 8 == t
        slots[32 + t] = jnp.where(hit_one, jnp.clip(own_one[8 * at_one + r], 0, 7), 8)
        slots[64 + t] = jnp.where(hit_two, table[at_two], 8)
        slots[96 + t] = jnp.where(hit_two, table[16 + at_two] + 1, 1)
        return (
            jnp.minimum(at_one + hit_one.astype(I32), 7),
            jnp.minimum(at_two + hit_two.astype(I32), 15),
        )

    lax.fori_loop(0, NT, find_targets, (jnp.int32(0), jnp.int32(0)))
    loads[2].wait()

    def assemble0():
        for step in STEPS:
            child_copy(2, step).wait_recv()

        def body(t, carry):
            origin, second = slots[64 + t], slots[96 + t] == 2
            total = front[t, pl.ds(0, TILE, stride=2), :] + got0[slots[32 + t], 0]
            total = total + got0[jnp.where(second, 8, origin), 1]
            sum0[t] = total + got2[jnp.where(second, origin, 8)]
            return carry

        lax.fori_loop(0, NT, body, 0)

    def assemble1():
        for step in STEPS:
            child_copy(1, step).wait_recv()

        def body(t, carry):
            sum1[t] = (
                front[t, pl.ds(1, TILE, stride=2), :] + got1[slots[32 + t], 0]
            ) + got1[slots[64 + t], slots[96 + t]]
            return carry

        lax.fori_loop(0, NT, body, 0)

    def dx_copy(step):
        held = lax.rem(c, 8)
        return pltpu.make_async_remote_copy(
            src_ref=dplane.at[held],
            dst_ref=dplane.at[held],
            send_sem=dx_send.at[step - 1],
            recv_sem=dx_recv.at[lax.rem(x, 2)],
            device_id=(r, at_col(step, 0)),
            device_id_type=MESH,
        )

    def dx_arrival(sx):
        held = 4 * sx + z
        return pltpu.make_async_remote_copy(
            src_ref=dplane.at[held],
            dst_ref=dplane.at[held],
            send_sem=dx_send.at[0],
            recv_sem=dx_recv.at[sx],
            device_id=(r, at_col(1, 0)),
            device_id_type=MESH,
        )

    def dz_copy(sx, step, back=0):
        held = 4 * sx + lax.rem(z + 4 - back, 4)
        return pltpu.make_async_remote_copy(
            src_ref=dplane.at[held],
            dst_ref=dplane.at[held],
            send_sem=dz_send.at[sx, step - 1],
            recv_sem=dz_recv.at[sx, step - 1],
            device_id=(r, at_col(0, step)),
            device_id_type=MESH,
        )

    for step in STEPS:
        child_copy(0, step).wait_recv()

    @pl.when(source)
    def _():
        total = front[0, pl.ds(0, TILE, stride=2), :] + got0[jnp.clip(own_one[r], 0, 7), 0]
        dplane[lax.rem(c, 8)] = total + got0[jnp.clip(own_two[r], 0, 7), 1]
        for step in (1, 3, 2):
            dx_copy(step).start()

    for sx in range(2):

        @pl.when(x != sx)
        def _():
            dx_arrival(sx).wait_recv()

        for step in (1, 3, 2):
            dz_copy(sx, step).start()
    def d_out(q, step):
        lo, hi = CHUNKS[q]
        return pltpu.make_async_remote_copy(
            src_ref=dplane.at[pl.ds(lo, hi - lo)],
            dst_ref=drows.at[r, pl.ds(lo, hi - lo)],
            send_sem=d_send.at[q, step - 1],
            recv_sem=d_recv.at[q, step - 1],
            device_id=(y_peer(step), c),
            device_id_type=MESH,
        )

    def d_pair(q, step):
        lo, hi = CHUNKS[q]
        held = y_peer(step)
        return pltpu.make_async_remote_copy(
            src_ref=dplane.at[pl.ds(lo, hi - lo)] if step == 0 else drows.at[held, pl.ds(lo, hi - lo)],
            dst_ref=drows.at[held, pl.ds(lo, hi - lo)],
            send_sem=d_send.at[q, 3 + step],
            recv_sem=d_recv.at[q, 3 + step],
            device_id=(y_peer(0, 1), c),
            device_id_type=MESH,
        )

    def d_start(q):
        @pl.when(r >= CHUNKS[q][0])
        def _():
            for step in (1, 3, 2):
                d_out(q, step).start()
            d_pair(q, 0).start()

    def d_relay(q):
        for step in (1, 3, 2):

            @pl.when(y_peer(4 - step) >= CHUNKS[q][0])
            def _():
                d_out(q, step).wait_recv()
                d_pair(q, 4 - step).start()

    def d_wait(q):
        for step in range(4):

            @pl.when(y_peer(step, 1) >= CHUNKS[q][0])
            def _():
                d_pair(q, step).wait_recv()

    def d_end(q):
        @pl.when(r >= CHUNKS[q][0])
        def _():
            for step in (1, 3, 2):
                d_out(q, step).wait_send()
            d_pair(q, 0).wait_send()

        for step in (1, 3, 2):

            @pl.when(y_peer(4 - step) >= CHUNKS[q][0])
            def _():
                d_pair(q, 4 - step).wait_send()

    assemble0()

    @pl.when(source)
    def _():
        for g in range(3):
            lo, hi, _ = GROUPS[g]
            panels[g][c] = sum0[lo:hi, :64, :]

    def spread(g):
        lo, hi, _ = GROUPS[g]
        return pltpu.make_async_remote_copy(
            src_ref=sum0.at[pl.ds(lo, hi - lo), pl.ds(64, 64)],
            dst_ref=panels[g].at[partner],
            send_sem=spread_send.at[g],
            recv_sem=spread_recv.at[g],
            device_id=(r, partner),
            device_id_type=MESH,
        )

    def part(slot, g, half):
        lo, hi, _ = GROUPS[g]
        count, panel = hi - lo, panels[g]
        upper = (count + 1) // 2
        if half is None:
            return panel.at[slot]
        return panel.at[slot, pl.ds(0, upper)] if half == 0 else panel.at[slot, pl.ds(upper, count - upper)]

    def move(g, axis, da, db, direction, half, index):
        x_first = GROUPS[g][2]
        offset = (da, db) if x_first else (db, da)
        along = (direction, 0) if (axis == 0) == x_first else (0, direction)
        ref = part(at_col(*offset), g, half)
        return pltpu.make_async_remote_copy(
            src_ref=ref,
            dst_ref=ref,
            send_sem=ring_send.at[g, index],
            recv_sem=ring_recv.at[g, index],
            device_id=(r, at_col(*along)),
            device_id_type=MESH,
        )

    def wait(spec):
        g, axis, da, db, direction, half, index = spec
        back = (da - direction, db) if axis == 0 else (da, db - direction)
        move(g, axis, back[0], back[1], direction, half, index).wait_recv()

    def first(g, k):
        return (g, 0, 0, 0, (1, -1)[k], None, k)

    def first_on(g, k):
        return (g, 0, (-1, 1)[k], 0, (1, -1)[k], k, 2 + k)

    def second(g, q, k):
        return (g, 1, (0, -1, 1, 2)[q], 0, (1, -1)[k], None, 4 + 4 * q + k)

    def second_on(g, q, k):
        return (g, 1, (0, -1, 1, 2)[q], (-1, 1)[k], (1, -1)[k], k, 6 + 4 * q + k)

    started = []

    def start(spec):
        started.append(spec)
        move(*spec).start()

    def own_blocks(g):
        return [first(g, 0), first(g, 1), second(g, 0, 0), second(g, 0, 1)]

    def s1(g):
        @pl.when(other)
        def _():
            spread(g).wait_recv()
            for spec in own_blocks(g):
                move(*spec).start()

    def s2(g):
        for k in range(2):
            wait(first(g, k))
            start(first_on(g, k))
        for q in (1, 2):
            for k in range(2):
                start(second(g, q, k))

    def s3(g):
        for k in range(2):
            wait(second(g, 0, k))
            start(second_on(g, 0, k))

    def s4(g):
        for k in range(2):
            wait(first_on(g, k))
        for k in range(2):
            start(second(g, 3, k))

    def s5a(g):
        for k in range(2):
            wait(second(g, 1, k))
            start(second_on(g, 1, k))

    def s5b(g):
        for k in range(2):
            wait(second(g, 2, k))
            start(second_on(g, 2, k))

    def s6(g):
        for k in range(2):
            wait(second(g, 3, k))
            start(second_on(g, 3, k))

    def s7(g):
        for q in range(4):
            for k in range(2):
                wait(second_on(g, q, k))

    b_row = lax.rem(c, 8)
    b_y, b_core = b_row // 2, b_row % 2
    b_root, b_even = r == b_row, core == b_core

    def bx_copy(q, t, target):
        held = lax.rem(c, 8)
        return pltpu.make_async_remote_copy(
            src_ref=sum0.at[t],
            dst_ref=brows.at[q, held],
            send_sem=bx_send.at[t - 1],
            recv_sem=bx_recv.at[q, held],
            device_id=(r, target),
            device_id_type=MESH,
        )

    def bx_arrival(q, held):
        return pltpu.make_async_remote_copy(
            src_ref=sum0.at[1],
            dst_ref=brows.at[q, held],
            send_sem=bx_send.at[0],
            recv_sem=bx_recv.at[q, held],
            device_id=(r, at_col(1, 0)),
            device_id_type=MESH,
        )

    def bx_start():
        @pl.when(source)
        def _():
            bx_copy(0, 1, r + 8).start()
            bx_copy(1, 3, r + 8).start()

        @pl.when(jnp.logical_and(source, c != r))
        def _():
            bx_copy(1, 2, r).start()

        @pl.when(jnp.logical_and(source, c == r))
        def _():
            brows[1, r] = sum0[2]

    def bx_end():
        @pl.when(source)
        def _():
            bx_copy(0, 1, r + 8).wait_send()
            bx_copy(1, 3, r + 8).wait_send()

        @pl.when(jnp.logical_and(source, c != r))
        def _():
            bx_copy(1, 2, r).wait_send()

    def b_out(q, step):
        return pltpu.make_async_remote_copy(
            src_ref=brows.at[q],
            dst_ref=brows.at[q],
            send_sem=b_send.at[q, step - 1],
            recv_sem=b_recv.at[q, step - 1],
            device_id=(y_peer(step), c),
            device_id_type=MESH,
        )

    def b_pair(q):
        return pltpu.make_async_remote_copy(
            src_ref=brows.at[q],
            dst_ref=brows.at[q],
            send_sem=b_send.at[q, 3],
            recv_sem=b_recv.at[q, 3],
            device_id=(y_peer(0, 1), c),
            device_id_type=MESH,
        )

    def with_b(q, condition):
        return condition if q == 1 else jnp.logical_and(condition, other)

    def b_start(_):
        for q in (1, 0):

            @pl.when(with_b(q, b_root))
            def _():
                for held in range(8):

                    @pl.when(c != held)
                    def _():
                        bx_arrival(q, held).wait_recv()

                for step in (1, 3, 2):
                    b_out(q, step).start()
                b_pair(q).start()

    def b_relay(_):
        for q in (1, 0):
            for step in (1, 2, 3):

                @pl.when(with_b(q, jnp.logical_and(b_even, lax.rem(b_y + step, 4) == y)))
                def _():
                    b_out(q, step).wait_recv()
                    b_pair(q).start()

    def b_wait(_):
        for q in (1, 0):

            @pl.when(with_b(q, jnp.logical_not(b_even)))
            def _():
                b_pair(q).wait_recv()

    def b_end():
        for q in (1, 0):

            @pl.when(with_b(q, b_root))
            def _():
                for step in (1, 2, 3):
                    b_out(q, step).wait_send()

            @pl.when(with_b(q, b_even))
            def _():
                b_pair(q).wait_send()

    def child1(_):
        for step in STEPS:
            child_copy(1, step).start()

    bx_start()
    for g in range(3):

        @pl.when(source)
        def _():
            spread(g).start()

    for g in range(3):
        started.extend(own_blocks(g))

    def s0(g):
        @pl.when(source)
        def _():
            for spec in own_blocks(g):
                move(*spec).start()

    s0(0)

    for step in (1, 3, 2):
        dz_copy(0, step, step).wait_recv()
    d_start(0)
    d_start(1)
    for step in (1, 3, 2):
        dz_copy(1, step, step).wait_recv()
    drows[r] = dplane[...]
    d_relay(0)
    d_start(2)
    d_wait(0)

    row = lax.broadcasted_iota(I32, (TILE, TILE), 0)
    col = lax.broadcasted_iota(I32, (TILE, TILE), 1)
    inv[...] = jnp.zeros_like(inv)

    b, e, f = 0, 1, 2
    before = {
        0: [(s0, e), (s1, b)],
        1: [(s0, f)],
        2: [(s3, b)],
        3: [],
        4: [(s2, f), (s3, e)],
        5: [(s4, e), (s5a, b), (b_relay, 0)],
        6: [(s4, f)],
        7: [(s6, e)],
    }
    after = {
        0: [(d_relay, 1), (d_wait, 1), (d_start, 3), (s1, e)],
        1: [(d_relay, 2), (d_wait, 2), (s1, f), (s2, b), (b_start, 0)],
        2: [(s2, e), (d_relay, 3)],
        3: [(s4, b), (d_wait, 3), (child1, 0)],
        4: [(s5b, b)],
        5: [(s5b, e), (s3, f)],
        6: [(s5a, e), (s6, b), (b_wait, 0)],
        7: [(s5a, f), (s5b, f)],
    }

    for j in range(PB):
        for act, g in before[j]:
            act(g)
        here, done = pl.ds(j * TILE, TILE), pl.ds(0, j * TILE)
        under = pl.ds((j + 1) * TILE, (PB - 1 - j) * TILE)
        square = drows[j, j]
        square = jnp.where(row >= col, square, 0.0) + jnp.where(row > col, square, 0.0).T
        if j > 0:
            left = lmat[here, done]
            square = square - dot(left, left, NTC)
            mixed = dot(left, inv[done, done], NN)
        if j + 1 < PB:
            below = jnp.concatenate([drows[i, j] for i in range(j + 1, PB)], 0)
            if j > 0:
                below = below - dot(lmat[under, done], left, NTC)
        if j + 1 == PB:
            unused = jnp.zeros((TILE, TILE), F32)
            mine = jnp.concatenate(
                [
                    jnp.concatenate([jnp.where(source, unused, brows[0, s]) for s in range(8)], 1),
                    jnp.concatenate([brows[1, s] for s in range(8)], 1),
                ],
                0,
            )
            for k in range(3):
                here_k, upto = pl.ds(256 * k, 256), 256 * (k + 1)
                half[:, here_k] = dot(mine[:, :upto], inv[here_k, :upto], NTC)
            for k in range(3):
                here_k, rest = pl.ds(256 * k, 256), pl.ds(256 * k, 768 - 256 * k)
                partial[:, here_k] = dot(half[:, rest], inv[rest, here_k], NN)
        upper, inverse = factor_tile(square)
        lmat[here, here] = upper.T
        if j > 0:
            inv[here, done] = -dot(inverse, mixed, NN)
        inv[here, here] = inverse
        if j + 1 < PB:
            lmat[under, here] = dot(below, inverse, NTC)
        for act, g in after[j]:
            act(g)

    last = pl.ds(768, 256)
    half[:, last] = dot(mine, inv[last, :], NTC)
    s6(f)
    own = inv.at[pl.ds(pl.multiple_of(lax.rem(c, 8) * TILE, TILE), TILE)]
    for k in range(4):
        here = pl.ds(256 * k, 256)
        weights = dot(half[:, last], inv[last, here], NN)
        if k < 3:
            weights = weights + partial[:, here]
        weights = jnp.concatenate([jnp.where(source, -own[:, here], weights[:TILE]), weights[TILE:]], 0)
        high = weights.astype(BF16)
        wt_hi[:, here] = high
        wt_lo[:, here] = (weights - high.astype(F32)).astype(BF16)

    assemble1()

    top, bottom = list(range(8)), [partner_slot(k) for k in range(8)]

    def finish(g, lo, hi):
        panel, base = panels[g], GROUPS[g][0]
        count = hi - lo
        for h, order in enumerate((top, bottom)):
            rows = jnp.concatenate(
                [panel[s, lo - base : hi - base].reshape(count * 64, TILE) for s in order], 1
            )
            rows_hi = rows.astype(BF16)
            rows_lo = (rows - rows_hi.astype(F32)).astype(BF16)
            update = lax.dot_general(rows_hi, wt_hi[...], NTC, preferred_element_type=F32)
            update += lax.dot_general(rows_lo, wt_hi[...], NTC, preferred_element_type=F32)
            update += lax.dot_general(rows_hi, wt_lo[...], NTC, preferred_element_type=F32)
            for t in range(lo, hi):
                piece = update[64 * (t - lo) : 64 * (t - lo + 1)]
                base0, base1 = sum0[t, pl.ds(64 * h, 64), :], sum1[t, pl.ds(64 * h, 64), :]
                new0 = jnp.where(source, 0.0, base0) - piece[:, :TILE]
                new1 = base1 - piece[:, TILE:]
                if t < 4:
                    i = 8 * t + r
                    new0 = jnp.where(i >= c, new0, base0)
                    new1 = jnp.where(i >= 16 + c, new1, base1)
                out[t, pl.ds(128 * h, 64, stride=2), :] = new0
                out[t, pl.ds(128 * h + 1, 64, stride=2), :] = new1

    def store(piece, lo, hi):
        return pltpu.make_async_copy(
            out.at[pl.ds(lo, hi - lo)], out_any.at[pl.ds(lo, hi - lo)], stored.at[piece]
        )

    block = lmat[
        pl.ds(pl.multiple_of(r * TILE, TILE), TILE), pl.ds(pl.multiple_of(lax.rem(c, 8) * TILE, TILE), TILE)
    ]
    factored = jnp.logical_and(source, r >= c)
    out[0, pl.ds(0, TILE, stride=2), :] = jnp.where(factored, block, sum0[0])
    out[0, pl.ds(1, TILE, stride=2), :] = sum1[0]
    store(0, 0, 1).start()
    for g, (lo, hi, _) in enumerate(GROUPS):
        s7(g)
        finish(g, lo, hi)
        store(1 + g, lo, hi).start()

    @pl.when(source)
    def _():
        for step in range(1, 4):
            dx_copy(step).wait_send()
        for g in range(3):
            spread(g).wait_send()

    for kind in range(3):
        for step in STEPS:
            child_copy(kind, step).wait_send()
    for sx in range(2):
        for step in range(1, 4):
            dz_copy(sx, step).wait_send()
    for spec in started:
        move(*spec).wait_send()
    for q in range(4):
        d_end(q)
    bx_end()
    b_end()
    store(0, 0, 1).wait()
    for g, (lo, hi, _) in enumerate(GROUPS):
        store(1 + g, lo, hi).wait()


def copy_kernel(source, out, buffer, load, store):
    parts = [pl.ds(6 * i, 6) for i in range(4)]
    loads = [pltpu.make_async_copy(source.at[p], buffer.at[p], load.at[i]) for i, p in enumerate(parts)]
    stores = [pltpu.make_async_copy(buffer.at[p], out.at[p], store.at[i]) for i, p in enumerate(parts)]
    for copy in loads:
        copy.start()
    for first, second in zip(loads, stores):
        first.wait()
        second.start()
    for copy in stores:
        copy.wait()


def shards(front, child_one, child_two, map_one, map_two, owner_one, owner_two):
    whole = pl.BlockSpec(memory_space=pl.ANY)
    smem = pl.BlockSpec(memory_space=pltpu.SMEM)
    dma = pltpu.SemaphoreType.DMA

    def space(*shape):
        return pltpu.VMEM(shape, F32)

    out = pl.pallas_call(
        kernel,
        out_shape=jax.ShapeDtypeStruct((NT, 256, TILE), F32),
        in_specs=[whole] * 3 + [smem] * 4,
        out_specs=whole,
        scratch_shapes=[
            space(NT, 256, TILE), space(8, 256, TILE), space(16, 256, TILE),
            space(8, 2, TILE, TILE), space(8, TILE, TILE), space(8, 3, TILE, TILE),
            space(9, 2, TILE, TILE), space(9, TILE, TILE), space(9, 3, TILE, TILE),
            space(NT, TILE, TILE), space(NT, TILE, TILE),
            *[space(16, hi - lo, 64, TILE) for lo, hi, _ in GROUPS],
            space(8, TILE, TILE), space(8, 8, TILE, TILE), space(2, 8, TILE, TILE),
            space(PB * TILE, PB * TILE), space(PB * TILE, PB * TILE),
            space(256, PB * TILE), space(256, 768),
            pltpu.VMEM((256, PB * TILE), BF16), pltpu.VMEM((256, PB * TILE), BF16),
            space(NT, 256, TILE),
            pltpu.SMEM((128,), I32), pltpu.SMEM((32,), I32),
            dma((3,)), dma((3, 7)), dma((3, 7)),
            dma((3,)), dma((3,)), dma((3, 20)), dma((3, 20)),
            dma((3,)), dma((2,)), dma((2, 3)), dma((2, 3)), dma((4, 7)), dma((4, 7)),
            dma((3,)), dma((2, 8)), dma((2, 4)), dma((2, 4)), dma((4,)),
        ],
        compiler_params=pltpu.CompilerParams(
            collective_id=0, has_side_effects=True, vmem_limit_bytes=60 * 2**20
        ),
    )(
        front.reshape(NT, 256, TILE),
        child_one.reshape(8, 256, TILE),
        child_two.reshape(16, 256, TILE),
        map_one, map_two, owner_one, owner_two,
    )
    out = pl.pallas_call(
        copy_kernel,
        out_shape=jax.ShapeDtypeStruct((NT, 256, TILE), F32),
        in_specs=[whole],
        out_specs=whole,
        scratch_shapes=[space(NT, 256, TILE), dma((4,)), dma((4,))],
        compiler_params=pltpu.CompilerParams(vmem_limit_bytes=60 * 2**20),
    )(out)
    return out.reshape(front.shape)


def solution(mesh):
    placed = P(None, "row", None, None, "col", None)
    return jax.shard_map(
        shards,
        mesh=mesh,
        in_specs=(placed, placed, placed, P(), P(), P(), P()),
        out_specs=placed,
        check_vma=False,
    )
```

```python
import functools

import jax
import jax.numpy as jnp
from jax import lax
from jax.experimental import pallas as pl
from jax.experimental.pallas import tpu as pltpu
from jax.sharding import PartitionSpec as P

F32, BF16, I32 = jnp.float32, jnp.bfloat16, jnp.int32
HIGHEST = lax.Precision.HIGHEST
MESH = pl.DeviceIdType.MESH
TILE, PB, NT = 128, 8, 24
LEAF = 16
NN = (((1,), (0,)), ((), ()))
NTC = (((1,), (1,)), ((), ()))
TN = (((0,), (0,)), ((), ()))
GROUPS = ((1, 9, True), (9, 18, False), (18, 24, True))
CHUNKS = ((0, 1), (1, 2), (2, 4), (4, 8))
STEPS = (1, 7, 2, 6, 3, 5, 4)


def dot(a, b, dims):
    return lax.dot_general(a, b, dims, precision=HIGHEST, preferred_element_type=F32)


def split3(v):
    high = v.astype(BF16)
    rest = v - high.astype(F32)
    middle = rest.astype(BF16)
    low = (rest - middle.astype(F32)).astype(BF16)
    return [part.astype(F32) for part in (high, middle, low)]


def rank_update(a, b):
    ah, am, al = split3(a)
    bh, bm, bl = split3(b)
    left = jnp.concatenate([ah, ah, am, ah, am, al], 0).astype(BF16)
    right = jnp.concatenate([bl, bm, bm, bh, bh, bh], 0).astype(BF16)
    return lax.dot_general(left, right, TN, preferred_element_type=F32)


def leaf(rows_u, rows_v, offset):
    count = rows_u.shape[0]
    index = lax.broadcasted_iota(I32, (count, TILE), 0)
    cols = [
        jnp.broadcast_to(rows_u[:, offset + k : offset + k + 1], (count, TILE)) for k in range(count)
    ]
    scale = jnp.zeros((count, TILE), F32)
    for j in range(count):
        pivot = cols[j][j : j + 1, :]
        scale = jnp.where(index == j, lax.rsqrt(pivot), scale)
        if j + 1 < count:
            ratio = cols[j] * (1.0 / pivot)
            for k in range(j + 1, count):
                cols[k] = cols[k] - ratio * cols[k][j : j + 1, :]
            ratio = jnp.where(index > j, ratio, 0.0)
            rows_u = rows_u - ratio * rows_u[j : j + 1, :]
            rows_v = rows_v - ratio * rows_v[j : j + 1, :]
    return rows_u * scale, rows_v * scale


def factor_tile(square):
    row = lax.broadcasted_iota(I32, (TILE, TILE), 0)
    col = lax.broadcasted_iota(I32, (TILE, TILE), 1)
    unit = jnp.where(row == col, 1.0, 0.0).astype(F32)
    count = TILE // LEAF
    left = [square[i * LEAF : (i + 1) * LEAF] for i in range(count)]
    right = [unit[i * LEAF : (i + 1) * LEAF] for i in range(count)]
    for b in range(count):
        left[b], right[b] = leaf(left[b], right[b], b * LEAF)
        if b + 1 < count:
            change = rank_update(left[b], jnp.concatenate([left[b], right[b]], 1))
            for i in range(b + 1, count):
                left[i] = left[i] - change[i * LEAF : (i + 1) * LEAF, :TILE]
                right[i] = right[i] - change[i * LEAF : (i + 1) * LEAF, TILE:]
    upper = jnp.where(col >= row, jnp.concatenate(left, 0), 0.0)
    inverse = jnp.where(col <= row, jnp.concatenate(right, 0), 0.0)
    return upper, inverse


def partner_slot(c):
    return 12 - 4 * (c // 4) + c % 4


def kernel(
    front_in, one_in, two_in, map_one, map_two, own_one, own_two, out_any,
    front, one, two, stage0, stage2, stage1, got0, got2, got1, sum0, sum1,
    panel_a, panel_b, panel_c, dplane, drows, brows, diag, lmat, inv, half, partial, wt_hi, wt_lo, out,
    slots, table,
    load, child_send, child_recv, spread_send, spread_recv, ring_send, ring_recv,
    dx_send, dx_recv, dz_send, dz_recv, d_send, d_recv, bx_send, bx_recv, b_send, b_recv, stored,
):
    r, c = lax.axis_index("row"), lax.axis_index("col")
    y, core = r // 2, r % 2
    x, z = c // 4, c % 4
    source = x < 2
    other = jnp.logical_not(source)
    partner = (3 - x) * 4 + z
    panels = (panel_a, panel_b, panel_c)

    def at_col(dx, dz):
        return lax.rem(x + dx + 4, 4) * 4 + lax.rem(z + dz + 4, 4)

    def row_peer(step):
        return lax.rem(r + step, 8)

    def y_peer(step, across=0):
        return lax.rem(y + step, 4) * 2 + (core if across == 0 else 1 - core)

    barrier = pltpu.get_barrier_semaphore()
    for step in range(1, 8):
        pl.semaphore_signal(barrier, inc=1, device_id=(row_peer(step), c), device_id_type=MESH)
    for step in range(1, 4):
        pl.semaphore_signal(barrier, inc=1, device_id=(r, at_col(step, 0)), device_id_type=MESH)
        pl.semaphore_signal(barrier, inc=1, device_id=(r, at_col(0, step)), device_id_type=MESH)

    @pl.when(lax.rem(c, 8) == r)
    def _():
        for held in range(8):

            @pl.when(c != held)
            def _():
                pl.semaphore_signal(barrier, inc=1, device_id=(r, held), device_id_type=MESH)

    loads = [
        pltpu.make_async_copy(a, b, load.at[i])
        for i, (a, b) in enumerate(((one_in, one), (two_in, two), (front_in, front)))
    ]
    for copy in loads:
        copy.start()

    def find_one(g, carry):
        seen, picks = carry[0], list(carry[1:])
        for v in range(8):
            mine = own_one[8 * g + v] == r
            picks[v] = jnp.where(mine, seen, picks[v])
            seen = seen + mine.astype(I32)
        return (seen, *picks)

    picks_one = lax.fori_loop(0, 8, find_one, (jnp.int32(0),) * 9)[1:]

    def find_two(g, carry):
        seen, first, second = carry[0], list(carry[1:9]), list(carry[9:])
        for v in range(8):
            mine = own_two[8 * g + v] == r
            first[v] = jnp.where(mine, second[v], first[v])
            second[v] = jnp.where(mine, seen, second[v])
            seen = seen + mine.astype(I32)
        return (seen, *first, *second)

    picks_two = lax.fori_loop(0, 16, find_two, (jnp.int32(0),) * 17)[1:]
    for v in range(8):
        slots[v] = jnp.minimum(picks_one[v], 7)
        slots[8 + v] = jnp.minimum(picks_two[v], 15)
        slots[16 + v] = jnp.minimum(picks_two[8 + v], 15)

    def stage0_rows(v, carry):
        pick = pl.ds(0, TILE, stride=2)
        stage0[v, 0] = one[slots[v], pick, :]
        stage0[v, 1] = two[slots[8 + v], pick, :]
        stage2[v] = two[slots[16 + v], pick, :]
        return carry

    def stage1_rows(v, carry):
        pick = pl.ds(1, TILE, stride=2)
        stage1[v, 0] = one[slots[v], pick, :]
        stage1[v, 1] = two[slots[8 + v], pick, :]
        stage1[v, 2] = two[slots[16 + v], pick, :]
        return carry

    def child_copy(kind, step):
        peer = row_peer(step)
        return pltpu.make_async_remote_copy(
            src_ref=(stage0, stage1, stage2)[kind].at[peer],
            dst_ref=(got0, got1, got2)[kind].at[r],
            send_sem=child_send.at[kind, step - 1],
            recv_sem=child_recv.at[kind, step - 1],
            device_id=(peer, c),
            device_id_type=MESH,
        )

    loads[0].wait()
    loads[1].wait()
    lax.fori_loop(0, 8, stage0_rows, 0)
    pl.semaphore_wait(
        barrier, 13 + source.astype(I32) + jnp.logical_and(source, c != r).astype(I32)
    )
    for kind in (0, 2):
        for step in STEPS:
            child_copy(kind, step).start()
    lax.fori_loop(0, 8, stage1_rows, 0)
    for buffer, staged in ((got0, stage0), (got1, stage1), (got2, stage2)):
        buffer[r] = staged[r]
        buffer[8] = jnp.zeros(buffer.shape[1:], F32)

    sources = [own_two[8 * g + r] for g in range(16)]
    for g in range(16):
        rank = jnp.int32(0)
        for h in range(g):
            rank = rank + (sources[h] == sources[g]).astype(I32)
        table[g] = jnp.clip(sources[g], 0, 7)
        table[16 + g] = jnp.minimum(rank, 1)

    def find_targets(t, carry):
        at_one, at_two = carry
        hit_one = map_one[8 * at_one] // 8 == t
        hit_two = map_two[8 * at_two] // 8 == t
        slots[32 + t] = jnp.where(hit_one, jnp.clip(own_one[8 * at_one + r], 0, 7), 8)
        slots[64 + t] = jnp.where(hit_two, table[at_two], 8)
        slots[96 + t] = jnp.where(hit_two, table[16 + at_two] + 1, 1)
        return (
            jnp.minimum(at_one + hit_one.astype(I32), 7),
            jnp.minimum(at_two + hit_two.astype(I32), 15),
        )

    lax.fori_loop(0, NT, find_targets, (jnp.int32(0), jnp.int32(0)))
    loads[2].wait()

    def assemble0():
        for step in STEPS:
            child_copy(2, step).wait_recv()

        def body(t, carry):
            origin, second = slots[64 + t], slots[96 + t] == 2
            total = front[t, pl.ds(0, TILE, stride=2), :] + got0[slots[32 + t], 0]
            total = total + got0[jnp.where(second, 8, origin), 1]
            sum0[t] = total + got2[jnp.where(second, origin, 8)]
            return carry

        lax.fori_loop(0, NT, body, 0)

    def assemble1():
        for step in STEPS:
            child_copy(1, step).wait_recv()

        def body(t, carry):
            sum1[t] = (
                front[t, pl.ds(1, TILE, stride=2), :] + got1[slots[32 + t], 0]
            ) + got1[slots[64 + t], slots[96 + t]]
            return carry

        lax.fori_loop(0, NT, body, 0)

    def dx_copy(step):
        held = lax.rem(c, 8)
        return pltpu.make_async_remote_copy(
            src_ref=dplane.at[held],
            dst_ref=dplane.at[held],
            send_sem=dx_send.at[step - 1],
            recv_sem=dx_recv.at[lax.rem(x, 2)],
            device_id=(r, at_col(step, 0)),
            device_id_type=MESH,
        )

    def dx_arrival(sx):
        held = 4 * sx + z
        return pltpu.make_async_remote_copy(
            src_ref=dplane.at[held],
            dst_ref=dplane.at[held],
            send_sem=dx_send.at[0],
            recv_sem=dx_recv.at[sx],
            device_id=(r, at_col(1, 0)),
            device_id_type=MESH,
        )

    def dz_copy(sx, step, back=0):
        held = 4 * sx + lax.rem(z + 4 - back, 4)
        return pltpu.make_async_remote_copy(
            src_ref=dplane.at[held],
            dst_ref=dplane.at[held],
            send_sem=dz_send.at[sx, step - 1],
            recv_sem=dz_recv.at[sx, step - 1],
            device_id=(r, at_col(0, step)),
            device_id_type=MESH,
        )

    for step in STEPS:
        child_copy(0, step).wait_recv()

    @pl.when(source)
    def _():
        total = front[0, pl.ds(0, TILE, stride=2), :] + got0[jnp.clip(own_one[r], 0, 7), 0]
        dplane[lax.rem(c, 8)] = total + got0[jnp.clip(own_two[r], 0, 7), 1]
        for step in (1, 3, 2):
            dx_copy(step).start()

    for sx in range(2):

        @pl.when(x != sx)
        def _():
            dx_arrival(sx).wait_recv()

        for step in (1, 3, 2):
            dz_copy(sx, step).start()
    def d_out(q, step):
        lo, hi = CHUNKS[q]
        return pltpu.make_async_remote_copy(
            src_ref=dplane.at[pl.ds(lo, hi - lo)],
            dst_ref=drows.at[r, pl.ds(lo, hi - lo)],
            send_sem=d_send.at[q, step - 1],
            recv_sem=d_recv.at[q, step - 1],
            device_id=(y_peer(step), c),
            device_id_type=MESH,
        )

    def d_pair(q, step):
        lo, hi = CHUNKS[q]
        held = y_peer(step)
        return pltpu.make_async_remote_copy(
            src_ref=dplane.at[pl.ds(lo, hi - lo)] if step == 0 else drows.at[held, pl.ds(lo, hi - lo)],
            dst_ref=drows.at[held, pl.ds(lo, hi - lo)],
            send_sem=d_send.at[q, 3 + step],
            recv_sem=d_recv.at[q, 3 + step],
            device_id=(y_peer(0, 1), c),
            device_id_type=MESH,
        )

    def d_start(q):
        @pl.when(r >= CHUNKS[q][0])
        def _():
            for step in (1, 3, 2):
                d_out(q, step).start()
            d_pair(q, 0).start()

    def d_relay(q):
        for step in (1, 3, 2):

            @pl.when(y_peer(4 - step) >= CHUNKS[q][0])
            def _():
                d_out(q, step).wait_recv()
                d_pair(q, 4 - step).start()

    def d_wait(q):
        for step in range(4):

            @pl.when(y_peer(step, 1) >= CHUNKS[q][0])
            def _():
                d_pair(q, step).wait_recv()

    def d_end(q):
        @pl.when(r >= CHUNKS[q][0])
        def _():
            for step in (1, 3, 2):
                d_out(q, step).wait_send()
            d_pair(q, 0).wait_send()

        for step in (1, 3, 2):

            @pl.when(y_peer(4 - step) >= CHUNKS[q][0])
            def _():
                d_pair(q, 4 - step).wait_send()

    assemble0()

    @pl.when(source)
    def _():
        for g in range(3):
            lo, hi, _ = GROUPS[g]
            panels[g][c] = sum0[lo:hi, :64, :]

    def spread(g):
        lo, hi, _ = GROUPS[g]
        return pltpu.make_async_remote_copy(
            src_ref=sum0.at[pl.ds(lo, hi - lo), pl.ds(64, 64)],
            dst_ref=panels[g].at[partner],
            send_sem=spread_send.at[g],
            recv_sem=spread_recv.at[g],
            device_id=(r, partner),
            device_id_type=MESH,
        )

    def part(slot, g, half):
        lo, hi, _ = GROUPS[g]
        count, panel = hi - lo, panels[g]
        upper = (count + 1) // 2
        if half is None:
            return panel.at[slot]
        return panel.at[slot, pl.ds(0, upper)] if half == 0 else panel.at[slot, pl.ds(upper, count - upper)]

    def move(g, axis, da, db, direction, half, index):
        x_first = GROUPS[g][2]
        offset = (da, db) if x_first else (db, da)
        along = (direction, 0) if (axis == 0) == x_first else (0, direction)
        ref = part(at_col(*offset), g, half)
        return pltpu.make_async_remote_copy(
            src_ref=ref,
            dst_ref=ref,
            send_sem=ring_send.at[g, index],
            recv_sem=ring_recv.at[g, index],
            device_id=(r, at_col(*along)),
            device_id_type=MESH,
        )

    def wait(spec):
        g, axis, da, db, direction, half, index = spec
        back = (da - direction, db) if axis == 0 else (da, db - direction)
        move(g, axis, back[0], back[1], direction, half, index).wait_recv()

    def first(g, k):
        return (g, 0, 0, 0, (1, -1)[k], None, k)

    def first_on(g, k):
        return (g, 0, (-1, 1)[k], 0, (1, -1)[k], k, 2 + k)

    def second(g, q, k):
        return (g, 1, (0, -1, 1, 2)[q], 0, (1, -1)[k], None, 4 + 4 * q + k)

    def second_on(g, q, k):
        return (g, 1, (0, -1, 1, 2)[q], (-1, 1)[k], (1, -1)[k], k, 6 + 4 * q + k)

    started = []

    def start(spec):
        started.append(spec)
        move(*spec).start()

    def own_blocks(g):
        return [first(g, 0), first(g, 1), second(g, 0, 0), second(g, 0, 1)]

    def s1(g):
        @pl.when(other)
        def _():
            spread(g).wait_recv()
            for spec in own_blocks(g):
                move(*spec).start()

    def s2(g):
        for k in range(2):
            wait(first(g, k))
            start(first_on(g, k))
        for q in (1, 2):
            for k in range(2):
                start(second(g, q, k))

    def s3(g):
        for k in range(2):
            wait(second(g, 0, k))
            start(second_on(g, 0, k))

    def s4(g):
        for k in range(2):
            wait(first_on(g, k))
        for k in range(2):
            start(second(g, 3, k))

    def s5a(g):
        for k in range(2):
            wait(second(g, 1, k))
            start(second_on(g, 1, k))

    def s5b(g):
        for k in range(2):
            wait(second(g, 2, k))
            start(second_on(g, 2, k))

    def s6(g):
        for k in range(2):
            wait(second(g, 3, k))
            start(second_on(g, 3, k))

    def s7(g):
        for q in range(4):
            for k in range(2):
                wait(second_on(g, q, k))

    b_row = lax.rem(c, 8)
    b_y, b_core = b_row // 2, b_row % 2
    b_root, b_even = r == b_row, core == b_core

    def bx_copy(q, t, target):
        held = lax.rem(c, 8)
        return pltpu.make_async_remote_copy(
            src_ref=sum0.at[t],
            dst_ref=brows.at[q, held],
            send_sem=bx_send.at[t - 1],
            recv_sem=bx_recv.at[q, held],
            device_id=(r, target),
            device_id_type=MESH,
        )

    def bx_arrival(q, held):
        return pltpu.make_async_remote_copy(
            src_ref=sum0.at[1],
            dst_ref=brows.at[q, held],
            send_sem=bx_send.at[0],
            recv_sem=bx_recv.at[q, held],
            device_id=(r, at_col(1, 0)),
            device_id_type=MESH,
        )

    def bx_start():
        @pl.when(source)
        def _():
            bx_copy(0, 1, r + 8).start()
            bx_copy(1, 3, r + 8).start()

        @pl.when(jnp.logical_and(source, c != r))
        def _():
            bx_copy(1, 2, r).start()

        @pl.when(jnp.logical_and(source, c == r))
        def _():
            brows[1, r] = sum0[2]

    def bx_end():
        @pl.when(source)
        def _():
            bx_copy(0, 1, r + 8).wait_send()
            bx_copy(1, 3, r + 8).wait_send()

        @pl.when(jnp.logical_and(source, c != r))
        def _():
            bx_copy(1, 2, r).wait_send()

    def b_out(q, step):
        return pltpu.make_async_remote_copy(
            src_ref=brows.at[q],
            dst_ref=brows.at[q],
            send_sem=b_send.at[q, step - 1],
            recv_sem=b_recv.at[q, step - 1],
            device_id=(y_peer(step), c),
            device_id_type=MESH,
        )

    def b_pair(q):
        return pltpu.make_async_remote_copy(
            src_ref=brows.at[q],
            dst_ref=brows.at[q],
            send_sem=b_send.at[q, 3],
            recv_sem=b_recv.at[q, 3],
            device_id=(y_peer(0, 1), c),
            device_id_type=MESH,
        )

    def with_b(q, condition):
        return condition if q == 1 else jnp.logical_and(condition, other)

    def b_start(_):
        for q in (1, 0):

            @pl.when(with_b(q, b_root))
            def _():
                for held in range(8):

                    @pl.when(c != held)
                    def _():
                        bx_arrival(q, held).wait_recv()

                for step in (1, 3, 2):
                    b_out(q, step).start()
                b_pair(q).start()

    def b_relay(_):
        for q in (1, 0):
            for step in (1, 2, 3):

                @pl.when(with_b(q, jnp.logical_and(b_even, lax.rem(b_y + step, 4) == y)))
                def _():
                    b_out(q, step).wait_recv()
                    b_pair(q).start()

    def b_wait(_):
        for q in (1, 0):

            @pl.when(with_b(q, jnp.logical_not(b_even)))
            def _():
                b_pair(q).wait_recv()

    def b_end():
        for q in (1, 0):

            @pl.when(with_b(q, b_root))
            def _():
                for step in (1, 2, 3):
                    b_out(q, step).wait_send()

            @pl.when(with_b(q, b_even))
            def _():
                b_pair(q).wait_send()

    def child1(_):
        for step in STEPS:
            child_copy(1, step).start()

    bx_start()
    for g in range(3):

        @pl.when(source)
        def _():
            spread(g).start()

    for g in range(3):
        started.extend(own_blocks(g))

    def s0(g):
        @pl.when(source)
        def _():
            for spec in own_blocks(g):
                move(*spec).start()

    s0(0)

    for step in (1, 3, 2):
        dz_copy(0, step, step).wait_recv()
    d_start(0)
    d_start(1)
    for step in (1, 3, 2):
        dz_copy(1, step, step).wait_recv()
    drows[r] = dplane[...]
    d_relay(0)
    d_start(2)
    d_wait(0)

    row = lax.broadcasted_iota(I32, (TILE, TILE), 0)
    col = lax.broadcasted_iota(I32, (TILE, TILE), 1)
    inv[...] = jnp.zeros_like(inv)

    b, e, f = 0, 1, 2
    before = {
        0: [(s0, e), (s1, b)],
        1: [(s0, f)],
        2: [(s3, b)],
        3: [],
        4: [(s2, f), (s3, e)],
        5: [(s4, e), (s5a, b), (b_relay, 0)],
        6: [(s4, f)],
        7: [(s6, e)],
    }
    after = {
        0: [(d_relay, 1), (d_wait, 1), (d_start, 3), (s1, e)],
        1: [(d_relay, 2), (d_wait, 2), (s1, f), (s2, b), (b_start, 0)],
        2: [(s2, e), (d_relay, 3)],
        3: [(s4, b), (d_wait, 3), (child1, 0)],
        4: [(s5b, b)],
        5: [(s5b, e), (s3, f)],
        6: [(s5a, e), (s6, b), (b_wait, 0)],
        7: [(s5a, f), (s5b, f)],
    }

    def window_rows():
        unused = jnp.zeros((TILE, TILE), F32)
        return jnp.concatenate(
            [
                jnp.concatenate([jnp.where(source, unused, brows[0, s]) for s in range(8)], 1),
                jnp.concatenate([brows[1, s] for s in range(8)], 1),
            ],
            0,
        )

    def step_tile(k, carry):
        for j in range(PB):

            @pl.when(k == j)
            def _():
                for act, g in before[j]:
                    act(g)
                here, done = pl.ds(j * TILE, TILE), pl.ds(0, j * TILE)
                under = pl.ds((j + 1) * TILE, (PB - 1 - j) * TILE)
                square = drows[j, j]
                square = jnp.where(row >= col, square, 0.0) + jnp.where(row > col, square, 0.0).T
                if j > 0:
                    left = lmat[here, done]
                    square = square - dot(left, left, NTC)
                    inv[here, done] = dot(left, inv[done, done], NN)
                diag[...] = square
                if j + 1 < PB:
                    below = jnp.concatenate([drows[i, j] for i in range(j + 1, PB)], 0)
                    if j > 0:
                        below = below - dot(lmat[under, done], left, NTC)
                    lmat[under, here] = below
                else:
                    mine = window_rows()
                    for i in range(3):
                        here_i, upto = pl.ds(256 * i, 256), 256 * (i + 1)
                        half[:, here_i] = dot(mine[:, :upto], inv[here_i, :upto], NTC)
                    for i in range(3):
                        here_i, rest = pl.ds(256 * i, 256), pl.ds(256 * i, 768 - 256 * i)
                        partial[:, here_i] = dot(half[:, rest], inv[rest, here_i], NN)

        upper, inverse = factor_tile(diag[...])
        diag[...] = inverse
        lower = upper.T
        for j in range(PB):

            @pl.when(k == j)
            def _():
                here, done = pl.ds(j * TILE, TILE), pl.ds(0, j * TILE)
                under = pl.ds((j + 1) * TILE, (PB - 1 - j) * TILE)
                inverse = diag[...]
                lmat[here, here] = lower
                if j > 0:
                    inv[here, done] = -dot(inverse, inv[here, done], NN)
                inv[here, here] = inverse
                if j + 1 < PB:
                    lmat[under, here] = dot(lmat[under, here], inverse, NTC)
                for act, g in after[j]:
                    act(g)

        return carry

    lax.fori_loop(0, PB, step_tile, 0)
    mine = window_rows()

    last = pl.ds(768, 256)
    half[:, last] = dot(mine, inv[last, :], NTC)
    s6(f)
    own = inv.at[pl.ds(pl.multiple_of(lax.rem(c, 8) * TILE, TILE), TILE)]
    for k in range(4):
        here = pl.ds(256 * k, 256)
        weights = dot(half[:, last], inv[last, here], NN)
        if k < 3:
            weights = weights + partial[:, here]
        weights = jnp.concatenate([jnp.where(source, -own[:, here], weights[:TILE]), weights[TILE:]], 0)
        high = weights.astype(BF16)
        wt_hi[:, here] = high
        wt_lo[:, here] = (weights - high.astype(F32)).astype(BF16)

    assemble1()

    def finish(g, lo, hi):
        panel = panels[g]
        count = hi - lo

        def half_rows(h, carry):
            order = [k + h * (partner_slot(k) - k) for k in range(8)]
            rows = jnp.concatenate([panel[s].reshape(count * 64, TILE) for s in order], 1)
            rows_hi = rows.astype(BF16)
            rows_lo = (rows - rows_hi.astype(F32)).astype(BF16)
            update = lax.dot_general(rows_hi, wt_hi[...], NTC, preferred_element_type=F32)
            update += lax.dot_general(rows_lo, wt_hi[...], NTC, preferred_element_type=F32)
            update += lax.dot_general(rows_hi, wt_lo[...], NTC, preferred_element_type=F32)
            for t in range(lo, hi):
                piece = update[64 * (t - lo) : 64 * (t - lo + 1)]
                rows_here = pl.ds(pl.multiple_of(64 * h, 64), 64)
                base0, base1 = sum0[t, rows_here, :], sum1[t, rows_here, :]
                new0 = jnp.where(source, 0.0, base0) - piece[:, :TILE]
                new1 = base1 - piece[:, TILE:]
                if t < 4:
                    i = 8 * t + r
                    new0 = jnp.where(i >= c, new0, base0)
                    new1 = jnp.where(i >= 16 + c, new1, base1)
                out[t, pl.ds(pl.multiple_of(128 * h, 128), 64, stride=2), :] = new0
                out[t, pl.ds(128 * h + 1, 64, stride=2), :] = new1
            return carry

        lax.fori_loop(0, 2, half_rows, 0)

    def store(piece, lo, hi):
        return pltpu.make_async_copy(
            out.at[pl.ds(lo, hi - lo)], out_any.at[pl.ds(lo, hi - lo)], stored.at[piece]
        )

    block = lmat[
        pl.ds(pl.multiple_of(r * TILE, TILE), TILE), pl.ds(pl.multiple_of(lax.rem(c, 8) * TILE, TILE), TILE)
    ]
    factored = jnp.logical_and(source, r >= c)
    out[0, pl.ds(0, TILE, stride=2), :] = jnp.where(factored, block, sum0[0])
    out[0, pl.ds(1, TILE, stride=2), :] = sum1[0]
    store(0, 0, 1).start()
    for g, (lo, hi, _) in enumerate(GROUPS):
        s7(g)
        finish(g, lo, hi)
        store(1 + g, lo, hi).start()

    @pl.when(source)
    def _():
        for step in range(1, 4):
            dx_copy(step).wait_send()
        for g in range(3):
            spread(g).wait_send()

    for kind in range(3):
        for step in STEPS:
            child_copy(kind, step).wait_send()
    for sx in range(2):
        for step in range(1, 4):
            dz_copy(sx, step).wait_send()
    for spec in started:
        move(*spec).wait_send()
    for q in range(4):
        d_end(q)
    bx_end()
    b_end()
    store(0, 0, 1).wait()
    for g, (lo, hi, _) in enumerate(GROUPS):
        store(1 + g, lo, hi).wait()


def copy_kernel(source, out, buffer, load, store):
    parts = [pl.ds(6 * i, 6) for i in range(4)]
    loads = [pltpu.make_async_copy(source.at[p], buffer.at[p], load.at[i]) for i, p in enumerate(parts)]
    stores = [pltpu.make_async_copy(buffer.at[p], out.at[p], store.at[i]) for i, p in enumerate(parts)]
    for copy in loads:
        copy.start()
    for first, second in zip(loads, stores):
        first.wait()
        second.start()
    for copy in stores:
        copy.wait()


def shards(front, child_one, child_two, map_one, map_two, owner_one, owner_two):
    whole = pl.BlockSpec(memory_space=pl.ANY)
    smem = pl.BlockSpec(memory_space=pltpu.SMEM)
    dma = pltpu.SemaphoreType.DMA

    def space(*shape):
        return pltpu.VMEM(shape, F32)

    out = pl.pallas_call(
        kernel,
        out_shape=jax.ShapeDtypeStruct((NT, 256, TILE), F32),
        in_specs=[whole] * 3 + [smem] * 4,
        out_specs=whole,
        scratch_shapes=[
            space(NT, 256, TILE), space(8, 256, TILE), space(16, 256, TILE),
            space(8, 2, TILE, TILE), space(8, TILE, TILE), space(8, 3, TILE, TILE),
            space(9, 2, TILE, TILE), space(9, TILE, TILE), space(9, 3, TILE, TILE),
            space(NT, TILE, TILE), space(NT, TILE, TILE),
            *[space(16, hi - lo, 64, TILE) for lo, hi, _ in GROUPS],
            space(8, TILE, TILE), space(8, 8, TILE, TILE), space(2, 8, TILE, TILE),
            space(TILE, TILE), space(PB * TILE, PB * TILE), space(PB * TILE, PB * TILE),
            space(256, PB * TILE), space(256, 768),
            pltpu.VMEM((256, PB * TILE), BF16), pltpu.VMEM((256, PB * TILE), BF16),
            space(NT, 256, TILE),
            pltpu.SMEM((128,), I32), pltpu.SMEM((32,), I32),
            dma((3,)), dma((3, 7)), dma((3, 7)),
            dma((3,)), dma((3,)), dma((3, 20)), dma((3, 20)),
            dma((3,)), dma((2,)), dma((2, 3)), dma((2, 3)), dma((4, 7)), dma((4, 7)),
            dma((3,)), dma((2, 8)), dma((2, 4)), dma((2, 4)), dma((4,)),
        ],
        compiler_params=pltpu.CompilerParams(
            collective_id=0, has_side_effects=True, vmem_limit_bytes=60 * 2**20
        ),
    )(
        front.reshape(NT, 256, TILE),
        child_one.reshape(8, 256, TILE),
        child_two.reshape(16, 256, TILE),
        map_one, map_two, owner_one, owner_two,
    )
    out = pl.pallas_call(
        copy_kernel,
        out_shape=jax.ShapeDtypeStruct((NT, 256, TILE), F32),
        in_specs=[whole],
        out_specs=whole,
        scratch_shapes=[space(NT, 256, TILE), dma((4,)), dma((4,))],
        compiler_params=pltpu.CompilerParams(vmem_limit_bytes=60 * 2**20),
    )(out)
    return out.reshape(front.shape)


def solution(mesh):
    placed = P(None, "row", None, None, "col", None)
    return jax.shard_map(
        shards,
        mesh=mesh,
        in_specs=(placed, placed, placed, P(), P(), P(), P()),
        out_specs=placed,
        check_vma=False,
    )
```

```python
import functools

import jax
import jax.numpy as jnp
from jax import lax
from jax.experimental import pallas as pl
from jax.experimental.pallas import tpu as pltpu
from jax.sharding import PartitionSpec as P

F32, BF16, I32 = jnp.float32, jnp.bfloat16, jnp.int32
HIGHEST = lax.Precision.HIGHEST
MESH = pl.DeviceIdType.MESH
TILE, PB, NT = 128, 8, 24
LEAF = 16
NN = (((1,), (0,)), ((), ()))
NTC = (((1,), (1,)), ((), ()))
TN = (((0,), (0,)), ((), ()))
GROUPS = ((1, 9, True), (9, 18, False), (18, 24, True))
CHUNKS = ((0, 1), (1, 2), (2, 4), (4, 8))
STEPS = (1, 7, 2, 6, 3, 5, 4)


def dot(a, b, dims):
    return lax.dot_general(a, b, dims, precision=HIGHEST, preferred_element_type=F32)


def split3(v):
    high = v.astype(BF16)
    rest = v - high.astype(F32)
    middle = rest.astype(BF16)
    low = (rest - middle.astype(F32)).astype(BF16)
    return [part.astype(F32) for part in (high, middle, low)]


def rank_update(a, b):
    ah, am, al = split3(a)
    bh, bm, bl = split3(b)
    left = jnp.concatenate([ah, ah, am, ah, am, al], 0).astype(BF16)
    right = jnp.concatenate([bl, bm, bm, bh, bh, bh], 0).astype(BF16)
    return lax.dot_general(left, right, TN, preferred_element_type=F32)


def leaf(rows_u, rows_v, offset):
    count = rows_u.shape[0]
    index = lax.broadcasted_iota(I32, (count, TILE), 0)
    cols = [
        jnp.broadcast_to(rows_u[:, offset + k : offset + k + 1], (count, TILE)) for k in range(count)
    ]
    scale = jnp.zeros((count, TILE), F32)
    for j in range(count):
        pivot = cols[j][j : j + 1, :]
        scale = jnp.where(index == j, lax.rsqrt(pivot), scale)
        if j + 1 < count:
            ratio = cols[j] * (1.0 / pivot)
            for k in range(j + 1, count):
                cols[k] = cols[k] - ratio * cols[k][j : j + 1, :]
            ratio = jnp.where(index > j, ratio, 0.0)
            rows_u = rows_u - ratio * rows_u[j : j + 1, :]
            rows_v = rows_v - ratio * rows_v[j : j + 1, :]
    return rows_u * scale, rows_v * scale


def factor_tile(square):
    row = lax.broadcasted_iota(I32, (TILE, TILE), 0)
    col = lax.broadcasted_iota(I32, (TILE, TILE), 1)
    unit = jnp.where(row == col, 1.0, 0.0).astype(F32)
    count = TILE // LEAF
    left = [square[i * LEAF : (i + 1) * LEAF] for i in range(count)]
    right = [unit[i * LEAF : (i + 1) * LEAF] for i in range(count)]
    for b in range(count):
        left[b], right[b] = leaf(left[b], right[b], b * LEAF)
        if b + 1 < count:
            change = rank_update(left[b], jnp.concatenate([left[b], right[b]], 1))
            for i in range(b + 1, count):
                left[i] = left[i] - change[i * LEAF : (i + 1) * LEAF, :TILE]
                right[i] = right[i] - change[i * LEAF : (i + 1) * LEAF, TILE:]
    upper = jnp.where(col >= row, jnp.concatenate(left, 0), 0.0)
    inverse = jnp.where(col <= row, jnp.concatenate(right, 0), 0.0)
    return upper, inverse


def partner_slot(c):
    return 12 - 4 * (c // 4) + c % 4


def kernel(
    front_in, one_in, two_in, map_one, map_two, own_one, own_two, out_any,
    front, one, two, stage0, stage2, stage1, got0, got2, got1, sum0, sum1,
    panel_a, panel_b, panel_c, dplane, drows, brows, diag, lmat, inv, half, partial, wt_hi, wt_lo, out,
    slots, table,
    load, child_send, child_recv, spread_send, spread_recv, ring_send, ring_recv,
    dx_send, dx_recv, dz_send, dz_recv, d_send, d_recv, bx_send, bx_recv, b_send, b_recv, stored,
):
    r, c = lax.axis_index("row"), lax.axis_index("col")
    y, core = r // 2, r % 2
    x, z = c // 4, c % 4
    source = x < 2
    other = jnp.logical_not(source)
    partner = (3 - x) * 4 + z
    panels = (panel_a, panel_b, panel_c)

    def at_col(dx, dz):
        return lax.rem(x + dx + 4, 4) * 4 + lax.rem(z + dz + 4, 4)

    def row_peer(step):
        return lax.rem(r + step, 8)

    def y_peer(step, across=0):
        return lax.rem(y + step, 4) * 2 + (core if across == 0 else 1 - core)

    barrier = pltpu.get_barrier_semaphore()
    for step in range(1, 8):
        pl.semaphore_signal(barrier, inc=1, device_id=(row_peer(step), c), device_id_type=MESH)
    for step in range(1, 4):
        pl.semaphore_signal(barrier, inc=1, device_id=(r, at_col(step, 0)), device_id_type=MESH)
        pl.semaphore_signal(barrier, inc=1, device_id=(r, at_col(0, step)), device_id_type=MESH)

    @pl.when(lax.rem(c, 8) == r)
    def _():
        for held in range(8):

            @pl.when(c != held)
            def _():
                pl.semaphore_signal(barrier, inc=1, device_id=(r, held), device_id_type=MESH)

    loads = [
        pltpu.make_async_copy(a, b, load.at[i])
        for i, (a, b) in enumerate(((one_in, one), (two_in, two), (front_in, front)))
    ]
    for copy in loads:
        copy.start()

    def find_one(g, carry):
        seen, picks = carry[0], list(carry[1:])
        for v in range(8):
            mine = own_one[8 * g + v] == r
            picks[v] = jnp.where(mine, seen, picks[v])
            seen = seen + mine.astype(I32)
        return (seen, *picks)

    picks_one = lax.fori_loop(0, 8, find_one, (jnp.int32(0),) * 9)[1:]

    def find_two(g, carry):
        seen, first, second = carry[0], list(carry[1:9]), list(carry[9:])
        for v in range(8):
            mine = own_two[8 * g + v] == r
            first[v] = jnp.where(mine, second[v], first[v])
            second[v] = jnp.where(mine, seen, second[v])
            seen = seen + mine.astype(I32)
        return (seen, *first, *second)

    picks_two = lax.fori_loop(0, 16, find_two, (jnp.int32(0),) * 17)[1:]
    for v in range(8):
        slots[v] = jnp.minimum(picks_one[v], 7)
        slots[8 + v] = jnp.minimum(picks_two[v], 15)
        slots[16 + v] = jnp.minimum(picks_two[8 + v], 15)

    def stage0_rows(v, carry):
        pick = pl.ds(0, TILE, stride=2)
        stage0[v, 0] = one[slots[v], pick, :]
        stage0[v, 1] = two[slots[8 + v], pick, :]
        stage2[v] = two[slots[16 + v], pick, :]
        return carry

    def stage1_rows(v, carry):
        pick = pl.ds(1, TILE, stride=2)
        stage1[v, 0] = one[slots[v], pick, :]
        stage1[v, 1] = two[slots[8 + v], pick, :]
        stage1[v, 2] = two[slots[16 + v], pick, :]
        return carry

    def child_copy(kind, step):
        peer = row_peer(step)
        return pltpu.make_async_remote_copy(
            src_ref=(stage0, stage1, stage2)[kind].at[peer],
            dst_ref=(got0, got1, got2)[kind].at[r],
            send_sem=child_send.at[kind, step - 1],
            recv_sem=child_recv.at[kind, step - 1],
            device_id=(peer, c),
            device_id_type=MESH,
        )

    loads[0].wait()
    loads[1].wait()
    lax.fori_loop(0, 8, stage0_rows, 0)
    pl.semaphore_wait(
        barrier, 13 + source.astype(I32) + jnp.logical_and(source, c != r).astype(I32)
    )
    for kind in (0, 2):
        for step in STEPS:
            child_copy(kind, step).start()
    lax.fori_loop(0, 8, stage1_rows, 0)
    for buffer, staged in ((got0, stage0), (got1, stage1), (got2, stage2)):
        buffer[r] = staged[r]
        buffer[8] = jnp.zeros(buffer.shape[1:], F32)

    sources = [own_two[8 * g + r] for g in range(16)]
    for g in range(16):
        rank = jnp.int32(0)
        for h in range(g):
            rank = rank + (sources[h] == sources[g]).astype(I32)
        table[g] = jnp.clip(sources[g], 0, 7)
        table[16 + g] = jnp.minimum(rank, 1)

    def find_targets(t, carry):
        at_one, at_two = carry
        hit_one = map_one[8 * at_one] // 8 == t
        hit_two = map_two[8 * at_two] // 8 == t
        slots[32 + t] = jnp.where(hit_one, jnp.clip(own_one[8 * at_one + r], 0, 7), 8)
        slots[64 + t] = jnp.where(hit_two, table[at_two], 8)
        slots[96 + t] = jnp.where(hit_two, table[16 + at_two] + 1, 1)
        return (
            jnp.minimum(at_one + hit_one.astype(I32), 7),
            jnp.minimum(at_two + hit_two.astype(I32), 15),
        )

    lax.fori_loop(0, NT, find_targets, (jnp.int32(0), jnp.int32(0)))
    loads[2].wait()

    def assemble0():
        for step in STEPS:
            child_copy(2, step).wait_recv()

        def body(t, carry):
            origin, second = slots[64 + t], slots[96 + t] == 2
            total = front[t, pl.ds(0, TILE, stride=2), :] + got0[slots[32 + t], 0]
            total = total + got0[jnp.where(second, 8, origin), 1]
            sum0[t] = total + got2[jnp.where(second, origin, 8)]
            return carry

        lax.fori_loop(0, NT, body, 0)

    def assemble1():
        for step in STEPS:
            child_copy(1, step).wait_recv()

        def body(t, carry):
            sum1[t] = (
                front[t, pl.ds(1, TILE, stride=2), :] + got1[slots[32 + t], 0]
            ) + got1[slots[64 + t], slots[96 + t]]
            return carry

        lax.fori_loop(0, NT, body, 0)

    def dx_copy(step):
        held = lax.rem(c, 8)
        return pltpu.make_async_remote_copy(
            src_ref=dplane.at[held],
            dst_ref=dplane.at[held],
            send_sem=dx_send.at[step - 1],
            recv_sem=dx_recv.at[lax.rem(x, 2)],
            device_id=(r, at_col(step, 0)),
            device_id_type=MESH,
        )

    def dx_arrival(sx):
        held = 4 * sx + z
        return pltpu.make_async_remote_copy(
            src_ref=dplane.at[held],
            dst_ref=dplane.at[held],
            send_sem=dx_send.at[0],
            recv_sem=dx_recv.at[sx],
            device_id=(r, at_col(1, 0)),
            device_id_type=MESH,
        )

    def dz_copy(sx, step, back=0):
        held = 4 * sx + lax.rem(z + 4 - back, 4)
        return pltpu.make_async_remote_copy(
            src_ref=dplane.at[held],
            dst_ref=dplane.at[held],
            send_sem=dz_send.at[sx, step - 1],
            recv_sem=dz_recv.at[sx, step - 1],
            device_id=(r, at_col(0, step)),
            device_id_type=MESH,
        )

    for step in STEPS:
        child_copy(0, step).wait_recv()

    @pl.when(source)
    def _():
        total = front[0, pl.ds(0, TILE, stride=2), :] + got0[jnp.clip(own_one[r], 0, 7), 0]
        dplane[lax.rem(c, 8)] = total + got0[jnp.clip(own_two[r], 0, 7), 1]
        for step in (1, 3, 2):
            dx_copy(step).start()

    for sx in range(2):

        @pl.when(x != sx)
        def _():
            dx_arrival(sx).wait_recv()

        for step in (1, 3, 2):
            dz_copy(sx, step).start()
    def d_out(q, step):
        lo, hi = CHUNKS[q]
        return pltpu.make_async_remote_copy(
            src_ref=dplane.at[pl.ds(lo, hi - lo)],
            dst_ref=drows.at[r, pl.ds(lo, hi - lo)],
            send_sem=d_send.at[q, step - 1],
            recv_sem=d_recv.at[q, step - 1],
            device_id=(y_peer(step), c),
            device_id_type=MESH,
        )

    def d_pair(q, step):
        lo, hi = CHUNKS[q]
        held = y_peer(step)
        return pltpu.make_async_remote_copy(
            src_ref=dplane.at[pl.ds(lo, hi - lo)] if step == 0 else drows.at[held, pl.ds(lo, hi - lo)],
            dst_ref=drows.at[held, pl.ds(lo, hi - lo)],
            send_sem=d_send.at[q, 3 + step],
            recv_sem=d_recv.at[q, 3 + step],
            device_id=(y_peer(0, 1), c),
            device_id_type=MESH,
        )

    def d_start(q):
        @pl.when(r >= CHUNKS[q][0])
        def _():
            for step in (1, 3, 2):
                d_out(q, step).start()
            d_pair(q, 0).start()

    def d_relay(q):
        for step in (1, 3, 2):

            @pl.when(y_peer(4 - step) >= CHUNKS[q][0])
            def _():
                d_out(q, step).wait_recv()
                d_pair(q, 4 - step).start()

    def d_wait(q):
        for step in range(4):

            @pl.when(y_peer(step, 1) >= CHUNKS[q][0])
            def _():
                d_pair(q, step).wait_recv()

    def d_end(q):
        @pl.when(r >= CHUNKS[q][0])
        def _():
            for step in (1, 3, 2):
                d_out(q, step).wait_send()
            d_pair(q, 0).wait_send()

        for step in (1, 3, 2):

            @pl.when(y_peer(4 - step) >= CHUNKS[q][0])
            def _():
                d_pair(q, 4 - step).wait_send()

    assemble0()

    @pl.when(source)
    def _():
        for g in range(3):
            lo, hi, _ = GROUPS[g]
            panels[g][c] = sum0[lo:hi, :64, :]

    def spread(g):
        lo, hi, _ = GROUPS[g]
        return pltpu.make_async_remote_copy(
            src_ref=sum0.at[pl.ds(lo, hi - lo), pl.ds(64, 64)],
            dst_ref=panels[g].at[partner],
            send_sem=spread_send.at[g],
            recv_sem=spread_recv.at[g],
            device_id=(r, partner),
            device_id_type=MESH,
        )

    def part(slot, g, half):
        lo, hi, _ = GROUPS[g]
        count, panel = hi - lo, panels[g]
        upper = (count + 1) // 2
        if half is None:
            return panel.at[slot]
        return panel.at[slot, pl.ds(0, upper)] if half == 0 else panel.at[slot, pl.ds(upper, count - upper)]

    def move(g, axis, da, db, direction, half, index):
        x_first = GROUPS[g][2]
        offset = (da, db) if x_first else (db, da)
        along = (direction, 0) if (axis == 0) == x_first else (0, direction)
        ref = part(at_col(*offset), g, half)
        return pltpu.make_async_remote_copy(
            src_ref=ref,
            dst_ref=ref,
            send_sem=ring_send.at[g, index],
            recv_sem=ring_recv.at[g, index],
            device_id=(r, at_col(*along)),
            device_id_type=MESH,
        )

    def wait(spec):
        g, axis, da, db, direction, half, index = spec
        back = (da - direction, db) if axis == 0 else (da, db - direction)
        move(g, axis, back[0], back[1], direction, half, index).wait_recv()

    def first(g, k):
        return (g, 0, 0, 0, (1, -1)[k], None, k)

    def first_on(g, k):
        return (g, 0, (-1, 1)[k], 0, (1, -1)[k], k, 2 + k)

    def second(g, q, k):
        return (g, 1, (0, -1, 1, 2)[q], 0, (1, -1)[k], None, 4 + 4 * q + k)

    def second_on(g, q, k):
        return (g, 1, (0, -1, 1, 2)[q], (-1, 1)[k], (1, -1)[k], k, 6 + 4 * q + k)

    started = []

    def start(spec):
        started.append(spec)
        move(*spec).start()

    def own_blocks(g):
        return [first(g, 0), first(g, 1), second(g, 0, 0), second(g, 0, 1)]

    def s1(g):
        @pl.when(other)
        def _():
            spread(g).wait_recv()
            for spec in own_blocks(g):
                move(*spec).start()

    def s2(g):
        for k in range(2):
            wait(first(g, k))
            start(first_on(g, k))
        for q in (1, 2):
            for k in range(2):
                start(second(g, q, k))

    def s3(g):
        for k in range(2):
            wait(second(g, 0, k))
            start(second_on(g, 0, k))

    def s4(g):
        for k in range(2):
            wait(first_on(g, k))
        for k in range(2):
            start(second(g, 3, k))

    def s5a(g):
        for k in range(2):
            wait(second(g, 1, k))
            start(second_on(g, 1, k))

    def s5b(g):
        for k in range(2):
            wait(second(g, 2, k))
            start(second_on(g, 2, k))

    def s6(g):
        for k in range(2):
            wait(second(g, 3, k))
            start(second_on(g, 3, k))

    def s7(g):
        for q in range(4):
            for k in range(2):
                wait(second_on(g, q, k))

    b_row = lax.rem(c, 8)
    b_y, b_core = b_row // 2, b_row % 2
    b_root, b_even = r == b_row, core == b_core

    def bx_copy(q, t, target):
        held = lax.rem(c, 8)
        return pltpu.make_async_remote_copy(
            src_ref=sum0.at[t],
            dst_ref=brows.at[q, held],
            send_sem=bx_send.at[t - 1],
            recv_sem=bx_recv.at[q, held],
            device_id=(r, target),
            device_id_type=MESH,
        )

    def bx_arrival(q, held):
        return pltpu.make_async_remote_copy(
            src_ref=sum0.at[1],
            dst_ref=brows.at[q, held],
            send_sem=bx_send.at[0],
            recv_sem=bx_recv.at[q, held],
            device_id=(r, at_col(1, 0)),
            device_id_type=MESH,
        )

    def bx_start():
        @pl.when(source)
        def _():
            bx_copy(0, 1, r + 8).start()
            bx_copy(1, 3, r + 8).start()

        @pl.when(jnp.logical_and(source, c != r))
        def _():
            bx_copy(1, 2, r).start()

        @pl.when(jnp.logical_and(source, c == r))
        def _():
            brows[1, r] = sum0[2]

    def bx_end():
        @pl.when(source)
        def _():
            bx_copy(0, 1, r + 8).wait_send()
            bx_copy(1, 3, r + 8).wait_send()

        @pl.when(jnp.logical_and(source, c != r))
        def _():
            bx_copy(1, 2, r).wait_send()

    def b_out(q, step):
        return pltpu.make_async_remote_copy(
            src_ref=brows.at[q],
            dst_ref=brows.at[q],
            send_sem=b_send.at[q, step - 1],
            recv_sem=b_recv.at[q, step - 1],
            device_id=(y_peer(step), c),
            device_id_type=MESH,
        )

    def b_pair(q):
        return pltpu.make_async_remote_copy(
            src_ref=brows.at[q],
            dst_ref=brows.at[q],
            send_sem=b_send.at[q, 3],
            recv_sem=b_recv.at[q, 3],
            device_id=(y_peer(0, 1), c),
            device_id_type=MESH,
        )

    def with_b(q, condition):
        return condition if q == 1 else jnp.logical_and(condition, other)

    def b_start(_):
        for q in (1, 0):

            @pl.when(with_b(q, b_root))
            def _():
                for held in range(8):

                    @pl.when(c != held)
                    def _():
                        bx_arrival(q, held).wait_recv()

                for step in (1, 3, 2):
                    b_out(q, step).start()
                b_pair(q).start()

    def b_relay(_):
        for q in (1, 0):
            for step in (1, 2, 3):

                @pl.when(with_b(q, jnp.logical_and(b_even, lax.rem(b_y + step, 4) == y)))
                def _():
                    b_out(q, step).wait_recv()
                    b_pair(q).start()

    def b_wait(_):
        for q in (1, 0):

            @pl.when(with_b(q, jnp.logical_not(b_even)))
            def _():
                b_pair(q).wait_recv()

    def b_end():
        for q in (1, 0):

            @pl.when(with_b(q, b_root))
            def _():
                for step in (1, 2, 3):
                    b_out(q, step).wait_send()

            @pl.when(with_b(q, b_even))
            def _():
                b_pair(q).wait_send()

    def child1(_):
        for step in STEPS:
            child_copy(1, step).start()

    bx_start()
    for g in range(3):

        @pl.when(source)
        def _():
            spread(g).start()

    for g in range(3):
        started.extend(own_blocks(g))

    def s0(g):
        @pl.when(source)
        def _():
            for spec in own_blocks(g):
                move(*spec).start()

    s0(0)

    for step in (1, 3, 2):
        dz_copy(0, step, step).wait_recv()
    d_start(0)
    d_start(1)
    for step in (1, 3, 2):
        dz_copy(1, step, step).wait_recv()
    drows[r] = dplane[...]
    d_relay(0)
    d_start(2)
    d_wait(0)

    row = lax.broadcasted_iota(I32, (TILE, TILE), 0)
    col = lax.broadcasted_iota(I32, (TILE, TILE), 1)
    inv[...] = jnp.zeros_like(inv)

    b, e, f = 0, 1, 2
    before = {
        0: [(s0, e), (s1, b)],
        1: [(s0, f)],
        2: [(s3, b)],
        3: [],
        4: [(s2, f), (s3, e)],
        5: [(s4, e), (s5a, b), (b_relay, 0)],
        6: [(s4, f)],
        7: [(s6, e)],
    }
    after = {
        0: [(d_relay, 1), (d_wait, 1), (d_start, 3), (s1, e)],
        1: [(d_relay, 2), (d_wait, 2), (s1, f), (s2, b), (b_start, 0)],
        2: [(s2, e), (d_relay, 3)],
        3: [(s4, b), (d_wait, 3), (child1, 0)],
        4: [(s5b, b)],
        5: [(s5b, e), (s3, f)],
        6: [(s5a, e), (s6, b), (b_wait, 0)],
        7: [(s5a, f), (s5b, f)],
    }

    def window_rows():
        unused = jnp.zeros((TILE, TILE), F32)
        return jnp.concatenate(
            [
                jnp.concatenate([jnp.where(source, unused, brows[0, s]) for s in range(8)], 1),
                jnp.concatenate([brows[1, s] for s in range(8)], 1),
            ],
            0,
        )

    def step_tile(k, carry):
        for j in range(PB):

            @pl.when(k == j)
            def _():
                for act, g in before[j]:
                    act(g)
                here, done = pl.ds(j * TILE, TILE), pl.ds(0, j * TILE)
                under = pl.ds((j + 1) * TILE, (PB - 1 - j) * TILE)
                square = drows[j, j]
                square = jnp.where(row >= col, square, 0.0) + jnp.where(row > col, square, 0.0).T
                if j > 0:
                    left = lmat[here, done]
                    square = square - dot(left, left, NTC)
                    inv[here, done] = dot(left, inv[done, done], NN)
                diag[...] = square
                if j + 1 < PB:
                    below = jnp.concatenate([drows[i, j] for i in range(j + 1, PB)], 0)
                    if j > 0:
                        below = below - dot(lmat[under, done], left, NTC)
                    lmat[under, here] = below
                else:
                    mine = window_rows()
                    for i in range(3):
                        here_i, upto = pl.ds(256 * i, 256), 256 * (i + 1)
                        half[:, here_i] = dot(mine[:, :upto], inv[here_i, :upto], NTC)
                    for i in range(3):
                        here_i, rest = pl.ds(256 * i, 256), pl.ds(256 * i, 768 - 256 * i)
                        partial[:, here_i] = dot(half[:, rest], inv[rest, here_i], NN)

        upper, inverse = factor_tile(diag[...])
        diag[...] = inverse
        lower = upper.T
        for j in range(PB):

            @pl.when(k == j)
            def _():
                here, done = pl.ds(j * TILE, TILE), pl.ds(0, j * TILE)
                under = pl.ds((j + 1) * TILE, (PB - 1 - j) * TILE)
                inverse = diag[...]
                lmat[here, here] = lower
                if j > 0:
                    inv[here, done] = -dot(inverse, inv[here, done], NN)
                inv[here, here] = inverse
                if j + 1 < PB:
                    lmat[under, here] = dot(lmat[under, here], inverse, NTC)
                for act, g in after[j]:
                    act(g)

        return carry

    lax.fori_loop(0, PB, step_tile, 0)
    mine = window_rows()

    last = pl.ds(768, 256)
    half[:, last] = dot(mine, inv[last, :], NTC)
    s6(f)
    own = inv.at[pl.ds(pl.multiple_of(lax.rem(c, 8) * TILE, TILE), TILE)]
    for k in range(4):
        here = pl.ds(256 * k, 256)
        weights = dot(half[:, last], inv[last, here], NN)
        if k < 3:
            weights = weights + partial[:, here]
        weights = jnp.concatenate([jnp.where(source, -own[:, here], weights[:TILE]), weights[TILE:]], 0)
        high = weights.astype(BF16)
        wt_hi[:, here] = high
        wt_lo[:, here] = (weights - high.astype(F32)).astype(BF16)

    assemble1()

    def finish(g, lo, hi):
        panel = panels[g]
        count = hi - lo

        def half_rows(h, carry):
            order = [k + h * (partner_slot(k) - k) for k in range(8)]
            rows = jnp.concatenate([panel[s].reshape(count * 64, TILE) for s in order], 1)
            rows_hi = rows.astype(BF16)
            rows_lo = (rows - rows_hi.astype(F32)).astype(BF16)
            update = lax.dot_general(rows_hi, wt_hi[...], NTC, preferred_element_type=F32)
            update += lax.dot_general(rows_lo, wt_hi[...], NTC, preferred_element_type=F32)
            update += lax.dot_general(rows_hi, wt_lo[...], NTC, preferred_element_type=F32)
            for t in range(lo, hi):
                piece = update[64 * (t - lo) : 64 * (t - lo + 1)]
                rows_here = pl.ds(pl.multiple_of(64 * h, 64), 64)
                base0, base1 = sum0[t, rows_here, :], sum1[t, rows_here, :]
                new0 = jnp.where(source, 0.0, base0) - piece[:, :TILE]
                new1 = base1 - piece[:, TILE:]
                if t < 4:
                    i = 8 * t + r
                    new0 = jnp.where(i >= c, new0, base0)
                    new1 = jnp.where(i >= 16 + c, new1, base1)
                out[t, pl.ds(pl.multiple_of(128 * h, 128), 64, stride=2), :] = new0
                out[t, pl.ds(128 * h + 1, 64, stride=2), :] = new1
            return carry

        lax.fori_loop(0, 2, half_rows, 0)

    def store(piece, lo, hi):
        return pltpu.make_async_copy(
            out.at[pl.ds(lo, hi - lo)], out_any.at[pl.ds(lo, hi - lo)], stored.at[piece]
        )

    block = lmat[
        pl.ds(pl.multiple_of(r * TILE, TILE), TILE), pl.ds(pl.multiple_of(lax.rem(c, 8) * TILE, TILE), TILE)
    ]
    factored = jnp.logical_and(source, r >= c)
    out[0, pl.ds(0, TILE, stride=2), :] = jnp.where(factored, block, sum0[0])
    out[0, pl.ds(1, TILE, stride=2), :] = sum1[0]
    store(0, 0, 1).start()
    def ring_sent(g):
        for spec in started:
            if spec[0] == g:
                move(*spec).wait_send()

    def early_sent():
        @pl.when(source)
        def _():
            for step in range(1, 4):
                dx_copy(step).wait_send()
            for g in range(3):
                spread(g).wait_send()

        for kind in range(3):
            for step in STEPS:
                child_copy(kind, step).wait_send()
        for sx in range(2):
            for step in range(1, 4):
                dz_copy(sx, step).wait_send()
        for q in range(4):
            d_end(q)
        bx_end()
        b_end()

    for g, (lo, hi, _) in enumerate(GROUPS):
        s7(g)
        finish(g, lo, hi)
        store(1 + g, lo, hi).start()
        if g == 0:
            early_sent()
        ring_sent(g)

    store(0, 0, 1).wait()
    for g, (lo, hi, _) in enumerate(GROUPS):
        store(1 + g, lo, hi).wait()


def copy_kernel(source, out, buffer, load, store):
    parts = [pl.ds(6 * i, 6) for i in range(4)]
    loads = [pltpu.make_async_copy(source.at[p], buffer.at[p], load.at[i]) for i, p in enumerate(parts)]
    stores = [pltpu.make_async_copy(buffer.at[p], out.at[p], store.at[i]) for i, p in enumerate(parts)]
    for copy in loads:
        copy.start()
    for first, second in zip(loads, stores):
        first.wait()
        second.start()
    for copy in stores:
        copy.wait()


def shards(front, child_one, child_two, map_one, map_two, owner_one, owner_two):
    whole = pl.BlockSpec(memory_space=pl.ANY)
    smem = pl.BlockSpec(memory_space=pltpu.SMEM)
    dma = pltpu.SemaphoreType.DMA

    def space(*shape):
        return pltpu.VMEM(shape, F32)

    out = pl.pallas_call(
        kernel,
        out_shape=jax.ShapeDtypeStruct((NT, 256, TILE), F32),
        in_specs=[whole] * 3 + [smem] * 4,
        out_specs=whole,
        scratch_shapes=[
            space(NT, 256, TILE), space(8, 256, TILE), space(16, 256, TILE),
            space(8, 2, TILE, TILE), space(8, TILE, TILE), space(8, 3, TILE, TILE),
            space(9, 2, TILE, TILE), space(9, TILE, TILE), space(9, 3, TILE, TILE),
            space(NT, TILE, TILE), space(NT, TILE, TILE),
            *[space(16, hi - lo, 64, TILE) for lo, hi, _ in GROUPS],
            space(8, TILE, TILE), space(8, 8, TILE, TILE), space(2, 8, TILE, TILE),
            space(TILE, TILE), space(PB * TILE, PB * TILE), space(PB * TILE, PB * TILE),
            space(256, PB * TILE), space(256, 768),
            pltpu.VMEM((256, PB * TILE), BF16), pltpu.VMEM((256, PB * TILE), BF16),
            space(NT, 256, TILE),
            pltpu.SMEM((128,), I32), pltpu.SMEM((32,), I32),
            dma((3,)), dma((3, 7)), dma((3, 7)),
            dma((3,)), dma((3,)), dma((3, 20)), dma((3, 20)),
            dma((3,)), dma((2,)), dma((2, 3)), dma((2, 3)), dma((4, 7)), dma((4, 7)),
            dma((3,)), dma((2, 8)), dma((2, 4)), dma((2, 4)), dma((4,)),
        ],
        compiler_params=pltpu.CompilerParams(
            collective_id=0, has_side_effects=True, vmem_limit_bytes=60 * 2**20
        ),
    )(
        front.reshape(NT, 256, TILE),
        child_one.reshape(8, 256, TILE),
        child_two.reshape(16, 256, TILE),
        map_one, map_two, owner_one, owner_two,
    )
    out = pl.pallas_call(
        copy_kernel,
        out_shape=jax.ShapeDtypeStruct((NT, 256, TILE), F32),
        in_specs=[whole],
        out_specs=whole,
        scratch_shapes=[space(NT, 256, TILE), dma((4,)), dma((4,))],
        compiler_params=pltpu.CompilerParams(vmem_limit_bytes=60 * 2**20),
    )(out)
    return out.reshape(front.shape)


def solution(mesh):
    placed = P(None, "row", None, None, "col", None)
    return jax.shard_map(
        shards,
        mesh=mesh,
        in_specs=(placed, placed, placed, P(), P(), P(), P()),
        out_specs=placed,
        check_vma=False,
    )
```
